32 devices in a mesh: rep: 8 (over y, x, core), fsdp: 4 (over z).
Axes of the slice: x: 2, y: 2, z: 4, core: 2. Of those that a mesh axis runs over, the one named last changes fastest.
Arguments:
- params: float32 [8, 2560, 2560], P('rep', 'fsdp'), may hold values from -6 to 6
- push_weight: float32 [8], P('rep'), may hold values from 0.5 to 2
- inbox_params: float32 [8, 2560, 2560], P('rep', 'fsdp'), may hold values from -3 to 3
- inbox_weight: float32 [8], P('rep'), may hold values from 0.25 to 1
- heads: bfloat16 [8, 1536, 2560], P('rep', 'fsdp'), may hold values from -6 to 6
- residual: bfloat16 [8, 1536, 2560], P('rep', 'fsdp'), may hold values from -40 to 40
- cotangent: bfloat16 [8, 1536, 2560], P('rep', 'fsdp'), may hold values from -6 to 6
- gain: float32 [2560], replicated, may hold values from 0.5 to 2
- offset: int32 [8], replicated, may hold values from 1 to 4, as said below
Outputs:
- new_params: float32 [8, 2560, 2560], P('rep', 'fsdp')
- new_weight: float32 [8], P('rep')
- outbox_params: float32 [8, 2560, 2560], P('rep', 'fsdp')
- outbox_weight: float32 [8], P('rep')
- grad_heads: bfloat16 [8, 1536, 2560], P('rep', 'fsdp')
The draws below stay inside these ranges and needn't reach their ends.
Inputs may be any that keep to these rules, and one draw needn't show every extreme that they name: `offset`: each entry a power of two below 8; 1 and 4 both occur in every plan.
All inputs are finite; a program needn't handle non-finite values.
Results may differ from the reference program's by a relative error of at most 0.0057.
Values may be sent and summed in bfloat16 or wider, within the bound.
No kernel may reach another device: no remote copies, remote signals or barrier semaphores. Data moves between devices by JAX's collectives and lax.ppermute only.
A program may use at most 192 MiB of HBM per device.

```python
import math
import jax
import jax.numpy as jnp
from jax import lax

D = 2560
HEADS = 20
HEAD_DIM = 128
PLAN = 8
INNER = 2560
GROUP_TOK = 1536
REPS = 8


def draw_residual(key, part):
    key = jax.random.fold_in(key, 3)
    key_base, key_rows, key_cols = jax.random.split(key, 3)
    shape = (REPS, GROUP_TOK, D)
    base = jnp.clip(jax.random.normal(key_base, shape, jnp.float32), -4.0, 4.0)
    rows = jnp.exp(jax.random.uniform(key_rows, (REPS, GROUP_TOK, 1), jnp.float32, -1.15, 1.15))
    cols = jnp.exp(jax.random.uniform(key_cols, (1, 1, D), jnp.float32, -1.15, 1.15))
    return (base * rows * cols).astype(jnp.bfloat16)


def draw_offset(key, part):
    key = jax.random.fold_in(key, 11)
    key_levels, key_places = jax.random.split(key, 2)
    levels = REPS.bit_length() - 1
    exponent = jax.random.randint(key_levels, (PLAN,), 0, levels).astype(jnp.int32)
    places = jax.random.permutation(key_places, jnp.arange(PLAN, dtype=jnp.int32))
    positions = jnp.arange(PLAN, dtype=jnp.int32)
    exponent = jnp.where(positions == places[0], levels - 1, exponent)
    exponent = jnp.where(positions == places[1], 0, exponent).astype(jnp.int32)
    return jnp.left_shift(jnp.ones((PLAN,), jnp.int32), exponent)


def steps_of(stream_key, shape, shards, smallest, high):
    level = 1.0
    for dim, parts in shards:
        draws = jax.random.uniform(jax.random.fold_in(jax.random.fold_in(stream_key, 6), dim), (parts,), jnp.float32, smallest / len(shards), high / len(shards))
        level = level * jnp.repeat(jnp.exp(draws), shape[dim] // parts).reshape((-1,) + (1,) * (len(shape) - 1 - dim))
    return level


def normal_values(rng, extent, width, reach, cuts=(), kind=jnp.bfloat16):
    entries = jax.random.normal(rng, extent, jnp.float32) * width
    if len(cuts) > 0:
        entries = steps_of(rng, extent, cuts, -0.22, 0.18) * entries
    return jnp.clip(entries, min=-reach, max=reach).astype(kind)


def setup_inputs(seed: int = 0) -> dict:
    key_of = jax.random.split(jax.random.key(seed), 10)
    params = normal_values(key_of[0], (REPS, INNER, D), 1.0, 6.0, ((0, 8), (1, 4)), jnp.float32)
    push_weight = jnp.clip(jnp.exp(math.log(2.0) - 1.3862944 * jax.random.uniform(key_of[1], (REPS,), jnp.float32) ** steps_of(key_of[1], (REPS,), ((0, 8),), -0.2, 0.2)), 0.5, 2.0)
    inbox_params = normal_values(key_of[2], (REPS, INNER, D), 0.5, 3.0, ((0, 8), (1, 4)), jnp.float32)
    inbox_weight = jnp.clip(jnp.exp(math.log(1.0) - 1.3862944 * jax.random.uniform(key_of[3], (REPS,), jnp.float32) ** steps_of(key_of[3], (REPS,), ((0, 8),), -0.2, 0.2)), 0.25, 1.0)
    heads = normal_values(key_of[4], (REPS, GROUP_TOK, INNER), 1.0, 6.0, ((0, 8), (1, 4)))
    residual = draw_residual(jax.random.fold_in(key_of[9], 71), 0)
    cotangent = normal_values(key_of[6], (REPS, GROUP_TOK, D), 1.0, 6.0, ((0, 8), (1, 4)))
    gain = jnp.clip(jnp.exp(jax.random.uniform(key_of[7], (D,), jnp.float32, math.log(0.5), math.log(2.0))), 0.5, 2.0)
    offset = draw_offset(jax.random.fold_in(key_of[9], 71), 0)
    return dict(params=params, push_weight=push_weight, inbox_params=inbox_params, inbox_weight=inbox_weight, heads=heads, residual=residual, cotangent=cotangent, gain=gain, offset=offset)


def reference(params, push_weight, inbox_params, inbox_weight, heads, residual, cotangent, gain, offset):
    scaling = (HEADS * HEAD_DIM) ** (-0.5)

    def per_replica(replica_items):
        numer, weight_one, head_rows, resid_rows, cot_rows = replica_items
        weights = (numer / weight_one * scaling).astype(jnp.bfloat16)
        summed = resid_rows.astype(jnp.float32) + jnp.dot(head_rows, weights, preferred_element_type=jnp.float32)
        inverse = lax.rsqrt(lax.optimization_barrier(jnp.mean(summed * summed, axis=-1, keepdims=True)) + 1e-05)
        scaled_cot = gain * cot_rows.astype(jnp.float32)
        unit_grad = (inverse * scaled_cot - summed * inverse ** 3 * lax.optimization_barrier(jnp.mean(scaled_cot * summed, axis=-1, keepdims=True))).astype(jnp.bfloat16)
        grad_rows = jnp.dot(unit_grad, weights.T, preferred_element_type=jnp.float32).astype(jnp.bfloat16)
        weight_grad = jnp.dot(head_rows.T, unit_grad, preferred_element_type=jnp.float32)
        kept_half = 0.5 * (numer - 0.004 * weight_grad)
        return (kept_half, grad_rows)
    kept_half, grad_heads = lax.map(per_replica, (params, push_weight, heads, residual, cotangent))
    new_params = kept_half + inbox_params
    new_weight = 0.5 * push_weight + inbox_weight
    source = (jnp.arange(REPS, dtype=jnp.int32) - offset[0]) % REPS
    outbox_params = jnp.take(kept_half, source, axis=0)
    outbox_weight = jnp.take(0.5 * push_weight, source, axis=0)
    return (new_params, new_weight, outbox_params, outbox_weight, grad_heads)
```

```python
from functools import partial

import jax
import jax.numpy as jnp
from jax import lax
from jax.sharding import PartitionSpec as P

CHUNKS = 2


def passed_along(value, axis, by):
    length = lax.axis_size(axis)
    return lax.ppermute(value, axis, [(i, (i + by) % length) for i in range(length)])


def deliver(payload, bit_place):
    return passed_along(payload, "rep", 1 << bit_place)


def swapped(blocks):
    return lax.all_to_all(blocks, "fsdp", 0, 0, tiled=False)


def local(
    params, push_weight, inbox_params, inbox_weight, heads, residual, cotangent, gain, offset
):
    numer = params[0]
    weight_one = push_weight[0]
    members = lax.axis_size("fsdp")
    tokens, inner = heads.shape[1:]
    rows, width = numer.shape
    scaling = inner ** (-0.5)
    weights = (numer / weight_one * scaling).astype(jnp.bfloat16)
    chunk = tokens // CHUNKS
    weight_grad = jnp.zeros((rows, width), jnp.float32)
    heads_mine = []
    for c in range(CHUNKS):
        piece = heads[0, c * chunk : (c + 1) * chunk].reshape(chunk, members, rows)
        heads_mine.append(swapped(piece.transpose(1, 0, 2)).reshape(members * chunk, rows))
    grads = []
    for c in range(CHUNKS):
        span = slice(c * chunk, (c + 1) * chunk)
        part = jnp.dot(heads_mine[c], weights, preferred_element_type=jnp.float32)
        product = lax.psum_scatter(
            part.astype(jnp.bfloat16), "fsdp", scatter_dimension=0, tiled=True
        )
        summed = residual[0, span].astype(jnp.float32) + product.astype(jnp.float32)
        inverse = lax.rsqrt(jnp.mean(summed * summed, axis=-1, keepdims=True) + 1e-05)
        scaled_cot = gain * cotangent[0, span].astype(jnp.float32)
        unit_grad = (
            inverse * scaled_cot
            - summed * inverse**3 * jnp.mean(scaled_cot * summed, axis=-1, keepdims=True)
        ).astype(jnp.bfloat16)
        units = lax.all_gather(unit_grad, "fsdp", axis=0, tiled=True)
        weight_grad = weight_grad + lax.dot_general(
            heads_mine[c], units, (((0,), (0,)), ((), ())), preferred_element_type=jnp.float32
        )
        grad_rows = lax.dot_general(
            units, weights, (((1,), (1,)), ((), ())), preferred_element_type=jnp.float32
        ).astype(jnp.bfloat16)
        back = swapped(grad_rows.reshape(members, chunk, rows))
        grads.append(back.transpose(1, 0, 2).reshape(chunk, inner))
    grad_heads = jnp.concatenate(grads, axis=0)
    kept_half = 0.5 * (numer - 0.004 * weight_grad)
    new_params = (kept_half + inbox_params[0])[None]
    new_weight = 0.5 * push_weight + inbox_weight
    levels = lax.axis_size("rep").bit_length() - 1
    powers = jnp.left_shift(jnp.ones((levels,), jnp.int32), jnp.arange(levels, dtype=jnp.int32))
    level_index = jnp.sum(jnp.where(powers == offset[0], jnp.arange(levels, dtype=jnp.int32), 0))
    payload = (kept_half[None].astype(jnp.bfloat16), 0.5 * push_weight)
    branches = [partial(deliver, payload, bit_place) for bit_place in range(levels)]
    outbox_params, outbox_weight = lax.switch(level_index, branches)
    return (
        new_params,
        new_weight,
        outbox_params.astype(jnp.float32),
        outbox_weight,
        grad_heads[None],
    )


def solution(mesh):
    placed = (
        P("rep", "fsdp", None),
        P("rep"),
        P("rep", "fsdp", None),
        P("rep"),
        P("rep", "fsdp", None),
        P("rep", "fsdp", None),
        P("rep", "fsdp", None),
        P(),
        P(),
    )
    return jax.shard_map(
        local,
        mesh=mesh,
        in_specs=placed,
        out_specs=(
            P("rep", "fsdp", None),
            P("rep"),
            P("rep", "fsdp", None),
            P("rep"),
            P("rep", "fsdp", None),
        ),
        check_vma=False,
    )
```

```python
from functools import partial

import jax
import jax.numpy as jnp
from jax import lax
from jax.sharding import PartitionSpec as P

CHUNKS = 2


def passed_along(value, axis, by):
    length = lax.axis_size(axis)
    return lax.ppermute(value, axis, [(i, (i + by) % length) for i in range(length)])


def deliver(payload, bit_place):
    return passed_along(payload, "rep", 1 << bit_place)


def swapped(blocks):
    return lax.all_to_all(blocks, "fsdp", 0, 0, tiled=False)


def hop(value, step, pairs):
    return lax.ppermute(value, "fsdp", [(i, i + step) for i in pairs])


def scattered_sum(parts):
    members = parts.shape[0]
    me = lax.axis_index("fsdp")

    def block(place):
        place = jnp.clip(place, 0, members - 1)
        return lax.dynamic_index_in_dim(parts, place, 0, keepdims=False)

    right = block(me + members - 1)
    left = block(me - members + 1)
    for t in range(members - 1):
        right = hop(right, 1, range(t + 1))
        left = hop(left, -1, range(members - 1 - t, members))
        if t < members - 2:
            right = right + block(me + members - 2 - t)
            left = left + block(me - members + 2 + t)
    return right.astype(jnp.float32) + left.astype(jnp.float32) + block(me).astype(jnp.float32)


def gathered(value):
    members = lax.axis_size("fsdp")
    me = lax.axis_index("fsdp")
    rights, lefts = [], []
    right = left = value
    for s in range(members - 1):
        right = hop(right, 1, range(s, members - 1))
        left = hop(left, -1, range(1, members - s))
        rights.append(right)
        lefts.append(left)
    return [value] + [
        jnp.where(me > k, rights[k], lefts[members - 2 - k]) for k in range(members - 1)
    ]


def local(
    params, push_weight, inbox_params, inbox_weight, heads, residual, cotangent, gain, offset
):
    numer = params[0]
    weight_one = push_weight[0]
    members = lax.axis_size("fsdp")
    tokens, inner = heads.shape[1:]
    rows, width = numer.shape
    scaling = inner ** (-0.5)
    weights = (numer / weight_one * scaling).astype(jnp.bfloat16)
    chunk = tokens // CHUNKS
    weight_grad = jnp.zeros((rows, width), jnp.float32)
    heads_mine = []
    for c in range(CHUNKS):
        piece = heads[0, c * chunk : (c + 1) * chunk].reshape(chunk, members, rows)
        heads_mine.append(swapped(piece.transpose(1, 0, 2)).reshape(members * chunk, rows))
    grads = []
    for c in range(CHUNKS):
        span = slice(c * chunk, (c + 1) * chunk)
        part = jnp.dot(heads_mine[c], weights, preferred_element_type=jnp.float32)
        product = scattered_sum(part.astype(jnp.bfloat16).reshape(members, chunk, width))
        summed = residual[0, span].astype(jnp.float32) + product
        inverse = lax.rsqrt(jnp.mean(summed * summed, axis=-1, keepdims=True) + 1e-05)
        scaled_cot = gain * cotangent[0, span].astype(jnp.float32)
        unit_grad = (
            inverse * scaled_cot
            - summed * inverse**3 * jnp.mean(scaled_cot * summed, axis=-1, keepdims=True)
        ).astype(jnp.bfloat16)
        units = gathered(unit_grad)
        mine = heads_mine[c].reshape(members, chunk, rows)
        me = lax.axis_index("fsdp")
        back = jnp.zeros((members, chunk, rows), jnp.bfloat16)
        for k, unit in enumerate(units):
            place = (me - k) % members
            of_place = lax.dynamic_index_in_dim(mine, place, 0, keepdims=False)
            weight_grad = weight_grad + lax.dot_general(
                of_place, unit, (((0,), (0,)), ((), ())), preferred_element_type=jnp.float32
            )
            grad_rows = lax.dot_general(
                unit, weights, (((1,), (1,)), ((), ())), preferred_element_type=jnp.float32
            ).astype(jnp.bfloat16)
            back = lax.dynamic_update_index_in_dim(back, grad_rows, place, 0)
        grads.append(swapped(back).transpose(1, 0, 2).reshape(chunk, inner))
    grad_heads = jnp.concatenate(grads, axis=0)
    kept_half = 0.5 * (numer - 0.004 * weight_grad)
    new_params = (kept_half + inbox_params[0])[None]
    new_weight = 0.5 * push_weight + inbox_weight
    levels = lax.axis_size("rep").bit_length() - 1
    powers = jnp.left_shift(jnp.ones((levels,), jnp.int32), jnp.arange(levels, dtype=jnp.int32))
    level_index = jnp.sum(jnp.where(powers == offset[0], jnp.arange(levels, dtype=jnp.int32), 0))
    payload = (kept_half[None].astype(jnp.bfloat16), 0.5 * push_weight)
    branches = [partial(deliver, payload, bit_place) for bit_place in range(levels)]
    outbox_params, outbox_weight = lax.switch(level_index, branches)
    return (
        new_params,
        new_weight,
        outbox_params.astype(jnp.float32),
        outbox_weight,
        grad_heads[None],
    )


def solution(mesh):
    placed = (
        P("rep", "fsdp", None),
        P("rep"),
        P("rep", "fsdp", None),
        P("rep"),
        P("rep", "fsdp", None),
        P("rep", "fsdp", None),
        P("rep", "fsdp", None),
        P(),
        P(),
    )
    return jax.shard_map(
        local,
        mesh=mesh,
        in_specs=placed,
        out_specs=(
            P("rep", "fsdp", None),
            P("rep"),
            P("rep", "fsdp", None),
            P("rep"),
            P("rep", "fsdp", None),
        ),
        check_vma=False,
    )
```

```python
from functools import partial

import jax
import jax.numpy as jnp
from jax import lax
from jax.experimental import pallas as pl
from jax.experimental.pallas import tpu as pltpu
from jax.sharding import PartitionSpec as P

SPLIT = (128, 128, 128)
ANY = pl.BlockSpec(memory_space=pl.ANY)
MIB = 1 << 20


def call(body, name, grid, in_specs, out_specs, out_shape, scalars=(), aliases=None, scratch=(), flops=0, moved=0):
    def run(*args):
        return pl.pallas_call(
            body,
            name=name,
            out_shape=out_shape,
            grid_spec=pltpu.PrefetchScalarGridSpec(
                num_scalar_prefetch=len(scalars),
                grid=grid,
                in_specs=in_specs,
                out_specs=out_specs,
                scratch_shapes=scratch,
            ),
            input_output_aliases=aliases or {},
            compiler_params=pltpu.CompilerParams(vmem_limit_bytes=40 * MIB),
            cost_estimate=pl.CostEstimate(flops=flops, bytes_accessed=moved, transcendentals=0),
        )(*scalars, *args)

    return run


def hop(value, step, pairs):
    return lax.ppermute(value, "fsdp", [(i, i + step) for i in pairs])


def tile_of(width):
    return 512 if width % 512 == 0 else width


def cut_heads(heads, start, size, members, tokens_of):
    inner = heads.shape[1]
    rows = inner // members
    step = 16

    def body(heads_ref, *refs):
        out_ref = refs[-1]
        for k in range(members):
            out_ref[k] = heads_ref[:, k * rows : (k + 1) * rows]

    return call(
        body,
        "cut_heads",
        (size // step,),
        [pl.BlockSpec((step, inner), lambda i: (start // step + i, 0))] + [ANY] * len(tokens_of),
        pl.BlockSpec((members, step, rows), lambda i: (0, i, 0)),
        jax.ShapeDtypeStruct((members, size, rows), heads.dtype),
        moved=4 * size * inner,
    )(heads, *tokens_of)


def partial_products(mine, weights, after):
    members, size, rows = mine.shape
    width = weights.shape[1]
    tile = tile_of(width)

    def body(mine_ref, weights_ref, *refs):
        out_ref = refs[-1]
        product = jnp.dot(
            mine_ref[...].reshape(members * size, rows),
            weights_ref[...],
            preferred_element_type=jnp.float32,
        )
        out_ref[...] = product.astype(jnp.bfloat16).reshape(members, size, tile)

    return call(
        body,
        "partial_products",
        (width // tile,),
        [
            pl.BlockSpec((members, size, rows), lambda j: (0, 0, 0)),
            pl.BlockSpec((rows, tile), lambda j: (0, j)),
        ]
        + [ANY] * len(after),
        pl.BlockSpec((members, size, tile), lambda j: (0, 0, j)),
        jax.ShapeDtypeStruct((members, size, width), jnp.bfloat16),
        flops=2 * members * size * rows * width,
        moved=2 * (members * size * (rows + width) + rows * width),
    )(mine, weights, *after)


def add_own(right, left, parts, places):
    members, size, width = parts.shape
    tile = tile_of(width)

    def body(places_ref, right_ref, left_ref, of_right, of_left, right_out, left_out):
        right_out[...] = (
            right_ref[...].astype(jnp.float32) + of_right[0].astype(jnp.float32)
        ).astype(jnp.bfloat16)
        left_out[...] = (
            left_ref[...].astype(jnp.float32) + of_left[0].astype(jnp.float32)
        ).astype(jnp.bfloat16)

    flat = pl.BlockSpec((size, tile), lambda j, s: (0, j))
    return call(
        body,
        "add_own",
        (width // tile,),
        [
            flat,
            flat,
            pl.BlockSpec((1, size, tile), lambda j, s: (s[0], 0, j)),
            pl.BlockSpec((1, size, tile), lambda j, s: (s[1], 0, j)),
        ],
        [flat, flat],
        [jax.ShapeDtypeStruct((size, width), jnp.bfloat16)] * 2,
        scalars=(places,),
        flops=2 * size * width,
        moved=12 * size * width,
    )(right, left, parts, parts)


def unit_gradient(right, left, parts, place, residual, cotangent, gain, start):
    members, size, width = parts.shape
    step = 32

    def body(place_ref, right_ref, left_ref, own_ref, residual_ref, cot_ref, gain_ref, out_ref):
        product = (
            right_ref[...].astype(jnp.float32)
            + left_ref[...].astype(jnp.float32)
            + own_ref[0].astype(jnp.float32)
        )
        summed = residual_ref[...].astype(jnp.float32) + product
        inverse = lax.rsqrt(jnp.mean(summed * summed, axis=-1, keepdims=True) + 1e-05)
        scaled_cot = gain_ref[...] * cot_ref[...].astype(jnp.float32)
        along = jnp.mean(scaled_cot * summed, axis=-1, keepdims=True)
        out_ref[...] = (
            inverse * scaled_cot - summed * (inverse * inverse * inverse * along)
        ).astype(jnp.bfloat16)

    here = pl.BlockSpec((step, width), lambda i, s: (i, 0))
    there = pl.BlockSpec((step, width), lambda i, s: (start // step + i, 0))
    return call(
        body,
        "unit_gradient",
        (size // step,),
        [
            here,
            here,
            pl.BlockSpec((1, step, width), lambda i, s: (s[0], i, 0)),
            there,
            there,
            pl.BlockSpec((1, width), lambda i, s: (0, 0)),
        ],
        here,
        jax.ShapeDtypeStruct((size, width), jnp.bfloat16),
        scalars=(place,),
        flops=12 * size * width,
        moved=12 * size * width,
    )(right, left, parts, residual, cotangent, gain)


def stacked(own, sides):
    return jnp.concatenate([own] + [a + b for a, b in sides], axis=0)


def sided(refs, members):
    rights, lefts = refs[1:members], refs[members : 2 * members - 1]
    return refs[0][...], [
        (rights[k][...], lefts[members - 2 - k][...]) for k in range(members - 1)
    ]


def grad_and_weight(units, weights, turned, total, order):
    members = (len(units) + 1) // 2
    size, width = units[0].shape
    rows = weights.shape[0]
    tile = tile_of(width)
    steps = width // tile
    count = len(units)

    def body(order_ref, *refs):
        units_ref = refs[:count]
        weights_ref, turned_ref = refs[count : count + 2]
        total_ref = refs[count + 2] if total is not None else None
        grad_ref, total_out, acc = refs[-3:]
        j = pl.program_id(0)
        stack = stacked(*sided(units_ref, members))
        weight = jnp.dot(turned_ref[...], stack, preferred_element_type=jnp.float32)
        total_out[...] = weight if total is None else total_ref[...] + weight
        grad = lax.dot_general(
            stack, weights_ref[...], (((1,), (1,)), ((), ())), preferred_element_type=jnp.float32
        )

        @pl.when(j == 0)
        def _():
            acc[...] = grad

        @pl.when(j > 0)
        def _():
            acc[...] += grad

        @pl.when(j == steps - 1)
        def _():
            for k in range(members):
                grad_ref[order_ref[k]] = acc[k * size : (k + 1) * size].astype(jnp.bfloat16)

    columns = pl.BlockSpec((rows, tile), lambda j, s: (0, j))
    more = [] if total is None else [columns]
    return call(
        body,
        "grad_and_weight",
        (steps,),
        [pl.BlockSpec((size, tile), lambda j, s: (0, j))] * count
        + [columns, pl.BlockSpec(turned.shape, lambda j, s: (0, 0))]
        + more,
        [pl.BlockSpec((members, size, rows), lambda j, s: (0, 0, 0)), columns],
        [
            jax.ShapeDtypeStruct((members, size, rows), jnp.bfloat16),
            jax.ShapeDtypeStruct((rows, width), jnp.float32),
        ],
        scalars=(order,),
        aliases={} if total is None else {count + 3: 1},
        scratch=[pltpu.VMEM((members * size, rows), jnp.float32)],
        flops=4 * members * size * rows * width,
        moved=2 * count * size * width + 10 * rows * width,
    )(*units, weights, turned, *([] if total is None else [total]))


def mixed(units, turned, total, numer, inbox):
    members = (len(units) + 1) // 2
    size, width = units[0].shape
    rows = numer.shape[0]
    tile = tile_of(width)
    count = len(units)

    def body(*refs):
        turned_ref, total_ref, numer_ref, inbox_ref, new_ref, kept_ref = refs[count:]
        stack = stacked(*sided(refs[:count], members))
        weight = total_ref[...] + jnp.dot(
            turned_ref[...], stack, preferred_element_type=jnp.float32
        )
        kept = 0.5 * (numer_ref[...] - 0.004 * weight)
        new_ref[...] = kept + inbox_ref[...]
        kept_ref[...] = kept.astype(jnp.bfloat16)

    columns = pl.BlockSpec((rows, tile), lambda j: (0, j))
    return call(
        body,
        "mixed",
        (width // tile,),
        [pl.BlockSpec((size, tile), lambda j: (0, j))] * count
        + [pl.BlockSpec(turned.shape, lambda j: (0, 0)), columns, columns, columns],
        [columns, columns],
        [
            jax.ShapeDtypeStruct((rows, width), jnp.float32),
            jax.ShapeDtypeStruct((rows, width), jnp.bfloat16),
        ],
        flops=2 * members * size * rows * width,
        moved=2 * count * size * width + 18 * rows * width,
    )(*units, turned, total, numer, inbox)


def grad_only(units, weights, order):
    members = (len(units) + 1) // 2
    size, width = units[0].shape
    rows = weights.shape[0]
    tile = tile_of(width)
    steps = width // tile
    count = len(units)

    def body(order_ref, *refs):
        weights_ref, grad_ref, acc = refs[count:]
        j = pl.program_id(0)
        stack = stacked(*sided(refs[:count], members))
        grad = lax.dot_general(
            stack, weights_ref[...], (((1,), (1,)), ((), ())), preferred_element_type=jnp.float32
        )

        @pl.when(j == 0)
        def _():
            acc[...] = grad

        @pl.when(j > 0)
        def _():
            acc[...] += grad

        @pl.when(j == steps - 1)
        def _():
            for k in range(members):
                grad_ref[order_ref[k]] = acc[k * size : (k + 1) * size].astype(jnp.bfloat16)

    return call(
        body,
        "grad_only",
        (steps,),
        [pl.BlockSpec((size, tile), lambda j, s: (0, j))] * count
        + [pl.BlockSpec((rows, tile), lambda j, s: (0, j))],
        pl.BlockSpec((members, size, rows), lambda j, s: (0, 0, 0)),
        jax.ShapeDtypeStruct((members, size, rows), jnp.bfloat16),
        scalars=(order,),
        scratch=[pltpu.VMEM((members * size, rows), jnp.float32)],
        flops=2 * members * size * rows * width,
        moved=2 * count * size * width + 2 * rows * width,
    )(*units, weights)


def swapped(blocks):
    return lax.all_to_all(blocks, "fsdp", 0, 0, tiled=False)


def tail(kept, units, weights, grads, order, bit_place):
    length = lax.axis_size("rep")
    sent = lax.ppermute(
        kept, "rep", [(i, (i + (1 << bit_place)) % length) for i in range(length)]
    )
    last = grad_only(units, weights, order)
    back = swapped(jnp.concatenate(grads + [last], axis=1))
    return sent, back


def local(
    params, push_weight, inbox_params, inbox_weight, heads, residual, cotangent, gain, offset
):
    numer = params[0]
    weight_one = push_weight[0]
    members = lax.axis_size("fsdp")
    me = lax.axis_index("fsdp")
    inner = heads.shape[2]
    tokens = heads.shape[1]
    rows, width = numer.shape
    scaling = inner ** (-0.5)
    chunks = len(SPLIT)
    starts = [sum(SPLIT[:c]) for c in range(chunks)]
    assert sum(SPLIT) == tokens

    order = jnp.mod(me - jnp.arange(members, dtype=jnp.int32), members)
    own = jnp.reshape(me, (1,)).astype(jnp.int32)

    weights = (numer / weight_one * scaling).astype(jnp.bfloat16)
    mine, turned = [None] * chunks, [None] * chunks

    def fetch(c, after):
        piece = cut_heads(heads[0], starts[c], SPLIT[c], members, after)
        mine[c] = swapped(piece)
        in_order = [
            lax.dynamic_index_in_dim(mine[c], order[k], 0, keepdims=False) for k in range(members)
        ]
        turned[c] = jnp.concatenate(in_order, axis=0).T

    fetch(0, ())
    after = ()
    units = []
    total = None
    grads = []
    for c in range(chunks):
        parts = partial_products(mine[c], weights, after)
        right, left = parts[members - 1], parts[0]
        for t in range(members - 1):
            right = hop(right, 1, range(t + 1))
            left = hop(left, -1, range(members - 1 - t, members))
            if t == 0 and c + 1 < chunks:
                fetch(c + 1, (right, left))
            if t == members - 3:
                after = (right, left)
            if t < members - 2:
                places = jnp.stack(
                    [
                        jnp.minimum(me + members - 2 - t, members - 1),
                        jnp.maximum(me - members + 2 + t, 0),
                    ]
                ).astype(jnp.int32)
                right, left = add_own(right, left, parts, places)
        unit = unit_gradient(
            right, left, parts, own, residual[0], cotangent[0], gain[None], starts[c]
        )
        rights, lefts = [], []
        right = left = unit
        for s in range(members - 1):
            right = hop(right, 1, range(s, members - 1))
            left = hop(left, -1, range(1, members - s))
            rights.append(right)
            lefts.append(left)
        units.append([unit] + rights + lefts)
        if c < chunks - 1:
            grad, total = grad_and_weight(units[c], weights, turned[c], total, order)
            grads.append(grad)

    new_params, kept = mixed(units[-1], turned[-1], total, numer, inbox_params[0])
    new_weight = 0.5 * push_weight + inbox_weight
    levels = lax.axis_size("rep").bit_length() - 1
    powers = jnp.left_shift(jnp.ones((levels,), jnp.int32), jnp.arange(levels, dtype=jnp.int32))
    level_index = jnp.sum(jnp.where(powers == offset[0], jnp.arange(levels, dtype=jnp.int32), 0))
    all_weights = lax.all_gather(push_weight, "rep", tiled=True)
    source = jnp.mod(lax.axis_index("rep") - offset[0], lax.axis_size("rep"))
    outbox_weight = 0.5 * lax.dynamic_slice(all_weights, (source,), (1,))
    branches = [
        partial(tail, kept, units[-1], weights, grads, order, place) for place in range(levels)
    ]
    sent, back = lax.switch(level_index, branches)
    grad_heads = back.transpose(1, 0, 2).reshape(1, tokens, inner)
    return (
        new_params[None],
        new_weight,
        sent.astype(jnp.float32)[None],
        outbox_weight,
        grad_heads,
    )


def solution(mesh):
    placed = (
        P("rep", "fsdp", None),
        P("rep"),
        P("rep", "fsdp", None),
        P("rep"),
        P("rep", "fsdp", None),
        P("rep", "fsdp", None),
        P("rep", "fsdp", None),
        P(),
        P(),
    )
    return jax.shard_map(
        local,
        mesh=mesh,
        in_specs=placed,
        out_specs=(
            P("rep", "fsdp", None),
            P("rep"),
            P("rep", "fsdp", None),
            P("rep"),
            P("rep", "fsdp", None),
        ),
        check_vma=False,
    )
```

```python
from functools import partial

import jax
import jax.numpy as jnp
from jax import lax
from jax.experimental import pallas as pl
from jax.experimental.pallas import tpu as pltpu
from jax.sharding import PartitionSpec as P

STREAMS = ((96, 96), (96, 96))
MIB = 1 << 20
TOKEN = jax.ShapeDtypeStruct((8, 128), jnp.float32)


def call(body, name, grid, ins, outs, scalars=(), scratch=(), flops=0, moved=0):
    return pl.pallas_call(
        body,
        name=name,
        out_shape=[jax.ShapeDtypeStruct(shape, kind) for shape, kind, _, _ in outs],
        grid_spec=pltpu.PrefetchScalarGridSpec(
            num_scalar_prefetch=len(scalars),
            grid=grid,
            in_specs=[pl.BlockSpec(block, place) for _, block, place in ins],
            out_specs=[pl.BlockSpec(block, place) for _, _, block, place in outs],
            scratch_shapes=scratch,
        ),
        compiler_params=pltpu.CompilerParams(vmem_limit_bytes=58 * MIB),
        cost_estimate=pl.CostEstimate(flops=flops, bytes_accessed=moved, transcendentals=0),
    )(*scalars, *(array for array, _, _ in ins))


def fixed(*place):
    return lambda *_: place


def token_in(token):
    return (token, (8, 128), fixed(0, 0))


TOKEN_OUT = ((8, 128), jnp.float32, (8, 128), fixed(0, 0))


def hop(value, step, pairs):
    return lax.ppermute(value, "fsdp", [(i, i + step) for i in pairs])


def hops(right, left, rights, lefts):
    return hop(right, 1, rights), hop(left, -1, lefts)


def tile_of(width):
    return 512 if width % 512 == 0 else width


def cut_heads(heads, start, size, members, token):
    inner = heads.shape[1]
    rows = inner // members
    step = 48

    def body(heads_ref, *refs):
        for k in range(members):
            refs[-1][k] = heads_ref[:, k * rows : (k + 1) * rows]

    return call(
        body,
        "cut_heads",
        (size // step,),
        [(heads, (step, inner), lambda i: (start // step + i, 0))]
        + ([] if token is None else [token_in(token)]),
        [((members, size, rows), heads.dtype, (members, step, rows), lambda i: (0, i, 0))],
        moved=4 * size * inner,
    )[0]


def partial_products(mine, weights, token):
    members, size, rows = mine.shape
    width = weights.shape[1]
    tile = tile_of(width)

    def body(mine_ref, weights_ref, token_ref, out_ref, last_ref, first_ref):
        product = jnp.dot(
            mine_ref[...].reshape(members * size, rows),
            weights_ref[...],
            preferred_element_type=jnp.float32,
        ).astype(jnp.bfloat16)
        out_ref[...] = product.reshape(members, size, tile)
        last_ref[...] = product[(members - 1) * size :]
        first_ref[...] = product[:size]

    flat = ((size, width), jnp.bfloat16, (size, tile), lambda j: (0, j))
    return call(
        body,
        "partial_products",
        (width // tile,),
        [
            (mine, (members, size, rows), fixed(0, 0, 0)),
            (weights, (rows, tile), lambda j: (0, j)),
            token_in(token),
        ],
        [
            (
                (members, size, width),
                jnp.bfloat16,
                (members, size, tile),
                lambda j: (0, 0, j),
            ),
            flat,
            flat,
        ],
        flops=2 * members * size * rows * width,
        moved=2 * (members * size * (rows + width) + rows * width),
    )


def next_payload(right, left, parts, scalars, pick):
    members, size, width = parts.shape
    tile = tile_of(width)

    def joined(arrived, part, counts):
        if pick:
            return jnp.where(counts, part, arrived)
        weight = jnp.where(counts, 1.0, 0.0)
        return (arrived.astype(jnp.float32) + weight * part.astype(jnp.float32)).astype(
            jnp.bfloat16
        )

    def body(s, right_ref, left_ref, of_right, of_left, right_out, left_out, token_out):
        right_out[...] = joined(right_ref[...], of_right[0], s[1] > 0)
        left_out[...] = joined(left_ref[...], of_left[0], s[3] > 0)
        token_out[...] = jnp.zeros((8, 128), jnp.float32)

    here = (size, tile), lambda j, s: (0, j)
    flat = ((size, width), jnp.bfloat16) + here
    return call(
        body,
        "next_payload",
        (width // tile,),
        [
            (right,) + here,
            (left,) + here,
            (parts, (1, size, tile), lambda j, s: (s[0], 0, j)),
            (parts, (1, size, tile), lambda j, s: (s[2], 0, j)),
        ],
        [flat, flat, TOKEN_OUT],
        scalars=(scalars,),
        flops=2 * size * width,
        moved=12 * size * width,
    )


def unit_gradient(right, left, parts, place, residual, cotangent, gain, start, token):
    members, size, width = parts.shape
    step = 32

    def body(s, right_ref, left_ref, own_ref, residual_ref, cot_ref, gain_ref, *refs):
        product = (
            right_ref[...].astype(jnp.float32)
            + left_ref[...].astype(jnp.float32)
            + own_ref[0].astype(jnp.float32)
        )
        summed = residual_ref[...].astype(jnp.float32) + product
        inverse = lax.rsqrt(jnp.mean(summed * summed, axis=-1, keepdims=True) + 1e-05)
        scaled_cot = gain_ref[...] * cot_ref[...].astype(jnp.float32)
        along = jnp.mean(scaled_cot * summed, axis=-1, keepdims=True)
        refs[-1][...] = (
            inverse * scaled_cot - summed * (inverse * inverse * inverse * along)
        ).astype(jnp.bfloat16)

    here = (step, width), lambda i, s: (i, 0)
    there = (step, width), lambda i, s: (start // step + i, 0)
    return call(
        body,
        "unit_gradient",
        (size // step,),
        [
            (right,) + here,
            (left,) + here,
            (parts, (1, step, width), lambda i, s: (s[0], i, 0)),
            (residual,) + there,
            (cotangent,) + there,
            (gain, (1, width), fixed(0, 0)),
        ]
        + ([] if token is None else [token_in(token)]),
        [((size, width), jnp.bfloat16) + here],
        scalars=(place,),
        flops=12 * size * width,
        moved=12 * size * width,
    )[0]


def stack_of(refs, members, me):
    count = 2 * members - 1
    rows = []
    for c in range(len(refs) // count):
        own, rights, lefts = (
            refs[c * count],
            refs[c * count + 1 : c * count + members],
            refs[c * count + members : (c + 1) * count],
        )
        rows.append(own[...])
        for k in range(members - 1):
            rows.append(jnp.where(me > k, rights[k][...], lefts[members - 2 - k][...]))
    return jnp.concatenate(rows, axis=0)


def unit_ins(units, tile):
    return [
        (unit, (unit.shape[0], tile), lambda j, s: (0, j)) for chunk in units for unit in chunk
    ]


def mine_ins(mine):
    return [(block, block.shape, fixed(0, 0, 0)) for block in mine]


def turned_into(scratch, mine_refs, order):
    members = mine_refs[0].shape[0]
    stack = jnp.concatenate([ref[order[k]] for ref in mine_refs for k in range(members)], axis=0)
    scratch[...] = stack.T


def weight_step(units, mine, order, kept, numer, inbox):
    members, _, rows = mine[0].shape
    width = numer.shape[1] if kept is None else kept.shape[1]
    tile = tile_of(width)
    count = len(units) * len(units[0])
    chunks = len(units)
    total = sum(members * block.shape[1] for block in mine)

    def body(s, *refs):
        units_ref, mine_refs = refs[:count], refs[count : count + chunks]
        rest = refs[count + chunks : -1]
        turned = refs[-1]

        @pl.when(pl.program_id(0) == 0)
        def _():
            turned_into(turned, mine_refs, s)

        weight = jnp.dot(
            turned[...], stack_of(units_ref, members, s[0]), preferred_element_type=jnp.float32
        )
        if kept is None:
            numer_ref, kept_out, token_out = rest
            kept_out[...] = 0.5 * (numer_ref[...] - 0.004 * weight)
            token_out[...] = jnp.zeros((8, 128), jnp.float32)
        else:
            kept_ref, inbox_ref, new_out, kept_out = rest
            now = kept_ref[...] - 0.5 * 0.004 * weight
            new_out[...] = now + inbox_ref[...]
            kept_out[...] = now.astype(jnp.bfloat16)

    columns = (rows, tile), lambda j, s: (0, j)
    whole = ((rows, width), jnp.float32) + columns
    return call(
        body,
        "weight_step",
        (width // tile,),
        unit_ins(units, tile)
        + mine_ins(mine)
        + ([(numer,) + columns] if kept is None else [(kept,) + columns, (inbox,) + columns]),
        [whole, TOKEN_OUT]
        if kept is None
        else [whole, ((rows, width), jnp.bfloat16) + columns],
        scalars=(order,),
        scratch=[pltpu.VMEM((rows, total), jnp.bfloat16)],
        flops=2 * total * rows * width,
        moved=2 * count * units[0][0].shape[0] * width + 12 * rows * width,
    )


def grad_rows(units, weights, order):
    members = (len(units[0]) + 1) // 2
    sizes = [chunk[0].shape[0] for chunk in units]
    rows, width = weights.shape
    tile = tile_of(width)
    steps = width // tile
    count = len(units) * len(units[0])
    total = members * sum(sizes)

    def body(s, *refs):
        weights_ref, grad_ref, acc = refs[count:]
        j = pl.program_id(0)
        grad = lax.dot_general(
            stack_of(refs[:count], members, s[0]),
            weights_ref[...],
            (((1,), (1,)), ((), ())),
            preferred_element_type=jnp.float32,
        )

        @pl.when(j == 0)
        def _():
            acc[...] = grad

        @pl.when(j > 0)
        def _():
            acc[...] += grad

        @pl.when(j == steps - 1)
        def _():
            at, row = 0, 0
            for size in sizes:
                for k in range(members):
                    grad_ref[s[k], row : row + size] = acc[at : at + size].astype(jnp.bfloat16)
                    at += size
                row += size

    return call(
        body,
        "grad_rows",
        (steps,),
        unit_ins(units, tile) + [(weights, (rows, tile), lambda j, s: (0, j))],
        [
            (
                (members, sum(sizes), rows),
                jnp.bfloat16,
                (members, sum(sizes), rows),
                fixed(0, 0, 0),
            )
        ],
        scalars=(order,),
        scratch=[pltpu.VMEM((total, rows), jnp.float32)],
        flops=2 * total * rows * width,
        moved=2 * count * sizes[0] * width + 2 * rows * width,
    )[0]


def joined_rows(blocks):
    members, tokens, rows = blocks.shape
    step = 96

    def body(blocks_ref, out_ref):
        for k in range(members):
            out_ref[:, k * rows : (k + 1) * rows] = blocks_ref[k]

    return call(
        body,
        "joined_rows",
        (tokens // step,),
        [(blocks, (members, step, rows), lambda i: (0, i, 0))],
        [
            (
                (tokens, members * rows),
                blocks.dtype,
                (step, members * rows),
                lambda i: (i, 0),
            )
        ],
        moved=4 * members * tokens * rows,
    )[0]


def widened(value):
    rows, width = value.shape
    step = 64

    def body(value_ref, out_ref):
        out_ref[...] = value_ref[...].astype(jnp.float32)

    block = (step, width), lambda i: (i, 0)
    return call(
        body,
        "widened",
        (rows // step,),
        [(value,) + block],
        [((rows, width), jnp.float32) + block],
        moved=6 * rows * width,
    )[0]


def swapped(blocks):
    return lax.all_to_all(blocks, "fsdp", 0, 0, tiled=False)


def tail(kept, units, weights, grads, order, bit_place):
    length = lax.axis_size("rep")
    sent = lax.ppermute(
        kept, "rep", [(i, (i + (1 << bit_place)) % length) for i in range(length)]
    )
    last = grad_rows(units, weights, order)
    back = swapped(jnp.concatenate(grads + [last], axis=1))
    return sent, joined_rows(back)


def local(
    params, push_weight, inbox_params, inbox_weight, heads, residual, cotangent, gain, offset
):
    numer = params[0]
    weight_one = push_weight[0]
    members = lax.axis_size("fsdp")
    me = lax.axis_index("fsdp").astype(jnp.int32)
    tokens, inner = heads.shape[1:]
    rows, width = numer.shape
    scaling = inner ** (-0.5)
    rounds = len(STREAMS[0])
    assert sum(map(sum, STREAMS)) == tokens

    replicas = lax.axis_size("rep")
    levels = replicas.bit_length() - 1
    powers = jnp.left_shift(jnp.ones((levels,), jnp.int32), jnp.arange(levels, dtype=jnp.int32))
    level_index = jnp.sum(jnp.where(powers == offset[0], jnp.arange(levels, dtype=jnp.int32), 0))
    half_weight = 0.5 * push_weight
    arrived = [
        lax.ppermute(half_weight, "rep", [(i, (i + (1 << b)) % replicas) for i in range(replicas)])
        for b in range(levels)
    ]
    outbox_weight = arrived[0]
    for b in range(1, levels):
        outbox_weight = jnp.where(level_index == b, arrived[b], outbox_weight)

    order = jnp.mod(me - jnp.arange(members, dtype=jnp.int32), members)
    own = me[None]
    weights = (numer / weight_one * scaling).astype(jnp.bfloat16)
    everyone = range(members - 1), range(1, members)

    def scalars(t):
        ahead = members - 1 - t
        return jnp.stack(
            [
                jnp.minimum(me + ahead, members - 1),
                (me <= t).astype(jnp.int32),
                jnp.maximum(me - ahead, 0),
                (me >= ahead).astype(jnp.int32),
            ]
        )

    at = 0
    starts = []
    for e in range(rounds):
        starts.append([])
        for sizes in STREAMS:
            starts[e].append(at)
            at += sizes[e]

    count = len(STREAMS)
    mine = [[None] * count for _ in range(rounds)]
    units = [[None] * count for _ in range(rounds)]
    before = [None] * count
    hint = [jnp.broadcast_to(outbox_weight[None], (8, 128))] * count
    kept = None
    grads = []

    def fetch(e, q, token):
        piece = cut_heads(heads[0], starts[e][q], STREAMS[q][e], members, token)
        mine[e][q] = swapped(piece)

    for q in range(count):
        fetch(0, q, None)
    done = None
    for e in range(rounds):
        parts, moving = [None] * count, [None] * count
        for q in range(count):
            parts[q], last, first = partial_products(mine[e][q], weights, hint[q])
            if e == 0:
                moving[q] = hops(last, first, range(1), range(members - 1, members))
            else:
                right, left, _ = next_payload(*before[q], parts[q], scalars(0), True)
                moving[q] = hops(right, left, *everyone)
                units[e - 1][q][1].append(moving[q][0])
                units[e - 1][q][2].append(moving[q][1])
        for t in range(1, members - 1):
            for q in range(count):
                right, left, token = next_payload(*moving[q], parts[q], scalars(t), False)
                if t == 1 and e + 1 < rounds:
                    fetch(e + 1, q, token)
                hint[q] = token
                if e == 0:
                    pairs = range(t + 1), range(members - 1 - t, members)
                else:
                    pairs = everyone
                moving[q] = hops(right, left, *pairs)
                if e > 0 and t < members - 2:
                    units[e - 1][q][1].append(moving[q][0])
                    units[e - 1][q][2].append(moving[q][1])
        if e > 0:
            flat = [[u] + r + l for u, r, l in units[e - 1]]
            kept, done = weight_step(flat, mine[e - 1], order, kept, numer, None)
            grads.append(grad_rows(flat, weights, order))
        for q in range(count):
            unit = unit_gradient(
                *moving[q],
                parts[q],
                own,
                residual[0],
                cotangent[0],
                gain[None],
                starts[e][q],
                done if q == count - 1 else None,
            )
            before[q] = hops(unit, unit, *everyone)
            units[e][q] = (unit, [before[q][0]], [before[q][1]])
    for s in range(1, members - 1):
        for q in range(count):
            before[q] = hops(*before[q], range(s, members - 1), range(1, members - s))
            units[-1][q][1].append(before[q][0])
            units[-1][q][2].append(before[q][1])
    flat = [[u] + r + l for u, r, l in units[-1]]
    new_params, half = weight_step(flat, mine[-1], order, kept, None, inbox_params[0])
    new_weight = 0.5 * push_weight + inbox_weight
    branches = [partial(tail, half, flat, weights, grads, order, place) for place in range(levels)]
    sent, grad_heads = lax.switch(level_index, branches)
    return (new_params[None], new_weight, widened(sent)[None], outbox_weight, grad_heads[None])


def solution(mesh):
    placed = (
        P("rep", "fsdp", None),
        P("rep"),
        P("rep", "fsdp", None),
        P("rep"),
        P("rep", "fsdp", None),
        P("rep", "fsdp", None),
        P("rep", "fsdp", None),
        P(),
        P(),
    )
    return jax.shard_map(
        local,
        mesh=mesh,
        in_specs=placed,
        out_specs=(
            P("rep", "fsdp", None),
            P("rep"),
            P("rep", "fsdp", None),
            P("rep"),
            P("rep", "fsdp", None),
        ),
        check_vma=False,
    )
```

```python
from functools import partial

import jax
import jax.numpy as jnp
from jax import lax
from jax.experimental import pallas as pl
from jax.experimental.pallas import tpu as pltpu
from jax.sharding import PartitionSpec as P

STREAMS = ((96, 96), (96, 96))
MIB = 1 << 20
TOKEN = jax.ShapeDtypeStruct((8, 128), jnp.float32)


def call(body, name, grid, ins, outs, scalars=(), scratch=(), flops=0, moved=0, vmem=12):
    return pl.pallas_call(
        body,
        name=name,
        out_shape=[jax.ShapeDtypeStruct(shape, kind) for shape, kind, _, _ in outs],
        grid_spec=pltpu.PrefetchScalarGridSpec(
            num_scalar_prefetch=len(scalars),
            grid=grid,
            in_specs=[pl.BlockSpec(block, place) for _, block, place in ins],
            out_specs=[pl.BlockSpec(block, place) for _, _, block, place in outs],
            scratch_shapes=scratch,
        ),
        compiler_params=pltpu.CompilerParams(vmem_limit_bytes=vmem * MIB),
        cost_estimate=pl.CostEstimate(flops=flops, bytes_accessed=moved, transcendentals=0),
    )(*scalars, *(array for array, _, _ in ins))


def fixed(*place):
    return lambda *_: place


def token_in(token):
    return (token, (8, 128), fixed(0, 0))


TOKEN_OUT = ((8, 128), jnp.float32, (8, 128), fixed(0, 0))


def hop(value, step, pairs):
    return lax.ppermute(value, "fsdp", [(i, i + step) for i in pairs])


def hops(right, left, rights, lefts):
    return hop(right, 1, rights), hop(left, -1, lefts)


def tile_of(width, most=512):
    tile = most
    while width % tile:
        tile //= 2
    return tile


def cut_heads(heads, start, size, members, token):
    inner = heads.shape[1]
    rows = inner // members
    step = 48

    def body(heads_ref, *refs):
        for k in range(members):
            refs[-1][k] = heads_ref[:, k * rows : (k + 1) * rows]

    return call(
        body,
        "cut_heads",
        (size // step,),
        [(heads, (step, inner), lambda i: (start // step + i, 0))]
        + ([] if token is None else [token_in(token)]),
        [((members, size, rows), heads.dtype, (members, step, rows), lambda i: (0, i, 0))],
        moved=4 * size * inner,
    )[0]


def partial_products(mine, weights, token):
    members, size, rows = mine.shape
    width = weights.shape[1]
    tile = tile_of(width, 1280)

    def body(mine_ref, weights_ref, *refs):
        out_ref, last_ref, first_ref = refs[-3:]
        product = jnp.dot(
            mine_ref[...].reshape(members * size, rows),
            weights_ref[...],
            preferred_element_type=jnp.float32,
        ).astype(jnp.bfloat16)
        out_ref[...] = product.reshape(members, size, tile)
        last_ref[...] = product[(members - 1) * size :]
        first_ref[...] = product[:size]

    flat = ((size, width), jnp.bfloat16, (size, tile), lambda j: (0, j))
    return call(
        body,
        "partial_products",
        (width // tile,),
        [
            (mine, (members, size, rows), fixed(0, 0, 0)),
            (weights, (rows, tile), lambda j: (0, j)),
        ]
        + ([] if token is None else [token_in(token)]),
        [
            (
                (members, size, width),
                jnp.bfloat16,
                (members, size, tile),
                lambda j: (0, 0, j),
            ),
            flat,
            flat,
        ],
        flops=2 * members * size * rows * width,
        moved=2 * (members * size * (rows + width) + rows * width),
        vmem=20,
    )


def next_payload(right, left, parts, scalars, pick):
    members, size, width = parts.shape
    step = 48

    def joined(arrived, part, counts):
        if pick:
            return jnp.where(counts, part, arrived)
        weight = jnp.where(counts, 1.0, 0.0)
        return (arrived.astype(jnp.float32) + weight * part.astype(jnp.float32)).astype(
            jnp.bfloat16
        )

    def body(s, right_ref, left_ref, of_right, of_left, right_out, left_out, token_out):
        right_out[...] = joined(right_ref[...], of_right[0], s[1] > 0)
        left_out[...] = joined(left_ref[...], of_left[0], s[3] > 0)
        token_out[...] = jnp.zeros((8, 128), jnp.float32)

    here = (step, width), lambda i, s: (i, 0)
    flat = ((size, width), jnp.bfloat16) + here
    return call(
        body,
        "next_payload",
        (size // step,),
        [
            (right,) + here,
            (left,) + here,
            (parts, (1, step, width), lambda i, s: (s[0], i, 0)),
            (parts, (1, step, width), lambda i, s: (s[2], i, 0)),
        ],
        [flat, flat, TOKEN_OUT],
        scalars=(scalars,),
        flops=2 * size * width,
        moved=12 * size * width,
    )


def unit_gradient(right, left, parts, place, residual, cotangent, gain, start, token):
    members, size, width = parts.shape
    step = 48

    def body(s, right_ref, left_ref, own_ref, residual_ref, cot_ref, gain_ref, *refs):
        product = (
            right_ref[...].astype(jnp.float32)
            + left_ref[...].astype(jnp.float32)
            + own_ref[0].astype(jnp.float32)
        )
        summed = residual_ref[...].astype(jnp.float32) + product
        inverse = lax.rsqrt(jnp.mean(summed * summed, axis=-1, keepdims=True) + 1e-05)
        scaled_cot = gain_ref[...] * cot_ref[...].astype(jnp.float32)
        along = jnp.mean(scaled_cot * summed, axis=-1, keepdims=True)
        refs[-1][...] = (
            inverse * scaled_cot - summed * (inverse * inverse * inverse * along)
        ).astype(jnp.bfloat16)

    here = (step, width), lambda i, s: (i, 0)
    there = (step, width), lambda i, s: (start // step + i, 0)
    return call(
        body,
        "unit_gradient",
        (size // step,),
        [
            (right,) + here,
            (left,) + here,
            (parts, (1, step, width), lambda i, s: (s[0], i, 0)),
            (residual,) + there,
            (cotangent,) + there,
            (gain, (1, width), fixed(0, 0)),
        ]
        + ([] if token is None else [token_in(token)]),
        [((size, width), jnp.bfloat16) + here],
        scalars=(place,),
        flops=12 * size * width,
        moved=12 * size * width,
    )[0]


def stack_of(refs, members, me):
    count = 2 * members - 1
    rows = []
    for c in range(len(refs) // count):
        own, rights, lefts = (
            refs[c * count],
            refs[c * count + 1 : c * count + members],
            refs[c * count + members : (c + 1) * count],
        )
        rows.append(own[...])
        for k in range(members - 1):
            rows.append(jnp.where(me > k, rights[k][...], lefts[members - 2 - k][...]))
    return jnp.concatenate(rows, axis=0)


def unit_ins(units, tile):
    ins = []
    for chunk in units:
        block = (chunk[0].shape[0], tile)
        members = (len(chunk) + 1) // 2
        ins.append((chunk[0], block, lambda j, s: (0, j)))
        for k in range(members - 1):
            place = lambda j, s, k=k: (0, jnp.where(s[0] > k, j, 0))
            ins.append((chunk[1 + k], block, place))
        for m in range(members - 1):
            place = lambda j, s, k=members - 2 - m: (0, jnp.where(s[0] > k, 0, j))
            ins.append((chunk[members + m], block, place))
    return ins


def mine_ins(mine):
    return [(block, block.shape, fixed(0, 0, 0)) for block in mine]


def turned_into(scratch, mine_refs, order):
    members = mine_refs[0].shape[0]
    stack = jnp.concatenate([ref[order[k]] for ref in mine_refs for k in range(members)], axis=0)
    scratch[...] = stack.T


def weight_step(units, mine, order, kept, numer, inbox):
    members, _, rows = mine[0].shape
    width = numer.shape[1] if kept is None else kept.shape[1]
    tile = tile_of(width)
    count = len(units) * len(units[0])
    chunks = len(units)
    total = sum(members * block.shape[1] for block in mine)

    def body(s, *refs):
        units_ref, mine_refs = refs[:count], refs[count : count + chunks]
        rest = refs[count + chunks : -1]
        turned = refs[-1]

        @pl.when(pl.program_id(0) == 0)
        def _():
            turned_into(turned, mine_refs, s)

        weight = jnp.dot(
            turned[...], stack_of(units_ref, members, s[0]), preferred_element_type=jnp.float32
        )
        if kept is None:
            numer_ref, kept_out, token_out = rest
            kept_out[...] = 0.5 * (numer_ref[...] - 0.004 * weight)
            token_out[...] = jnp.zeros((8, 128), jnp.float32)
        else:
            kept_ref, inbox_ref, new_out, kept_out = rest
            now = kept_ref[...] - 0.5 * 0.004 * weight
            new_out[...] = now + inbox_ref[...]
            kept_out[...] = now.astype(jnp.bfloat16)

    columns = (rows, tile), lambda j, s: (0, j)
    whole = ((rows, width), jnp.float32) + columns
    return call(
        body,
        "weight_step",
        (width // tile,),
        unit_ins(units, tile)
        + mine_ins(mine)
        + ([(numer,) + columns] if kept is None else [(kept,) + columns, (inbox,) + columns]),
        [whole, TOKEN_OUT]
        if kept is None
        else [whole, ((rows, width), jnp.bfloat16) + columns],
        scalars=(order,),
        scratch=[pltpu.VMEM((rows, total), jnp.bfloat16)],
        flops=2 * total * rows * width,
        moved=2 * count * units[0][0].shape[0] * width + 12 * rows * width,
        vmem=26,
    )


def grad_rows(units, weights, order):
    members = (len(units[0]) + 1) // 2
    sizes = [chunk[0].shape[0] for chunk in units]
    rows, width = weights.shape
    tile = tile_of(width)
    steps = width // tile
    count = len(units) * len(units[0])
    total = members * sum(sizes)

    def body(s, *refs):
        weights_ref, grad_ref, acc = refs[count:]
        j = pl.program_id(0)
        grad = lax.dot_general(
            stack_of(refs[:count], members, s[0]),
            weights_ref[...],
            (((1,), (1,)), ((), ())),
            preferred_element_type=jnp.float32,
        )

        @pl.when(j == 0)
        def _():
            acc[...] = grad

        @pl.when(j > 0)
        def _():
            acc[...] += grad

        @pl.when(j == steps - 1)
        def _():
            at, row = 0, 0
            for size in sizes:
                for k in range(members):
                    grad_ref[s[k], row : row + size] = acc[at : at + size].astype(jnp.bfloat16)
                    at += size
                row += size

    return call(
        body,
        "grad_rows",
        (steps,),
        unit_ins(units, tile) + [(weights, (rows, tile), lambda j, s: (0, j))],
        [
            (
                (members, sum(sizes), rows),
                jnp.bfloat16,
                (members, sum(sizes), rows),
                fixed(0, 0, 0),
            )
        ],
        scalars=(order,),
        scratch=[pltpu.VMEM((total, rows), jnp.float32)],
        flops=2 * total * rows * width,
        moved=2 * count * sizes[0] * width + 2 * rows * width,
        vmem=20,
    )[0]


def joined_rows(blocks):
    members, tokens, rows = blocks.shape
    step = 96

    def body(blocks_ref, out_ref):
        for k in range(members):
            out_ref[:, k * rows : (k + 1) * rows] = blocks_ref[k]

    return call(
        body,
        "joined_rows",
        (tokens // step,),
        [(blocks, (members, step, rows), lambda i: (0, i, 0))],
        [
            (
                (tokens, members * rows),
                blocks.dtype,
                (step, members * rows),
                lambda i: (i, 0),
            )
        ],
        moved=4 * members * tokens * rows,
    )[0]


def widened(value):
    rows, width = value.shape
    step = 160

    def body(value_ref, out_ref):
        out_ref[...] = value_ref[...].astype(jnp.float32)

    block = (step, width), lambda i: (i, 0)
    return call(
        body,
        "widened",
        (rows // step,),
        [(value,) + block],
        [((rows, width), jnp.float32) + block],
        moved=6 * rows * width,
        vmem=20,
    )[0]


def swapped(blocks):
    return lax.all_to_all(blocks, "fsdp", 0, 0, tiled=False)


def tail(kept, units, weights, grads, order, bit_place):
    length = lax.axis_size("rep")
    sent = lax.ppermute(
        kept, "rep", [(i, (i + (1 << bit_place)) % length) for i in range(length)]
    )
    last = grad_rows(units, weights, order)
    back = swapped(jnp.concatenate(grads + [last], axis=1))
    return sent, joined_rows(back)


def local(
    params, push_weight, inbox_params, inbox_weight, heads, residual, cotangent, gain, offset
):
    numer = params[0]
    weight_one = push_weight[0]
    members = lax.axis_size("fsdp")
    me = lax.axis_index("fsdp").astype(jnp.int32)
    tokens, inner = heads.shape[1:]
    rows, width = numer.shape
    scaling = inner ** (-0.5)
    rounds = len(STREAMS[0])
    assert sum(map(sum, STREAMS)) == tokens

    replicas = lax.axis_size("rep")
    levels = replicas.bit_length() - 1
    powers = jnp.left_shift(jnp.ones((levels,), jnp.int32), jnp.arange(levels, dtype=jnp.int32))
    level_index = jnp.sum(jnp.where(powers == offset[0], jnp.arange(levels, dtype=jnp.int32), 0))
    half_weight = 0.5 * push_weight
    arrived = [
        lax.ppermute(half_weight, "rep", [(i, (i + (1 << b)) % replicas) for i in range(replicas)])
        for b in range(levels)
    ]
    outbox_weight = arrived[0]
    for b in range(1, levels):
        outbox_weight = jnp.where(level_index == b, arrived[b], outbox_weight)

    order = jnp.mod(me - jnp.arange(members, dtype=jnp.int32), members)
    own = me[None]
    weights = (numer / weight_one * scaling).astype(jnp.bfloat16)
    everyone = range(members - 1), range(1, members)

    def scalars(t):
        ahead = members - 1 - t
        return jnp.stack(
            [
                jnp.minimum(me + ahead, members - 1),
                (me <= t).astype(jnp.int32),
                jnp.maximum(me - ahead, 0),
                (me >= ahead).astype(jnp.int32),
            ]
        )

    at = 0
    starts = []
    for e in range(rounds):
        starts.append([])
        for sizes in STREAMS:
            starts[e].append(at)
            at += sizes[e]

    count = len(STREAMS)
    mine = [[None] * count for _ in range(rounds)]
    units = [[None] * count for _ in range(rounds)]
    before = [None] * count
    hint = [None] * (count - 1) + [jnp.broadcast_to(outbox_weight[None], (8, 128))]
    kept = None
    grads = []

    def fetch(e, q, token):
        piece = cut_heads(heads[0], starts[e][q], STREAMS[q][e], members, token)
        mine[e][q] = swapped(piece)

    for q in range(count):
        fetch(0, q, None)
    done = None
    for e in range(rounds):
        parts, moving = [None] * count, [None] * count
        for q in range(count):
            parts[q], last, first = partial_products(mine[e][q], weights, hint[q])
            if e == 0:
                moving[q] = hops(last, first, range(1), range(members - 1, members))
            else:
                right, left, _ = next_payload(*before[q], parts[q], scalars(0), True)
                moving[q] = hops(right, left, *everyone)
                units[e - 1][q][1].append(moving[q][0])
                units[e - 1][q][2].append(moving[q][1])
        for t in range(1, members - 1):
            for q in range(count):
                right, left, token = next_payload(*moving[q], parts[q], scalars(t), False)
                if t == 1 and e + 1 < rounds:
                    fetch(e + 1, q, token)
                hint[q] = token
                if e == 0:
                    pairs = range(t + 1), range(members - 1 - t, members)
                else:
                    pairs = everyone
                moving[q] = hops(right, left, *pairs)
                if e > 0 and t < members - 2:
                    units[e - 1][q][1].append(moving[q][0])
                    units[e - 1][q][2].append(moving[q][1])
        if e > 0:
            flat = [[u] + r + l for u, r, l in units[e - 1]]
            kept, done = weight_step(flat, mine[e - 1], order, kept, numer, None)
            grads.append(grad_rows(flat, weights, order))
        for q in range(count):
            unit = unit_gradient(
                *moving[q],
                parts[q],
                own,
                residual[0],
                cotangent[0],
                gain[None],
                starts[e][q],
                done if q == count - 1 else None,
            )
            before[q] = hops(unit, unit, *everyone)
            units[e][q] = (unit, [before[q][0]], [before[q][1]])
    for s in range(1, members - 1):
        for q in range(count):
            before[q] = hops(*before[q], range(s, members - 1), range(1, members - s))
            units[-1][q][1].append(before[q][0])
            units[-1][q][2].append(before[q][1])
    flat = [[u] + r + l for u, r, l in units[-1]]
    new_params, half = weight_step(flat, mine[-1], order, kept, None, inbox_params[0])
    new_weight = 0.5 * push_weight + inbox_weight
    branches = [partial(tail, half, flat, weights, grads, order, place) for place in range(levels)]
    sent, grad_heads = lax.switch(level_index, branches)
    return (new_params[None], new_weight, widened(sent)[None], outbox_weight, grad_heads[None])


def solution(mesh):
    placed = (
        P("rep", "fsdp", None),
        P("rep"),
        P("rep", "fsdp", None),
        P("rep"),
        P("rep", "fsdp", None),
        P("rep", "fsdp", None),
        P("rep", "fsdp", None),
        P(),
        P(),
    )
    return jax.shard_map(
        local,
        mesh=mesh,
        in_specs=placed,
        out_specs=(
            P("rep", "fsdp", None),
            P("rep"),
            P("rep", "fsdp", None),
            P("rep"),
            P("rep", "fsdp", None),
        ),
        check_vma=False,
    )
```

```python
from functools import partial

import jax
import jax.numpy as jnp
from jax import lax
from jax.experimental import pallas as pl
from jax.experimental.pallas import tpu as pltpu
from jax.sharding import PartitionSpec as P

STREAMS = ((96, 96), (96, 96))
MIB = 1 << 20
TOKEN = jax.ShapeDtypeStruct((8, 128), jnp.float32)


def call(body, name, grid, ins, outs, scalars=(), scratch=(), flops=0, moved=0, vmem=12):
    return pl.pallas_call(
        body,
        name=name,
        out_shape=[jax.ShapeDtypeStruct(shape, kind) for shape, kind, _, _ in outs],
        grid_spec=pltpu.PrefetchScalarGridSpec(
            num_scalar_prefetch=len(scalars),
            grid=grid,
            in_specs=[pl.BlockSpec(block, place) for _, block, place in ins],
            out_specs=[pl.BlockSpec(block, place) for _, _, block, place in outs],
            scratch_shapes=scratch,
        ),
        compiler_params=pltpu.CompilerParams(vmem_limit_bytes=vmem * MIB),
        cost_estimate=pl.CostEstimate(flops=flops, bytes_accessed=moved, transcendentals=0),
    )(*scalars, *(array for array, _, _ in ins))


def fixed(*place):
    return lambda *_: place


def token_in(token):
    return (token, (8, 128), fixed(0, 0))


TOKEN_OUT = ((8, 128), jnp.float32, (8, 128), fixed(0, 0))


def hop(value, step, pairs):
    return lax.ppermute(value, "fsdp", [(i, i + step) for i in pairs])


def hops(right, left, rights, lefts):
    return hop(right, 1, rights), hop(left, -1, lefts)


def tile_of(width, most=512):
    tile = most
    while width % tile:
        tile //= 2
    return tile


def cut_heads(heads, start, size, members, token):
    inner = heads.shape[1]
    rows = inner // members
    step = 48

    def body(heads_ref, *refs):
        for k in range(members):
            refs[-1][k] = heads_ref[:, k * rows : (k + 1) * rows]

    return call(
        body,
        "cut_heads",
        (size // step,),
        [(heads, (step, inner), lambda i: (start // step + i, 0))]
        + ([] if token is None else [token_in(token)]),
        [((members, size, rows), heads.dtype, (members, step, rows), lambda i: (0, i, 0))],
        moved=4 * size * inner,
    )[0]


def scaled_weights(numer, weight_one, scaling, token):
    rows, width = numer.shape
    step = rows // 4

    def body(numer_ref, one_ref, *refs):
        out_ref, token_out = refs[-2:]
        out_ref[...] = (numer_ref[...] / one_ref[...] * scaling).astype(jnp.bfloat16)
        token_out[...] = jnp.zeros((8, 128), jnp.float32)

    block = (step, width), lambda i: (i, 0)
    return call(
        body,
        "scaled_weights",
        (rows // step,),
        [(numer,) + block, (weight_one.reshape(1, 1), (1, 1), fixed(0, 0)), token_in(token)],
        [((rows, width), jnp.bfloat16) + block, TOKEN_OUT],
        flops=2 * rows * width,
        moved=6 * rows * width,
    )[0]


def partial_products(mine, weights, token):
    mine, index, size = mine
    members, _, rows = mine.shape
    width = weights.shape[1]
    tile = tile_of(width, 1280)

    def body(mine_ref, weights_ref, *refs):
        out_ref, last_ref, first_ref, token_out = refs[-4:]
        product = jnp.dot(
            mine_ref[...].reshape(members * size, rows),
            weights_ref[...],
            preferred_element_type=jnp.float32,
        ).astype(jnp.bfloat16)
        out_ref[...] = product.reshape(members, size, tile)
        last_ref[...] = product[(members - 1) * size :]
        first_ref[...] = product[:size]
        token_out[...] = jnp.zeros((8, 128), jnp.float32)

    flat = ((size, width), jnp.bfloat16, (size, tile), lambda j: (0, j))
    return call(
        body,
        "partial_products",
        (width // tile,),
        [
            (mine, (members, size, rows), fixed(0, index, 0)),
            (weights, (rows, tile), lambda j: (0, j)),
        ]
        + ([] if token is None else [token_in(token)]),
        [
            (
                (members, size, width),
                jnp.bfloat16,
                (members, size, tile),
                lambda j: (0, 0, j),
            ),
            flat,
            flat,
            TOKEN_OUT,
        ],
        flops=2 * members * size * rows * width,
        moved=2 * (members * size * (rows + width) + rows * width),
        vmem=20,
    )


def next_payload(right, left, parts, scalars, pick):
    members, size, width = parts.shape
    step = 48

    def joined(arrived, part, counts):
        if pick:
            return jnp.where(counts, part, arrived)
        weight = jnp.where(counts, 1.0, 0.0)
        return (arrived.astype(jnp.float32) + weight * part.astype(jnp.float32)).astype(
            jnp.bfloat16
        )

    def body(s, right_ref, left_ref, of_right, of_left, right_out, left_out, token_out):
        right_out[...] = joined(right_ref[...], of_right[0], s[1] > 0)
        left_out[...] = joined(left_ref[...], of_left[0], s[3] > 0)
        token_out[...] = jnp.zeros((8, 128), jnp.float32)

    here = (step, width), lambda i, s: (i, 0)
    flat = ((size, width), jnp.bfloat16) + here
    return call(
        body,
        "next_payload",
        (size // step,),
        [
            (right,) + here,
            (left,) + here,
            (parts, (1, step, width), lambda i, s: (s[0], i, 0)),
            (parts, (1, step, width), lambda i, s: (s[2], i, 0)),
        ],
        [flat, flat, TOKEN_OUT],
        scalars=(scalars,),
        flops=2 * size * width,
        moved=12 * size * width,
    )


def unit_gradient(right, left, parts, place, residual, cotangent, gain, start, token):
    members, size, width = parts.shape
    step = 48

    def body(s, right_ref, left_ref, own_ref, residual_ref, cot_ref, gain_ref, *refs):
        product = (
            right_ref[...].astype(jnp.float32)
            + left_ref[...].astype(jnp.float32)
            + own_ref[0].astype(jnp.float32)
        )
        summed = residual_ref[...].astype(jnp.float32) + product
        inverse = lax.rsqrt(jnp.mean(summed * summed, axis=-1, keepdims=True) + 1e-05)
        scaled_cot = gain_ref[...] * cot_ref[...].astype(jnp.float32)
        along = jnp.mean(scaled_cot * summed, axis=-1, keepdims=True)
        refs[-1][...] = (
            inverse * scaled_cot - summed * (inverse * inverse * inverse * along)
        ).astype(jnp.bfloat16)

    here = (step, width), lambda i, s: (i, 0)
    there = (step, width), lambda i, s: (start // step + i, 0)
    return call(
        body,
        "unit_gradient",
        (size // step,),
        [
            (right,) + here,
            (left,) + here,
            (parts, (1, step, width), lambda i, s: (s[0], i, 0)),
            (residual,) + there,
            (cotangent,) + there,
            (gain, (1, width), fixed(0, 0)),
        ]
        + ([] if token is None else [token_in(token)]),
        [((size, width), jnp.bfloat16) + here],
        scalars=(place,),
        flops=12 * size * width,
        moved=12 * size * width,
    )[0]


def stack_of(refs, members, me):
    count = 2 * members - 1
    rows = []
    for c in range(len(refs) // count):
        own, rights, lefts = (
            refs[c * count],
            refs[c * count + 1 : c * count + members],
            refs[c * count + members : (c + 1) * count],
        )
        rows.append(own[...])
        for k in range(members - 1):
            rows.append(jnp.where(me > k, rights[k][...], lefts[members - 2 - k][...]))
    return jnp.concatenate(rows, axis=0)


def unit_ins(units, tile):
    ins = []
    for chunk in units:
        block = (chunk[0].shape[0], tile)
        members = (len(chunk) + 1) // 2
        ins.append((chunk[0], block, lambda j, s: (0, j)))
        for k in range(members - 1):
            place = lambda j, s, k=k: (0, jnp.where(s[0] > k, j, 0))
            ins.append((chunk[1 + k], block, place))
        for m in range(members - 1):
            place = lambda j, s, k=members - 2 - m: (0, jnp.where(s[0] > k, 0, j))
            ins.append((chunk[members + m], block, place))
    return ins


def mine_ins(mine):
    return [
        (array, (array.shape[0], size, array.shape[2]), fixed(0, index, 0))
        for array, index, size in mine
    ]


def turned_into(scratch, mine_refs, order):
    members = mine_refs[0].shape[0]
    stack = jnp.concatenate([ref[order[k]] for ref in mine_refs for k in range(members)], axis=0)
    scratch[...] = stack.T


def weight_step(units, mine, order, kept, numer, inbox):
    members, _, rows = mine[0][0].shape
    width = numer.shape[1] if kept is None else kept.shape[1]
    tile = tile_of(width)
    count = len(units) * len(units[0])
    chunks = len(units)
    total = sum(members * size for _, _, size in mine)

    def body(s, *refs):
        units_ref, mine_refs = refs[:count], refs[count : count + chunks]
        rest = refs[count + chunks : -1]
        turned = refs[-1]

        @pl.when(pl.program_id(0) == 0)
        def _():
            turned_into(turned, mine_refs, s)

        weight = jnp.dot(
            turned[...], stack_of(units_ref, members, s[0]), preferred_element_type=jnp.float32
        )
        if kept is None:
            numer_ref, kept_out, token_out = rest
            kept_out[...] = 0.5 * (numer_ref[...] - 0.004 * weight)
            token_out[...] = jnp.zeros((8, 128), jnp.float32)
        else:
            kept_ref, inbox_ref, new_out, kept_out = rest
            now = kept_ref[...] - 0.5 * 0.004 * weight
            new_out[...] = now + inbox_ref[...]
            kept_out[...] = now.astype(jnp.bfloat16)

    columns = (rows, tile), lambda j, s: (0, j)
    whole = ((rows, width), jnp.float32) + columns
    return call(
        body,
        "weight_step",
        (width // tile,),
        unit_ins(units, tile)
        + mine_ins(mine)
        + ([(numer,) + columns] if kept is None else [(kept,) + columns, (inbox,) + columns]),
        [whole, TOKEN_OUT]
        if kept is None
        else [whole, ((rows, width), jnp.bfloat16) + columns],
        scalars=(order,),
        scratch=[pltpu.VMEM((rows, total), jnp.bfloat16)],
        flops=2 * total * rows * width,
        moved=2 * count * units[0][0].shape[0] * width + 12 * rows * width,
        vmem=26,
    )


def grad_rows(units, weights, order):
    members = (len(units[0]) + 1) // 2
    sizes = [chunk[0].shape[0] for chunk in units]
    rows, width = weights.shape
    tile = tile_of(width)
    steps = width // tile
    count = len(units) * len(units[0])
    total = members * sum(sizes)

    def body(s, *refs):
        weights_ref, grad_ref, token_out, acc = refs[count:]
        token_out[...] = jnp.zeros((8, 128), jnp.float32)
        j = pl.program_id(0)
        grad = lax.dot_general(
            stack_of(refs[:count], members, s[0]),
            weights_ref[...],
            (((1,), (1,)), ((), ())),
            preferred_element_type=jnp.float32,
        )

        @pl.when(j == 0)
        def _():
            acc[...] = grad

        @pl.when(j > 0)
        def _():
            acc[...] += grad

        @pl.when(j == steps - 1)
        def _():
            at, row = 0, 0
            for size in sizes:
                for k in range(members):
                    grad_ref[s[k], row : row + size] = acc[at : at + size].astype(jnp.bfloat16)
                    at += size
                row += size

    return call(
        body,
        "grad_rows",
        (steps,),
        unit_ins(units, tile) + [(weights, (rows, tile), lambda j, s: (0, j))],
        [
            (
                (members, sum(sizes), rows),
                jnp.bfloat16,
                (members, sum(sizes), rows),
                fixed(0, 0, 0),
            ),
            TOKEN_OUT,
        ],
        scalars=(order,),
        scratch=[pltpu.VMEM((total, rows), jnp.float32)],
        flops=2 * total * rows * width,
        moved=2 * count * sizes[0] * width + 2 * rows * width,
        vmem=20,
    )


def passed(right, left, token):
    size, width = right.shape
    step = 48

    def body(right_ref, left_ref, token_ref, right_out, left_out):
        right_out[...] = right_ref[...]
        left_out[...] = left_ref[...]

    here = (step, width), lambda i: (i, 0)
    flat = ((size, width), right.dtype) + here
    return call(
        body,
        "passed",
        (size // step,),
        [(right,) + here, (left,) + here, token_in(token)],
        [flat, flat],
        moved=8 * size * width,
    )


def joined_rows(blocks):
    members, tokens, rows = blocks.shape
    step = 96

    def body(blocks_ref, out_ref):
        for k in range(members):
            out_ref[:, k * rows : (k + 1) * rows] = blocks_ref[k]

    return call(
        body,
        "joined_rows",
        (tokens // step,),
        [(blocks, (members, step, rows), lambda i: (0, i, 0))],
        [
            (
                (tokens, members * rows),
                blocks.dtype,
                (step, members * rows),
                lambda i: (i, 0),
            )
        ],
        moved=4 * members * tokens * rows,
    )[0]


def widened(value):
    rows, width = value.shape
    step = rows // 2

    def body(value_ref, out_ref):
        out_ref[...] = value_ref[...].astype(jnp.float32)

    block = (step, width), lambda i: (i, 0)
    return call(
        body,
        "widened",
        (rows // step,),
        [(value,) + block],
        [((rows, width), jnp.float32) + block],
        moved=6 * rows * width,
        vmem=20,
    )[0]


def swapped(blocks):
    return lax.all_to_all(blocks, "fsdp", 0, 0, tiled=False)


def tail(kept, units, weights, grads, order, bit_place):
    length = lax.axis_size("rep")
    sent = lax.ppermute(
        kept, "rep", [(i, (i + (1 << bit_place)) % length) for i in range(length)]
    )
    last, _ = grad_rows(units, weights, order)
    back = swapped(jnp.concatenate(grads + [last], axis=1))
    return sent, joined_rows(back)


def local(
    params, push_weight, inbox_params, inbox_weight, heads, residual, cotangent, gain, offset
):
    numer = params[0]
    weight_one = push_weight[0]
    members = lax.axis_size("fsdp")
    me = lax.axis_index("fsdp").astype(jnp.int32)
    tokens, inner = heads.shape[1:]
    rows, width = numer.shape
    scaling = inner ** (-0.5)
    rounds = len(STREAMS[0])
    assert sum(map(sum, STREAMS)) == tokens

    replicas = lax.axis_size("rep")
    levels = replicas.bit_length() - 1
    powers = jnp.left_shift(jnp.ones((levels,), jnp.int32), jnp.arange(levels, dtype=jnp.int32))
    level_index = jnp.sum(jnp.where(powers == offset[0], jnp.arange(levels, dtype=jnp.int32), 0))
    half_weight = 0.5 * push_weight
    arrived = [
        lax.ppermute(half_weight, "rep", [(i, (i + (1 << b)) % replicas) for i in range(replicas)])
        for b in range(levels)
    ]
    outbox_weight = arrived[0]
    for b in range(1, levels):
        outbox_weight = jnp.where(level_index == b, arrived[b], outbox_weight)

    order = jnp.mod(me - jnp.arange(members, dtype=jnp.int32), members)
    own = me[None]
    weights = scaled_weights(
        numer, weight_one, scaling, jnp.broadcast_to(outbox_weight[None], (8, 128))
    )
    everyone = range(members - 1), range(1, members)

    def scalars(t):
        ahead = members - 1 - t
        return jnp.stack(
            [
                jnp.minimum(me + ahead, members - 1),
                (me <= t).astype(jnp.int32),
                jnp.maximum(me - ahead, 0),
                (me >= ahead).astype(jnp.int32),
            ]
        )

    at = 0
    starts = []
    for e in range(rounds):
        starts.append([])
        for sizes in STREAMS:
            starts[e].append(at)
            at += sizes[e]

    count = len(STREAMS)
    mine = [[None] * count for _ in range(rounds)]
    units = [[None] * count for _ in range(rounds)]
    before = [None] * count
    hint = [None] * count
    kept = None
    grads = []

    def fetch(e, members_of, token):
        size = STREAMS[members_of[0]][e]
        piece = cut_heads(
            heads[0], starts[e][members_of[0]], size * len(members_of), members, token
        )
        array = swapped(piece)
        for index, q in enumerate(members_of):
            mine[e][q] = (array, index, size)

    fetch(0, [0], None)
    done = None
    for e in range(rounds):
        parts, moving = [None] * count, [None] * count
        for q in range(count):
            parts[q], last, first, token = partial_products(mine[e][q], weights, hint[q])
            if e == 0 and q + 1 < count:
                fetch(0, [q + 1], token)
            if e == 0:
                moving[q] = hops(last, first, range(1), range(members - 1, members))
            else:
                right, left, _ = next_payload(*before[q], parts[q], scalars(0), True)
                moving[q] = hops(right, left, *everyone)
                units[e - 1][q][1].append(moving[q][0])
                units[e - 1][q][2].append(moving[q][1])
        for t in range(1, members - 1):
            for q in range(count):
                right, left, token = next_payload(*moving[q], parts[q], scalars(t), False)
                if t == 1 and q == 0 and e + 1 < rounds:
                    fetch(e + 1, list(range(count)), token)
                hint[q] = token
                if e == 0:
                    pairs = range(t + 1), range(members - 1 - t, members)
                else:
                    pairs = everyone
                moving[q] = hops(right, left, *pairs)
                if e > 0 and t < members - 2:
                    units[e - 1][q][1].append(moving[q][0])
                    units[e - 1][q][2].append(moving[q][1])
        if e > 0:
            flat = [[u] + r + l for u, r, l in units[e - 1]]
            kept, done = weight_step(flat, mine[e - 1], order, kept, numer, None)
            grad, grad_done = grad_rows(flat, weights, order)
            grads.append(grad)
        for q in range(count):
            unit = unit_gradient(
                *moving[q],
                parts[q],
                own,
                residual[0],
                cotangent[0],
                gain[None],
                starts[e][q],
                None,
            )
            before[q] = hops(unit, unit, *everyone)
            units[e][q] = (unit, [before[q][0]], [before[q][1]])
    for s in range(1, members - 1):
        for q in range(count):
            if (s, q) == (1, count - 1):
                before[q] = passed(*before[q], done)
            if (s, q) == (2, 0):
                before[q] = passed(*before[q], grad_done)
            before[q] = hops(*before[q], range(s, members - 1), range(1, members - s))
            units[-1][q][1].append(before[q][0])
            units[-1][q][2].append(before[q][1])
    flat = [[u] + r + l for u, r, l in units[-1]]
    new_params, half = weight_step(flat, mine[-1], order, kept, None, inbox_params[0])
    new_weight = 0.5 * push_weight + inbox_weight
    branches = [partial(tail, half, flat, weights, grads, order, place) for place in range(levels)]
    sent, grad_heads = lax.switch(level_index, branches)
    return (new_params[None], new_weight, widened(sent)[None], outbox_weight, grad_heads[None])


def solution(mesh):
    placed = (
        P("rep", "fsdp", None),
        P("rep"),
        P("rep", "fsdp", None),
        P("rep"),
        P("rep", "fsdp", None),
        P("rep", "fsdp", None),
        P("rep", "fsdp", None),
        P(),
        P(),
    )
    return jax.shard_map(
        local,
        mesh=mesh,
        in_specs=placed,
        out_specs=(
            P("rep", "fsdp", None),
            P("rep"),
            P("rep", "fsdp", None),
            P("rep"),
            P("rep", "fsdp", None),
        ),
        check_vma=False,
    )
```

```python
from functools import partial

import jax
import jax.numpy as jnp
from jax import lax
from jax.experimental import pallas as pl
from jax.experimental.pallas import tpu as pltpu
from jax.sharding import PartitionSpec as P

STREAMS = ((64, 64, 64), (64, 64, 64))
MIB = 1 << 20
TOKEN = jax.ShapeDtypeStruct((8, 128), jnp.float32)


def call(body, name, grid, ins, outs, scalars=(), scratch=(), flops=0, moved=0, vmem=12):
    return pl.pallas_call(
        body,
        name=name,
        out_shape=[jax.ShapeDtypeStruct(shape, kind) for shape, kind, _, _ in outs],
        grid_spec=pltpu.PrefetchScalarGridSpec(
            num_scalar_prefetch=len(scalars),
            grid=grid,
            in_specs=[pl.BlockSpec(block, place) for _, block, place in ins],
            out_specs=[pl.BlockSpec(block, place) for _, _, block, place in outs],
            scratch_shapes=scratch,
        ),
        compiler_params=pltpu.CompilerParams(vmem_limit_bytes=vmem * MIB),
        cost_estimate=pl.CostEstimate(flops=flops, bytes_accessed=moved, transcendentals=0),
    )(*scalars, *(array for array, _, _ in ins))


def fixed(*place):
    return lambda *_: place


def token_in(token):
    return (token, (8, 128), fixed(0, 0))


TOKEN_OUT = ((8, 128), jnp.float32, (8, 128), fixed(0, 0))


def hop(value, step, pairs):
    return lax.ppermute(value, "fsdp", [(i, i + step) for i in pairs])


def hops(right, left, rights, lefts):
    return hop(right, 1, rights), hop(left, -1, lefts)


def tile_of(width, most=512):
    tile = most
    while width % tile:
        tile //= 2
    return tile


def cut_heads(heads, start, size, members, token):
    inner = heads.shape[1]
    rows = inner // members
    step = size // 2

    def body(heads_ref, *refs):
        for k in range(members):
            refs[-1][k] = heads_ref[:, k * rows : (k + 1) * rows]

    return call(
        body,
        "cut_heads",
        (size // step,),
        [(heads, (step, inner), lambda i: (start // step + i, 0))]
        + ([] if token is None else [token_in(token)]),
        [((members, size, rows), heads.dtype, (members, step, rows), lambda i: (0, i, 0))],
        moved=4 * size * inner,
        vmem=12 if start else 56,
    )[0]


def scaled_weights(numer, weight_one, scaling, token):
    rows, width = numer.shape
    step = rows // 4

    def body(numer_ref, one_ref, *refs):
        out_ref, token_out = refs[-2:]
        out_ref[...] = (numer_ref[...] / one_ref[...] * scaling).astype(jnp.bfloat16)
        token_out[...] = jnp.zeros((8, 128), jnp.float32)

    block = (step, width), lambda i: (i, 0)
    return call(
        body,
        "scaled_weights",
        (rows // step,),
        [(numer,) + block, (weight_one.reshape(1, 1), (1, 1), fixed(0, 0)), token_in(token)],
        [((rows, width), jnp.bfloat16) + block, TOKEN_OUT],
        flops=2 * rows * width,
        moved=6 * rows * width,
        vmem=56,
    )[0]


def partial_products(mine, weights, token):
    mine, index, size = mine
    members, _, rows = mine.shape
    width = weights.shape[1]
    tile = tile_of(width, 1280)

    def body(mine_ref, weights_ref, *refs):
        out_ref, last_ref, first_ref = refs[-3:]
        product = jnp.dot(
            mine_ref[...].reshape(members * size, rows),
            weights_ref[...],
            preferred_element_type=jnp.float32,
        ).astype(jnp.bfloat16)
        out_ref[...] = product.reshape(members, size, tile)
        last_ref[...] = product[(members - 1) * size :]
        first_ref[...] = product[:size]

    flat = ((size, width), jnp.bfloat16, (size, tile), lambda j: (0, j))
    return call(
        body,
        "partial_products",
        (width // tile,),
        [
            (mine, (members, size, rows), fixed(0, index, 0)),
            (weights, (rows, tile), lambda j: (0, j)),
        ]
        + ([] if token is None else [token_in(token)]),
        [
            (
                (members, size, width),
                jnp.bfloat16,
                (members, size, tile),
                lambda j: (0, 0, j),
            ),
            flat,
            flat,
        ],
        flops=2 * members * size * rows * width,
        moved=2 * (members * size * (rows + width) + rows * width),
        vmem=20,
    )


def next_payload(right, left, parts, scalars, pick):
    members, size, width = parts.shape
    step = size // 2

    def joined(arrived, part, counts):
        if pick:
            return jnp.where(counts, part, arrived)
        weight = jnp.where(counts, 1.0, 0.0)
        return (arrived.astype(jnp.float32) + weight * part.astype(jnp.float32)).astype(
            jnp.bfloat16
        )

    def body(s, right_ref, left_ref, of_right, of_left, right_out, left_out, token_out):
        right_out[...] = joined(right_ref[...], of_right[0], s[1] > 0)
        left_out[...] = joined(left_ref[...], of_left[0], s[3] > 0)
        token_out[...] = jnp.zeros((8, 128), jnp.float32)

    here = (step, width), lambda i, s: (i, 0)
    flat = ((size, width), jnp.bfloat16) + here
    return call(
        body,
        "next_payload",
        (size // step,),
        [
            (right,) + here,
            (left,) + here,
            (parts, (1, step, width), lambda i, s: (s[0], i, 0)),
            (parts, (1, step, width), lambda i, s: (s[2], i, 0)),
        ],
        [flat, flat, TOKEN_OUT],
        scalars=(scalars,),
        flops=2 * size * width,
        moved=12 * size * width,
    )


def unit_gradient(right, left, parts, place, residual, cotangent, gain, start):
    members, size, width = parts.shape
    step = size // 2

    def body(s, right_ref, left_ref, own_ref, residual_ref, cot_ref, gain_ref, out_ref):
        product = (
            right_ref[...].astype(jnp.float32)
            + left_ref[...].astype(jnp.float32)
            + own_ref[0].astype(jnp.float32)
        )
        summed = residual_ref[...].astype(jnp.float32) + product
        inverse = lax.rsqrt(jnp.mean(summed * summed, axis=-1, keepdims=True) + 1e-05)
        scaled_cot = gain_ref[...] * cot_ref[...].astype(jnp.float32)
        along = jnp.mean(scaled_cot * summed, axis=-1, keepdims=True)
        out_ref[...] = (
            inverse * scaled_cot - summed * (inverse * inverse * inverse * along)
        ).astype(jnp.bfloat16)

    here = (step, width), lambda i, s: (i, 0)
    there = (step, width), lambda i, s: (start // step + i, 0)
    return call(
        body,
        "unit_gradient",
        (size // step,),
        [
            (right,) + here,
            (left,) + here,
            (parts, (1, step, width), lambda i, s: (s[0], i, 0)),
            (residual,) + there,
            (cotangent,) + there,
            (gain, (1, width), fixed(0, 0)),
        ],
        [((size, width), jnp.bfloat16) + here],
        scalars=(place,),
        flops=12 * size * width,
        moved=12 * size * width,
    )[0]


def stack_of(refs, members, me):
    count = 2 * members - 1
    rows = []
    for c in range(len(refs) // count):
        own, rights, lefts = (
            refs[c * count],
            refs[c * count + 1 : c * count + members],
            refs[c * count + members : (c + 1) * count],
        )
        rows.append(own[...])
        for k in range(members - 1):
            rows.append(jnp.where(me > k, rights[k][...], lefts[members - 2 - k][...]))
    return jnp.concatenate(rows, axis=0)


def unit_ins(units, tile):
    ins = []
    for chunk in units:
        block = (chunk[0].shape[0], tile)
        members = (len(chunk) + 1) // 2
        ins.append((chunk[0], block, lambda j, s: (0, j)))
        for k in range(members - 1):
            place = lambda j, s, k=k: (0, jnp.where(s[0] > k, j, 0))
            ins.append((chunk[1 + k], block, place))
        for m in range(members - 1):
            place = lambda j, s, k=members - 2 - m: (0, jnp.where(s[0] > k, 0, j))
            ins.append((chunk[members + m], block, place))
    return ins


def mine_ins(mine):
    return [
        (array, (array.shape[0], size, array.shape[2]), fixed(0, index, 0))
        for array, index, size in mine
    ]


def turned_into(scratch, mine_refs, order):
    members = mine_refs[0].shape[0]
    stack = jnp.concatenate([ref[order[k]] for ref in mine_refs for k in range(members)], axis=0)
    scratch[...] = stack.T


def weight_step(units, mine, order, kept, numer, inbox):
    members, _, rows = mine[0][0].shape
    width = numer.shape[1] if kept is None else kept.shape[1]
    tile = tile_of(width)
    count = len(units) * len(units[0])
    chunks = len(units)
    total = sum(members * size for _, _, size in mine)

    def body(s, *refs):
        units_ref, mine_refs = refs[:count], refs[count : count + chunks]
        rest = refs[count + chunks : -1]
        turned = refs[-1]

        @pl.when(pl.program_id(0) == 0)
        def _():
            turned_into(turned, mine_refs, s)

        weight = jnp.dot(
            turned[...], stack_of(units_ref, members, s[0]), preferred_element_type=jnp.float32
        )
        if kept is None:
            numer_ref, kept_out, token_out = rest
            kept_out[...] = 0.5 * (numer_ref[...] - 0.004 * weight)
            token_out[...] = jnp.zeros((8, 128), jnp.float32)
        else:
            kept_ref, inbox_ref, new_out, kept_out = rest
            now = kept_ref[...] - 0.5 * 0.004 * weight
            new_out[...] = now + inbox_ref[...]
            kept_out[...] = now.astype(jnp.bfloat16)

    columns = (rows, tile), lambda j, s: (0, j)
    whole = ((rows, width), jnp.float32) + columns
    return call(
        body,
        "weight_step",
        (width // tile,),
        unit_ins(units, tile)
        + mine_ins(mine)
        + ([(numer,) + columns] if kept is None else [(kept,) + columns, (inbox,) + columns]),
        [whole, TOKEN_OUT]
        if kept is None
        else [whole, ((rows, width), jnp.bfloat16) + columns],
        scalars=(order,),
        scratch=[pltpu.VMEM((rows, total), jnp.bfloat16)],
        flops=2 * total * rows * width,
        moved=2 * count * units[0][0].shape[0] * width + 12 * rows * width,
        vmem=50,
    )


def grad_rows(units, weights, order):
    members = (len(units[0]) + 1) // 2
    sizes = [chunk[0].shape[0] for chunk in units]
    rows, width = weights.shape
    tile = tile_of(width)
    steps = width // tile
    count = len(units) * len(units[0])
    total = members * sum(sizes)

    def body(s, *refs):
        weights_ref, grad_ref, acc = refs[count:]
        j = pl.program_id(0)
        grad = lax.dot_general(
            stack_of(refs[:count], members, s[0]),
            weights_ref[...],
            (((1,), (1,)), ((), ())),
            preferred_element_type=jnp.float32,
        )

        @pl.when(j == 0)
        def _():
            acc[...] = grad

        @pl.when(j > 0)
        def _():
            acc[...] += grad

        @pl.when(j == steps - 1)
        def _():
            at, row = 0, 0
            for size in sizes:
                for k in range(members):
                    grad_ref[s[k], row : row + size] = acc[at : at + size].astype(jnp.bfloat16)
                    at += size
                row += size

    return call(
        body,
        "grad_rows",
        (steps,),
        unit_ins(units, tile) + [(weights, (rows, tile), lambda j, s: (0, j))],
        [
            (
                (members, sum(sizes), rows),
                jnp.bfloat16,
                (members, sum(sizes), rows),
                fixed(0, 0, 0),
            )
        ],
        scalars=(order,),
        scratch=[pltpu.VMEM((total, rows), jnp.float32)],
        flops=2 * total * rows * width,
        moved=2 * count * sizes[0] * width + 2 * rows * width,
        vmem=50,
    )[0]


def passed(right, left, token):
    size, width = right.shape
    step = size // 2

    def body(right_ref, left_ref, token_ref, right_out, left_out):
        right_out[...] = right_ref[...]
        left_out[...] = left_ref[...]

    here = (step, width), lambda i: (i, 0)
    flat = ((size, width), right.dtype) + here
    return call(
        body,
        "passed",
        (size // step,),
        [(right,) + here, (left,) + here, token_in(token)],
        [flat, flat],
        moved=8 * size * width,
    )


def joined_rows(blocks):
    members, tokens, rows = blocks.shape
    step = 96

    def body(blocks_ref, out_ref):
        for k in range(members):
            out_ref[:, k * rows : (k + 1) * rows] = blocks_ref[k]

    return call(
        body,
        "joined_rows",
        (tokens // step,),
        [(blocks, (members, step, rows), lambda i: (0, i, 0))],
        [
            (
                (tokens, members * rows),
                blocks.dtype,
                (step, members * rows),
                lambda i: (i, 0),
            )
        ],
        moved=4 * members * tokens * rows,
    )[0]


def widened(value):
    rows, width = value.shape
    step = rows // 2

    def body(value_ref, out_ref):
        out_ref[...] = value_ref[...].astype(jnp.float32)

    block = (step, width), lambda i: (i, 0)
    return call(
        body,
        "widened",
        (rows // step,),
        [(value,) + block],
        [((rows, width), jnp.float32) + block],
        moved=6 * rows * width,
        vmem=20,
    )[0]


def swapped(blocks):
    return lax.all_to_all(blocks, "fsdp", 0, 0, tiled=False)


def tail(kept, units, weights, order, bit_place):
    length = lax.axis_size("rep")
    sent = lax.ppermute(
        kept, "rep", [(i, (i + (1 << bit_place)) % length) for i in range(length)]
    )
    return sent, joined_rows(swapped(grad_rows(units, weights, order)))


def local(
    params, push_weight, inbox_params, inbox_weight, heads, residual, cotangent, gain, offset
):
    numer = params[0]
    weight_one = push_weight[0]
    members = lax.axis_size("fsdp")
    me = lax.axis_index("fsdp").astype(jnp.int32)
    tokens, inner = heads.shape[1:]
    rows, width = numer.shape
    scaling = inner ** (-0.5)
    rounds = len(STREAMS[0])
    assert sum(map(sum, STREAMS)) == tokens

    replicas = lax.axis_size("rep")
    levels = replicas.bit_length() - 1
    powers = jnp.left_shift(jnp.ones((levels,), jnp.int32), jnp.arange(levels, dtype=jnp.int32))
    level_index = jnp.sum(jnp.where(powers == offset[0], jnp.arange(levels, dtype=jnp.int32), 0))
    half_weight = 0.5 * push_weight
    arrived = [
        lax.ppermute(half_weight, "rep", [(i, (i + (1 << b)) % replicas) for i in range(replicas)])
        for b in range(levels)
    ]
    outbox_weight = arrived[0]
    for b in range(1, levels):
        outbox_weight = jnp.where(level_index == b, arrived[b], outbox_weight)

    order = jnp.mod(me - jnp.arange(members, dtype=jnp.int32), members)
    own = me[None]
    weights = scaled_weights(
        numer, weight_one, scaling, jnp.broadcast_to(outbox_weight[None], (8, 128))
    )
    everyone = range(members - 1), range(1, members)

    def scalars(t):
        ahead = members - 1 - t
        return jnp.stack(
            [
                jnp.minimum(me + ahead, members - 1),
                (me <= t).astype(jnp.int32),
                jnp.maximum(me - ahead, 0),
                (me >= ahead).astype(jnp.int32),
            ]
        )

    at = 0
    starts = []
    for e in range(rounds):
        starts.append([])
        for sizes in STREAMS:
            starts[e].append(at)
            at += sizes[e]

    count = len(STREAMS)
    mine = [[None] * count for _ in range(rounds)]
    units = [[None] * count for _ in range(rounds)]
    before = [None] * count
    hint = [None] * count

    def fetch(e, members_of, token):
        size = STREAMS[members_of[0]][e]
        piece = cut_heads(
            heads[0], starts[e][members_of[0]], size * len(members_of), members, token
        )
        array = swapped(piece)
        for index, q in enumerate(members_of):
            mine[e][q] = (array, index, size)

    fetch(0, list(range(count)), None)
    for e in range(rounds):
        parts, moving = [None] * count, [None] * count
        for q in range(count):
            parts[q], last, first = partial_products(mine[e][q], weights, hint[q])
            if e == 0:
                moving[q] = hops(last, first, range(1), range(members - 1, members))
            else:
                right, left, _ = next_payload(*before[q], parts[q], scalars(0), True)
                moving[q] = hops(right, left, *everyone)
                units[e - 1][q][1].append(moving[q][0])
                units[e - 1][q][2].append(moving[q][1])
        for t in range(1, members - 1):
            for q in range(count):
                right, left, token = next_payload(*moving[q], parts[q], scalars(t), False)
                if t == 1 and q == 0 and e + 1 < rounds:
                    fetch(e + 1, list(range(count)), token)
                hint[q] = token
                if e == 0:
                    pairs = range(t + 1), range(members - 1 - t, members)
                else:
                    pairs = everyone
                moving[q] = hops(right, left, *pairs)
                if e > 0 and t < members - 2:
                    units[e - 1][q][1].append(moving[q][0])
                    units[e - 1][q][2].append(moving[q][1])
        for q in range(count):
            unit = unit_gradient(
                *moving[q],
                parts[q],
                own,
                residual[0],
                cotangent[0],
                gain[None],
                starts[e][q],
            )
            before[q] = hops(unit, unit, *everyone)
            units[e][q] = (unit, [before[q][0]], [before[q][1]])
    kept = None
    for s in range(1, members - 1):
        for q in range(count):
            if (s, q) == (1, count - 1):
                early = [[u] + r + l for of_round in units[:-1] for u, r, l in of_round]
                kept, done = weight_step(
                    early, [m for of_round in mine[:-1] for m in of_round], order, None, numer, None
                )
                before[q] = passed(*before[q], done)
            before[q] = hops(*before[q], range(s, members - 1), range(1, members - s))
            units[-1][q][1].append(before[q][0])
            units[-1][q][2].append(before[q][1])
    flat = [[u] + r + l for u, r, l in units[-1]]
    new_params, half = weight_step(flat, mine[-1], order, kept, None, inbox_params[0])
    new_weight = 0.5 * push_weight + inbox_weight
    branches = [partial(tail, half, early + flat, weights, order, place) for place in range(levels)]
    sent, grad_heads = lax.switch(level_index, branches)
    return (new_params[None], new_weight, widened(sent)[None], outbox_weight, grad_heads[None])


def solution(mesh):
    placed = (
        P("rep", "fsdp", None),
        P("rep"),
        P("rep", "fsdp", None),
        P("rep"),
        P("rep", "fsdp", None),
        P("rep", "fsdp", None),
        P("rep", "fsdp", None),
        P(),
        P(),
    )
    return jax.shard_map(
        local,
        mesh=mesh,
        in_specs=placed,
        out_specs=(
            P("rep", "fsdp", None),
            P("rep"),
            P("rep", "fsdp", None),
            P("rep"),
            P("rep", "fsdp", None),
        ),
        check_vma=False,
    )
```

```python
from functools import partial

import jax
import jax.numpy as jnp
from jax import lax
from jax.experimental import pallas as pl
from jax.experimental.pallas import tpu as pltpu
from jax.sharding import PartitionSpec as P

STREAMS = ((96, 96), (96, 96))
MIB = 1 << 20
TOKEN = jax.ShapeDtypeStruct((8, 128), jnp.float32)


def call(body, name, grid, ins, outs, scalars=(), scratch=(), flops=0, moved=0, vmem=12):
    return pl.pallas_call(
        body,
        name=name,
        out_shape=[jax.ShapeDtypeStruct(shape, kind) for shape, kind, _, _ in outs],
        grid_spec=pltpu.PrefetchScalarGridSpec(
            num_scalar_prefetch=len(scalars),
            grid=grid,
            in_specs=[pl.BlockSpec(block, place) for _, block, place in ins],
            out_specs=[pl.BlockSpec(block, place) for _, _, block, place in outs],
            scratch_shapes=scratch,
        ),
        compiler_params=pltpu.CompilerParams(vmem_limit_bytes=vmem * MIB),
        cost_estimate=pl.CostEstimate(flops=flops, bytes_accessed=moved, transcendentals=0),
    )(*scalars, *(array for array, _, _ in ins))


def fixed(*place):
    return lambda *_: place


def token_in(token):
    return (token, (8, 128), fixed(0, 0))


TOKEN_OUT = ((8, 128), jnp.float32, (8, 128), fixed(0, 0))


def hop(value, step, pairs):
    return lax.ppermute(value, "fsdp", [(i, i + step) for i in pairs])


def hops(right, left, rights, lefts):
    return hop(right, 1, rights), hop(left, -1, lefts)


def tile_of(width, most=512):
    tile = most
    while width % tile:
        tile //= 2
    return tile


def cut_heads(heads, start, size, members, token):
    inner = heads.shape[1]
    rows = inner // members
    step = size // 2

    def body(heads_ref, *refs):
        for k in range(members):
            refs[-1][k] = heads_ref[:, k * rows : (k + 1) * rows]

    return call(
        body,
        "cut_heads",
        (size // step,),
        [(heads, (step, inner), lambda i: (start // step + i, 0))]
        + ([] if token is None else [token_in(token)]),
        [((members, size, rows), heads.dtype, (members, step, rows), lambda i: (0, i, 0))],
        moved=4 * size * inner,
        vmem=12 if start else 56,
    )[0]


def scaled_weights(numer, weight_one, scaling):
    rows, width = numer.shape
    step = rows // 4

    def body(numer_ref, one_ref, out_ref):
        out_ref[...] = (numer_ref[...] / one_ref[...] * scaling).astype(jnp.bfloat16)

    block = (step, width), lambda i: (i, 0)
    return call(
        body,
        "scaled_weights",
        (rows // step,),
        [(numer,) + block, (weight_one.reshape(1, 1), (1, 1), fixed(0, 0))],
        [((rows, width), jnp.bfloat16) + block],
        flops=2 * rows * width,
        moved=6 * rows * width,
        vmem=56,
    )[0]


def partial_products(mine, weights, ends):
    mine, index, size = mine
    members, _, rows = mine.shape
    width = weights.shape[1]
    tile = tile_of(width, 1280)

    def body(mine_ref, weights_ref, out_ref, token_out, *end_refs):
        product = jnp.dot(
            mine_ref[...].reshape(members * size, rows),
            weights_ref[...],
            preferred_element_type=jnp.float32,
        ).astype(jnp.bfloat16)
        out_ref[...] = product.reshape(members, size, tile)
        token_out[...] = jnp.zeros((8, 128), jnp.float32)
        if ends:
            end_refs[0][...] = product[(members - 1) * size :]
            end_refs[1][...] = product[:size]

    flat = ((size, width), jnp.bfloat16, (size, tile), lambda j: (0, j))
    return call(
        body,
        "partial_products",
        (width // tile,),
        [
            (mine, (members, size, rows), fixed(0, index, 0)),
            (weights, (rows, tile), lambda j: (0, j)),
        ],
        [
            ((members, size, width), jnp.bfloat16, (members, size, tile), lambda j: (0, 0, j)),
            TOKEN_OUT,
        ]
        + [flat, flat] * ends,
        flops=2 * members * size * rows * width,
        moved=2 * (members * size * (rows + width) + rows * width),
        vmem=20,
    )


def next_payload(right, left, parts, scalars, pick):
    members, size, width = parts.shape
    step = size // 2

    def joined(arrived, part, counts):
        if pick:
            return jnp.where(counts, part, arrived)
        weight = jnp.where(counts, 1.0, 0.0)
        return (arrived.astype(jnp.float32) + weight * part.astype(jnp.float32)).astype(
            jnp.bfloat16
        )

    def body(s, right_ref, left_ref, of_right, of_left, right_out, left_out, token_out):
        right_out[...] = joined(right_ref[...], of_right[0], s[1] > 0)
        left_out[...] = joined(left_ref[...], of_left[0], s[3] > 0)
        token_out[...] = jnp.zeros((8, 128), jnp.float32)

    here = (step, width), lambda i, s: (i, 0)
    flat = ((size, width), jnp.bfloat16) + here
    return call(
        body,
        "next_payload",
        (size // step,),
        [
            (right,) + here,
            (left,) + here,
            (parts, (1, step, width), lambda i, s: (s[0], i, 0)),
            (parts, (1, step, width), lambda i, s: (s[2], i, 0)),
        ],
        [flat, flat, TOKEN_OUT],
        scalars=(scalars,),
        flops=2 * size * width,
        moved=12 * size * width,
    )


def unit_gradient(right, left, parts, place, residual, cotangent, gain, start, token):
    members, size, width = parts.shape
    step = size // 2

    def body(s, right_ref, left_ref, own_ref, residual_ref, cot_ref, gain_ref, *refs):
        product = (
            right_ref[...].astype(jnp.float32)
            + left_ref[...].astype(jnp.float32)
            + own_ref[0].astype(jnp.float32)
        )
        summed = residual_ref[...].astype(jnp.float32) + product
        inverse = lax.rsqrt(jnp.mean(summed * summed, axis=-1, keepdims=True) + 1e-05)
        scaled_cot = gain_ref[...] * cot_ref[...].astype(jnp.float32)
        along = jnp.mean(scaled_cot * summed, axis=-1, keepdims=True)
        refs[-1][...] = (
            inverse * scaled_cot - summed * (inverse * inverse * inverse * along)
        ).astype(jnp.bfloat16)

    here = (step, width), lambda i, s: (i, 0)
    there = (step, width), lambda i, s: (start // step + i, 0)
    return call(
        body,
        "unit_gradient",
        (size // step,),
        [
            (right,) + here,
            (left,) + here,
            (parts, (1, step, width), lambda i, s: (s[0], i, 0)),
            (residual,) + there,
            (cotangent,) + there,
            (gain, (1, width), fixed(0, 0)),
        ]
        + ([] if token is None else [token_in(token)]),
        [((size, width), jnp.bfloat16) + here],
        scalars=(place,),
        flops=12 * size * width,
        moved=12 * size * width,
    )[0]


def stack_of(refs, members, me):
    count = 2 * members - 1
    rows = []
    for c in range(len(refs) // count):
        own, rights, lefts = (
            refs[c * count],
            refs[c * count + 1 : c * count + members],
            refs[c * count + members : (c + 1) * count],
        )
        rows.append(own[...])
        for k in range(members - 1):
            rows.append(jnp.where(me > k, rights[k][...], lefts[members - 2 - k][...]))
    return jnp.concatenate(rows, axis=0)


def unit_ins(units, tile):
    ins = []
    for chunk in units:
        block = (chunk[0].shape[0], tile)
        members = (len(chunk) + 1) // 2
        ins.append((chunk[0], block, lambda j, s: (0, j)))
        for k in range(members - 1):
            place = lambda j, s, k=k: (0, jnp.where(s[0] > k, j, 0))
            ins.append((chunk[1 + k], block, place))
        for m in range(members - 1):
            place = lambda j, s, k=members - 2 - m: (0, jnp.where(s[0] > k, 0, j))
            ins.append((chunk[members + m], block, place))
    return ins


def mine_ins(mine):
    return [
        (array, (array.shape[0], size, array.shape[2]), fixed(0, index, 0))
        for array, index, size in mine
    ]


def turned_into(scratch, mine_refs, order):
    members = mine_refs[0].shape[0]
    stack = jnp.concatenate([ref[order[k]] for ref in mine_refs for k in range(members)], axis=0)
    scratch[...] = stack.T


def weight_step(units, mine, order, kept, numer, inbox, token=None):
    members, _, rows = mine[0][0].shape
    width = numer.shape[1] if kept is None else kept.shape[1]
    tile = tile_of(width)
    count = len(units) * len(units[0])
    chunks = len(units)
    total = sum(members * size for _, _, size in mine)

    def body(s, *refs):
        units_ref, mine_refs = refs[:count], refs[count : count + chunks]
        rest = refs[count + chunks : -1]
        turned = refs[-1]

        @pl.when(pl.program_id(0) == 0)
        def _():
            turned_into(turned, mine_refs, s)

        weight = jnp.dot(
            turned[...], stack_of(units_ref, members, s[0]), preferred_element_type=jnp.float32
        )
        if kept is None:
            numer_ref, kept_out, token_out = rest
            kept_out[...] = 0.5 * (numer_ref[...] - 0.004 * weight)
            token_out[...] = jnp.zeros((8, 128), jnp.float32)
        else:
            kept_ref, inbox_ref, _, new_out, kept_out = rest
            now = kept_ref[...] - 0.5 * 0.004 * weight
            new_out[...] = now + inbox_ref[...]
            kept_out[...] = now.astype(jnp.bfloat16)

    columns = (rows, tile), lambda j, s: (0, j)
    whole = ((rows, width), jnp.float32) + columns
    return call(
        body,
        "weight_step",
        (width // tile,),
        unit_ins(units, tile)
        + mine_ins(mine)
        + ([(numer,) + columns] if kept is None else [(kept,) + columns, (inbox,) + columns, token_in(token)]),
        [whole, TOKEN_OUT]
        if kept is None
        else [whole, ((rows, width), jnp.bfloat16) + columns],
        scalars=(order,),
        scratch=[pltpu.VMEM((rows, total), jnp.bfloat16)],
        flops=2 * total * rows * width,
        moved=2 * count * units[0][0].shape[0] * width + 12 * rows * width,
        vmem=26,
    )


def grad_rows(units, weights, order):
    members = (len(units[0]) + 1) // 2
    sizes = [chunk[0].shape[0] for chunk in units]
    rows, width = weights.shape
    tile = tile_of(width)
    steps = width // tile
    count = len(units) * len(units[0])
    total = members * sum(sizes)

    def body(s, *refs):
        weights_ref, grad_ref, acc = refs[count:]
        j = pl.program_id(0)
        grad = lax.dot_general(
            stack_of(refs[:count], members, s[0]),
            weights_ref[...],
            (((1,), (1,)), ((), ())),
            preferred_element_type=jnp.float32,
        )

        @pl.when(j == 0)
        def _():
            acc[...] = grad

        @pl.when(j > 0)
        def _():
            acc[...] += grad

        @pl.when(j == steps - 1)
        def _():
            at, row = 0, 0
            for size in sizes:
                for k in range(members):
                    grad_ref[s[k], row : row + size] = acc[at : at + size].astype(jnp.bfloat16)
                    at += size
                row += size

    return call(
        body,
        "grad_rows",
        (steps,),
        unit_ins(units, tile) + [(weights, (rows, tile), lambda j, s: (0, j))],
        [
            (
                (members, sum(sizes), rows),
                jnp.bfloat16,
                (members, sum(sizes), rows),
                fixed(0, 0, 0),
            )
        ],
        scalars=(order,),
        scratch=[pltpu.VMEM((total, rows), jnp.float32)],
        flops=2 * total * rows * width,
        moved=2 * count * sizes[0] * width + 2 * rows * width,
        vmem=50,
    )[0]


def passed(right, left, token):
    size, width = right.shape
    step = size // 2

    def body(right_ref, left_ref, token_ref, right_out, left_out):
        right_out[...] = right_ref[...]
        left_out[...] = left_ref[...]

    here = (step, width), lambda i: (i, 0)
    flat = ((size, width), right.dtype) + here
    return call(
        body,
        "passed",
        (size // step,),
        [(right,) + here, (left,) + here, token_in(token)],
        [flat, flat],
        moved=8 * size * width,
    )


def joined_rows(blocks):
    members, tokens, rows = blocks.shape
    step = 96

    def body(blocks_ref, out_ref):
        for k in range(members):
            out_ref[:, k * rows : (k + 1) * rows] = blocks_ref[k]

    return call(
        body,
        "joined_rows",
        (tokens // step,),
        [(blocks, (members, step, rows), lambda i: (0, i, 0))],
        [
            (
                (tokens, members * rows),
                blocks.dtype,
                (step, members * rows),
                lambda i: (i, 0),
            )
        ],
        moved=4 * members * tokens * rows,
    )[0]


def widened(value):
    rows, width = value.shape
    step = rows // 2

    def body(value_ref, out_ref):
        out_ref[...] = value_ref[...].astype(jnp.float32)

    block = (step, width), lambda i: (i, 0)
    return call(
        body,
        "widened",
        (rows // step,),
        [(value,) + block],
        [((rows, width), jnp.float32) + block],
        moved=6 * rows * width,
        vmem=20,
    )[0]


def swapped(blocks):
    return lax.all_to_all(blocks, "fsdp", 0, 0, tiled=False)


def tail(kept, units, weights, order, bit_place):
    length = lax.axis_size("rep")
    sent = lax.ppermute(
        kept, "rep", [(i, (i + (1 << bit_place)) % length) for i in range(length)]
    )
    return sent, joined_rows(swapped(grad_rows(units, weights, order)))


def local(
    params, push_weight, inbox_params, inbox_weight, heads, residual, cotangent, gain, offset
):
    numer = params[0]
    weight_one = push_weight[0]
    members = lax.axis_size("fsdp")
    me = lax.axis_index("fsdp").astype(jnp.int32)
    tokens, inner = heads.shape[1:]
    rows, width = numer.shape
    scaling = inner ** (-0.5)
    rounds = len(STREAMS[0])
    assert sum(map(sum, STREAMS)) == tokens

    replicas = lax.axis_size("rep")
    levels = replicas.bit_length() - 1
    powers = jnp.left_shift(jnp.ones((levels,), jnp.int32), jnp.arange(levels, dtype=jnp.int32))
    level_index = jnp.sum(jnp.where(powers == offset[0], jnp.arange(levels, dtype=jnp.int32), 0))

    def sent_weight(token):
        half = 0.5 * push_weight + token[0, :1]
        arrived = [
            lax.ppermute(half, "rep", [(i, (i + (1 << b)) % replicas) for i in range(replicas)])
            for b in range(levels)
        ]
        chosen = arrived[0]
        for b in range(1, levels):
            chosen = jnp.where(level_index == b, arrived[b], chosen)
        return chosen

    order = jnp.mod(me - jnp.arange(members, dtype=jnp.int32), members)
    own = me[None]
    weights = scaled_weights(numer, weight_one, scaling)
    everyone = range(members - 1), range(1, members)

    def scalars(t):
        ahead = members - 1 - t
        return jnp.stack(
            [
                jnp.minimum(me + ahead, members - 1),
                (me <= t).astype(jnp.int32),
                jnp.maximum(me - ahead, 0),
                (me >= ahead).astype(jnp.int32),
            ]
        )

    at = 0
    starts = []
    for e in range(rounds):
        starts.append([])
        for sizes in STREAMS:
            starts[e].append(at)
            at += sizes[e]

    count = len(STREAMS)
    mine = [[None] * count for _ in range(rounds)]
    units = [[None] * count for _ in range(rounds)]
    before = [None] * count
    hint = [None] * count

    def fetch(e, members_of, token):
        size = STREAMS[members_of[0]][e]
        piece = cut_heads(
            heads[0], starts[e][members_of[0]], size * len(members_of), members, token
        )
        array = swapped(piece)
        for index, q in enumerate(members_of):
            mine[e][q] = (array, index, size)

    fetch(0, list(range(count)), None)
    parts = [None] * count
    for q in range(count):
        parts[q], _, last, first = partial_products(mine[0][q], weights, True)
        hint[q] = (last, first)
    for e in range(rounds):
        moving = [None] * count
        for q in range(count):
            if e == 0:
                moving[q] = hops(*hint[q], range(1), range(members - 1, members))
            else:
                right, left, _ = next_payload(*before[q], parts[q], scalars(0), True)
                moving[q] = hops(right, left, *everyone)
                units[e - 1][q][1].append(moving[q][0])
                units[e - 1][q][2].append(moving[q][1])
        for t in range(1, members - 1):
            for q in range(count):
                right, left, token = next_payload(*moving[q], parts[q], scalars(t), False)
                if t == 1 and q == 0 and e + 1 < rounds:
                    fetch(e + 1, list(range(count)), token)
                if t == 1 and q == 0 and e + 1 == rounds:
                    outbox_weight = sent_weight(token)
                if e == 0:
                    pairs = range(t + 1), range(members - 1 - t, members)
                else:
                    pairs = everyone
                moving[q] = hops(right, left, *pairs)
                if e > 0 and t < members - 2:
                    units[e - 1][q][1].append(moving[q][0])
                    units[e - 1][q][2].append(moving[q][1])
        later = [None] * count
        for q in range(count):
            token = None
            if e + 1 < rounds:
                later[q], token = partial_products(mine[e + 1][q], weights, False)
            unit = unit_gradient(
                *moving[q],
                parts[q],
                own,
                residual[0],
                cotangent[0],
                gain[None],
                starts[e][q],
                token,
            )
            before[q] = hops(unit, unit, *everyone)
            units[e][q] = (unit, [before[q][0]], [before[q][1]])
        parts = later
    kept = None
    for s in range(1, members - 1):
        for q in range(count):
            if (s, q) == (1, count - 1):
                early = [[u] + r + l for of_round in units[:-1] for u, r, l in of_round]
                kept, done = weight_step(
                    early, [m for of_round in mine[:-1] for m in of_round], order, None, numer, None
                )
                before[q] = passed(*before[q], done)
            before[q] = hops(*before[q], range(s, members - 1), range(1, members - s))
            units[-1][q][1].append(before[q][0])
            units[-1][q][2].append(before[q][1])
    flat = [[u] + r + l for u, r, l in units[-1]]
    late = jnp.broadcast_to(outbox_weight[None], (8, 128))
    new_params, half = weight_step(flat, mine[-1], order, kept, None, inbox_params[0], late)
    new_weight = 0.5 * push_weight + inbox_weight
    branches = [partial(tail, half, early + flat, weights, order, place) for place in range(levels)]
    sent, grad_heads = lax.switch(level_index, branches)
    return (new_params[None], new_weight, widened(sent)[None], outbox_weight, grad_heads[None])


def solution(mesh):
    placed = (
        P("rep", "fsdp", None),
        P("rep"),
        P("rep", "fsdp", None),
        P("rep"),
        P("rep", "fsdp", None),
        P("rep", "fsdp", None),
        P("rep", "fsdp", None),
        P(),
        P(),
    )
    return jax.shard_map(
        local,
        mesh=mesh,
        in_specs=placed,
        out_specs=(
            P("rep", "fsdp", None),
            P("rep"),
            P("rep", "fsdp", None),
            P("rep"),
            P("rep", "fsdp", None),
        ),
        check_vma=False,
    )
```

```python
from functools import partial

import jax
import jax.numpy as jnp
from jax import lax
from jax.experimental import pallas as pl
from jax.experimental.pallas import tpu as pltpu
from jax.sharding import PartitionSpec as P

STREAMS = ((96, 96), (96, 96))
MIB = 1 << 20
TOKEN = jax.ShapeDtypeStruct((8, 128), jnp.float32)


def call(body, name, grid, ins, outs, scalars=(), scratch=(), flops=0, moved=0, vmem=12):
    return pl.pallas_call(
        body,
        name=name,
        out_shape=[jax.ShapeDtypeStruct(shape, kind) for shape, kind, _, _ in outs],
        grid_spec=pltpu.PrefetchScalarGridSpec(
            num_scalar_prefetch=len(scalars),
            grid=grid,
            in_specs=[pl.BlockSpec(block, place) for _, block, place in ins],
            out_specs=[pl.BlockSpec(block, place) for _, _, block, place in outs],
            scratch_shapes=scratch,
        ),
        compiler_params=pltpu.CompilerParams(vmem_limit_bytes=vmem * MIB),
        cost_estimate=pl.CostEstimate(flops=flops, bytes_accessed=moved, transcendentals=0),
    )(*scalars, *(array for array, _, _ in ins))


def fixed(*place):
    return lambda *_: place


def token_in(token):
    return (token, (8, 128), fixed(0, 0))


TOKEN_OUT = ((8, 128), jnp.float32, (8, 128), fixed(0, 0))


def hop(value, step, pairs):
    return lax.ppermute(value, "fsdp", [(i, i + step) for i in pairs])


def hops(right, left, rights, lefts):
    return hop(right, 1, rights), hop(left, -1, lefts)


def tile_of(width, most=512):
    tile = most
    while width % tile:
        tile //= 2
    return tile


def cut_heads(heads, start, size, members, token):
    inner = heads.shape[1]
    rows = inner // members
    step = size // 2

    def body(heads_ref, *refs):
        for k in range(members):
            refs[-1][k] = heads_ref[:, k * rows : (k + 1) * rows]

    return call(
        body,
        "cut_heads",
        (size // step,),
        [(heads, (step, inner), lambda i: (start // step + i, 0))]
        + ([] if token is None else [token_in(token)]),
        [((members, size, rows), heads.dtype, (members, step, rows), lambda i: (0, i, 0))],
        moved=4 * size * inner,
        vmem=12 if start else 56,
    )[0]


def scaled_weights(numer, weight_one, scaling):
    rows, width = numer.shape
    step = rows // 4

    def body(numer_ref, one_ref, out_ref, token_out):
        out_ref[...] = (numer_ref[...] / one_ref[...] * scaling).astype(jnp.bfloat16)
        token_out[...] = jnp.zeros((8, 128), jnp.float32)

    block = (step, width), lambda i: (i, 0)
    return call(
        body,
        "scaled_weights",
        (rows // step,),
        [(numer,) + block, (weight_one.reshape(1, 1), (1, 1), fixed(0, 0))],
        [((rows, width), jnp.bfloat16) + block, TOKEN_OUT],
        flops=2 * rows * width,
        moved=6 * rows * width,
        vmem=56,
    )


def partial_products(mine, weights, ends):
    mine, index, size = mine
    members, _, rows = mine.shape
    width = weights.shape[1]
    tile = tile_of(width, 1280)

    def body(mine_ref, weights_ref, out_ref, token_out, *end_refs):
        product = jnp.dot(
            mine_ref[...].reshape(members * size, rows),
            weights_ref[...],
            preferred_element_type=jnp.float32,
        ).astype(jnp.bfloat16)
        out_ref[...] = product.reshape(members, size, tile)
        token_out[...] = jnp.zeros((8, 128), jnp.float32)
        if ends:
            end_refs[0][...] = product[(members - 1) * size :]
            end_refs[1][...] = product[:size]

    flat = ((size, width), jnp.bfloat16, (size, tile), lambda j: (0, j))
    return call(
        body,
        "partial_products",
        (width // tile,),
        [
            (mine, (members, size, rows), fixed(0, index, 0)),
            (weights, (rows, tile), lambda j: (0, j)),
        ],
        [
            ((members, size, width), jnp.bfloat16, (members, size, tile), lambda j: (0, 0, j)),
            TOKEN_OUT,
        ]
        + [flat, flat] * ends,
        flops=2 * members * size * rows * width,
        moved=2 * (members * size * (rows + width) + rows * width),
        vmem=20,
    )


def next_payload(right, left, parts, scalars, pick):
    members, size, width = parts.shape
    step = size // 2

    def joined(arrived, part, counts):
        if pick:
            return jnp.where(counts, part, arrived)
        weight = jnp.where(counts, 1.0, 0.0)
        return (arrived.astype(jnp.float32) + weight * part.astype(jnp.float32)).astype(
            jnp.bfloat16
        )

    def body(s, right_ref, left_ref, of_right, of_left, right_out, left_out, token_out):
        right_out[...] = joined(right_ref[...], of_right[0], s[1] > 0)
        left_out[...] = joined(left_ref[...], of_left[0], s[3] > 0)
        token_out[...] = jnp.zeros((8, 128), jnp.float32)

    here = (step, width), lambda i, s: (i, 0)
    flat = ((size, width), jnp.bfloat16) + here
    return call(
        body,
        "next_payload",
        (size // step,),
        [
            (right,) + here,
            (left,) + here,
            (parts, (1, step, width), lambda i, s: (s[0], i, 0)),
            (parts, (1, step, width), lambda i, s: (s[2], i, 0)),
        ],
        [flat, flat, TOKEN_OUT],
        scalars=(scalars,),
        flops=2 * size * width,
        moved=12 * size * width,
    )


def unit_gradient(right, left, parts, place, residual, cotangent, gain, start, token):
    members, size, width = parts.shape
    step = size // 2

    def body(s, right_ref, left_ref, own_ref, residual_ref, cot_ref, gain_ref, *refs):
        product = (
            right_ref[...].astype(jnp.float32)
            + left_ref[...].astype(jnp.float32)
            + own_ref[0].astype(jnp.float32)
        )
        summed = residual_ref[...].astype(jnp.float32) + product
        inverse = lax.rsqrt(jnp.mean(summed * summed, axis=-1, keepdims=True) + 1e-05)
        scaled_cot = gain_ref[...] * cot_ref[...].astype(jnp.float32)
        along = jnp.mean(scaled_cot * summed, axis=-1, keepdims=True)
        refs[-1][...] = (
            inverse * scaled_cot - summed * (inverse * inverse * inverse * along)
        ).astype(jnp.bfloat16)

    here = (step, width), lambda i, s: (i, 0)
    there = (step, width), lambda i, s: (start // step + i, 0)
    return call(
        body,
        "unit_gradient",
        (size // step,),
        [
            (right,) + here,
            (left,) + here,
            (parts, (1, step, width), lambda i, s: (s[0], i, 0)),
            (residual,) + there,
            (cotangent,) + there,
            (gain, (1, width), fixed(0, 0)),
        ]
        + ([] if token is None else [token_in(token)]),
        [((size, width), jnp.bfloat16) + here],
        scalars=(place,),
        flops=12 * size * width,
        moved=12 * size * width,
    )[0]


def stack_of(refs, members, me):
    count = 2 * members - 1
    rows = []
    for c in range(len(refs) // count):
        own, rights, lefts = (
            refs[c * count],
            refs[c * count + 1 : c * count + members],
            refs[c * count + members : (c + 1) * count],
        )
        rows.append(own[...])
        for k in range(members - 1):
            rows.append(jnp.where(me > k, rights[k][...], lefts[members - 2 - k][...]))
    return jnp.concatenate(rows, axis=0)


def unit_ins(units, tile):
    ins = []
    for chunk in units:
        block = (chunk[0].shape[0], tile)
        members = (len(chunk) + 1) // 2
        ins.append((chunk[0], block, lambda j, s: (0, j)))
        for k in range(members - 1):
            place = lambda j, s, k=k: (0, jnp.where(s[0] > k, j, 0))
            ins.append((chunk[1 + k], block, place))
        for m in range(members - 1):
            place = lambda j, s, k=members - 2 - m: (0, jnp.where(s[0] > k, 0, j))
            ins.append((chunk[members + m], block, place))
    return ins


def mine_ins(mine):
    return [
        (array, (array.shape[0], size, array.shape[2]), fixed(0, index, 0))
        for array, index, size in mine
    ]


def turned_into(scratch, mine_refs, order):
    members = mine_refs[0].shape[0]
    stack = jnp.concatenate([ref[order[k]] for ref in mine_refs for k in range(members)], axis=0)
    scratch[...] = stack.T


def weight_step(units, mine, order, kept, numer, inbox):
    members, _, rows = mine[0][0].shape
    width = numer.shape[1] if kept is None else kept.shape[1]
    tile = tile_of(width)
    count = len(units) * len(units[0])
    chunks = len(units)
    total = sum(members * size for _, _, size in mine)

    def body(s, *refs):
        units_ref, mine_refs = refs[:count], refs[count : count + chunks]
        rest = refs[count + chunks : -1]
        turned = refs[-1]

        @pl.when(pl.program_id(0) == 0)
        def _():
            turned_into(turned, mine_refs, s)

        weight = jnp.dot(
            turned[...], stack_of(units_ref, members, s[0]), preferred_element_type=jnp.float32
        )
        if kept is None:
            numer_ref, kept_out, token_out = rest
            kept_out[...] = 0.5 * (numer_ref[...] - 0.004 * weight)
            token_out[...] = jnp.zeros((8, 128), jnp.float32)
        else:
            kept_ref, inbox_ref, new_out, kept_out = rest
            now = kept_ref[...] - 0.5 * 0.004 * weight
            new_out[...] = now + inbox_ref[...]
            kept_out[...] = now.astype(jnp.bfloat16)

    columns = (rows, tile), lambda j, s: (0, j)
    whole = ((rows, width), jnp.float32) + columns
    return call(
        body,
        "weight_step",
        (width // tile,),
        unit_ins(units, tile)
        + mine_ins(mine)
        + ([(numer,) + columns] if kept is None else [(kept,) + columns, (inbox,) + columns]),
        [whole, TOKEN_OUT]
        if kept is None
        else [whole, ((rows, width), jnp.bfloat16) + columns],
        scalars=(order,),
        scratch=[pltpu.VMEM((rows, total), jnp.bfloat16)],
        flops=2 * total * rows * width,
        moved=2 * count * units[0][0].shape[0] * width + 12 * rows * width,
        vmem=52,
    )


def grad_rows(units, weights, order):
    members = (len(units[0]) + 1) // 2
    sizes = [chunk[0].shape[0] for chunk in units]
    rows, width = weights.shape
    tile = tile_of(width)
    steps = width // tile
    count = len(units) * len(units[0])
    total = members * sum(sizes)

    def body(s, *refs):
        weights_ref, grad_ref, acc = refs[count:]
        j = pl.program_id(0)
        grad = lax.dot_general(
            stack_of(refs[:count], members, s[0]),
            weights_ref[...],
            (((1,), (1,)), ((), ())),
            preferred_element_type=jnp.float32,
        )

        @pl.when(j == 0)
        def _():
            acc[...] = grad

        @pl.when(j > 0)
        def _():
            acc[...] += grad

        @pl.when(j == steps - 1)
        def _():
            at, row = 0, 0
            for size in sizes:
                for k in range(members):
                    grad_ref[s[k], row : row + size] = acc[at : at + size].astype(jnp.bfloat16)
                    at += size
                row += size

    return call(
        body,
        "grad_rows",
        (steps,),
        unit_ins(units, tile) + [(weights, (rows, tile), lambda j, s: (0, j))],
        [
            (
                (members, sum(sizes), rows),
                jnp.bfloat16,
                (members, sum(sizes), rows),
                fixed(0, 0, 0),
            )
        ],
        scalars=(order,),
        scratch=[pltpu.VMEM((total, rows), jnp.float32)],
        flops=2 * total * rows * width,
        moved=2 * count * sizes[0] * width + 2 * rows * width,
        vmem=50,
    )[0]


def passed(right, left, token):
    size, width = right.shape
    step = size // 2

    def body(right_ref, left_ref, token_ref, right_out, left_out):
        right_out[...] = right_ref[...]
        left_out[...] = left_ref[...]

    here = (step, width), lambda i: (i, 0)
    flat = ((size, width), right.dtype) + here
    return call(
        body,
        "passed",
        (size // step,),
        [(right,) + here, (left,) + here, token_in(token)],
        [flat, flat],
        moved=8 * size * width,
    )


def joined_rows(blocks):
    members, tokens, rows = blocks.shape
    step = 96

    def body(blocks_ref, out_ref):
        for k in range(members):
            out_ref[:, k * rows : (k + 1) * rows] = blocks_ref[k]

    return call(
        body,
        "joined_rows",
        (tokens // step,),
        [(blocks, (members, step, rows), lambda i: (0, i, 0))],
        [
            (
                (tokens, members * rows),
                blocks.dtype,
                (step, members * rows),
                lambda i: (i, 0),
            )
        ],
        moved=4 * members * tokens * rows,
    )[0]


def widened(value):
    rows, width = value.shape
    step = rows // 2

    def body(value_ref, out_ref):
        out_ref[...] = value_ref[...].astype(jnp.float32)

    block = (step, width), lambda i: (i, 0)
    return call(
        body,
        "widened",
        (rows // step,),
        [(value,) + block],
        [((rows, width), jnp.float32) + block],
        moved=6 * rows * width,
        vmem=20,
    )[0]


def swapped(blocks):
    return lax.all_to_all(blocks, "fsdp", 0, 0, tiled=False)


def tail(kept, units, weights, order, bit_place):
    length = lax.axis_size("rep")
    sent = lax.ppermute(
        kept, "rep", [(i, (i + (1 << bit_place)) % length) for i in range(length)]
    )
    return sent, joined_rows(swapped(grad_rows(units, weights, order)))


def local(
    params, push_weight, inbox_params, inbox_weight, heads, residual, cotangent, gain, offset
):
    numer = params[0]
    weight_one = push_weight[0]
    members = lax.axis_size("fsdp")
    me = lax.axis_index("fsdp").astype(jnp.int32)
    tokens, inner = heads.shape[1:]
    rows, width = numer.shape
    scaling = inner ** (-0.5)
    rounds = len(STREAMS[0])
    assert sum(map(sum, STREAMS)) == tokens

    replicas = lax.axis_size("rep")
    levels = replicas.bit_length() - 1
    powers = jnp.left_shift(jnp.ones((levels,), jnp.int32), jnp.arange(levels, dtype=jnp.int32))
    level_index = jnp.sum(jnp.where(powers == offset[0], jnp.arange(levels, dtype=jnp.int32), 0))

    def sent_weight(token):
        half = 0.5 * push_weight + token[0, :1]
        arrived = [
            lax.ppermute(half, "rep", [(i, (i + (1 << b)) % replicas) for i in range(replicas)])
            for b in range(levels)
        ]
        chosen = arrived[0]
        for b in range(1, levels):
            chosen = jnp.where(level_index == b, arrived[b], chosen)
        return chosen

    order = jnp.mod(me - jnp.arange(members, dtype=jnp.int32), members)
    own = me[None]
    weights, token = scaled_weights(numer, weight_one, scaling)
    everyone = range(members - 1), range(1, members)

    def scalars(t):
        ahead = members - 1 - t
        return jnp.stack(
            [
                jnp.minimum(me + ahead, members - 1),
                (me <= t).astype(jnp.int32),
                jnp.maximum(me - ahead, 0),
                (me >= ahead).astype(jnp.int32),
            ]
        )

    at = 0
    starts = []
    for e in range(rounds):
        starts.append([])
        for sizes in STREAMS:
            starts[e].append(at)
            at += sizes[e]

    count = len(STREAMS)
    mine = [[None] * count for _ in range(rounds)]
    units = [[None] * count for _ in range(rounds)]
    before = [None] * count
    hint = [None] * count

    def fetch(e, members_of, token):
        size = STREAMS[members_of[0]][e]
        piece = cut_heads(
            heads[0], starts[e][members_of[0]], size * len(members_of), members, token
        )
        array = swapped(piece)
        for index, q in enumerate(members_of):
            mine[e][q] = (array, index, size)

    for q in range(count):
        fetch(0, [q], token if q else None)
    parts = [None] * count
    for q in range(count):
        parts[q], _, last, first = partial_products(mine[0][q], weights, True)
        hint[q] = (last, first)
    for e in range(rounds):
        moving = [None] * count
        for q in range(count):
            if e == 0:
                moving[q] = hops(*hint[q], range(1), range(members - 1, members))
            else:
                right, left, _ = next_payload(*before[q], parts[q], scalars(0), True)
                moving[q] = hops(right, left, *everyone)
                units[e - 1][q][1].append(moving[q][0])
                units[e - 1][q][2].append(moving[q][1])
        for t in range(1, members - 1):
            for q in range(count):
                right, left, token = next_payload(*moving[q], parts[q], scalars(t), False)
                if t == 1 and e + 1 < rounds:
                    fetch(e + 1, [q], token)
                if e == 0:
                    pairs = range(t + 1), range(members - 1 - t, members)
                else:
                    pairs = everyone
                moving[q] = hops(right, left, *pairs)
                if e > 0 and t < members - 2:
                    units[e - 1][q][1].append(moving[q][0])
                    units[e - 1][q][2].append(moving[q][1])
        later = [None] * count
        for q in range(count):
            token = None
            if e + 1 < rounds:
                later[q], token = partial_products(mine[e + 1][q], weights, False)
            unit = unit_gradient(
                *moving[q],
                parts[q],
                own,
                residual[0],
                cotangent[0],
                gain[None],
                starts[e][q],
                token,
            )
            before[q] = hops(unit, unit, *everyone)
            units[e][q] = (unit, [before[q][0]], [before[q][1]])
        parts = later
    kept = None
    for s in range(1, members - 1):
        for q in range(count):
            if (s, q) == (1, count - 1):
                early = [[u] + r + l for of_round in units[:-1] for u, r, l in of_round]
                kept, done = weight_step(
                    early, [m for of_round in mine[:-1] for m in of_round], order, None, numer, None
                )
                before[q] = passed(*before[q], done)
                outbox_weight = sent_weight(done)
            if (s, q) == (2, 0):
                before[q] = passed(*before[q], jnp.broadcast_to(outbox_weight[None], (8, 128)))
            before[q] = hops(*before[q], range(s, members - 1), range(1, members - s))
            units[-1][q][1].append(before[q][0])
            units[-1][q][2].append(before[q][1])
    flat = [[u] + r + l for u, r, l in units[-1]]
    new_params, half = weight_step(flat, mine[-1], order, kept, None, inbox_params[0])
    new_weight = 0.5 * push_weight + inbox_weight
    branches = [partial(tail, half, early + flat, weights, order, place) for place in range(levels)]
    sent, grad_heads = lax.switch(level_index, branches)
    return (new_params[None], new_weight, widened(sent)[None], outbox_weight, grad_heads[None])


def solution(mesh):
    placed = (
        P("rep", "fsdp", None),
        P("rep"),
        P("rep", "fsdp", None),
        P("rep"),
        P("rep", "fsdp", None),
        P("rep", "fsdp", None),
        P("rep", "fsdp", None),
        P(),
        P(),
    )
    return jax.shard_map(
        local,
        mesh=mesh,
        in_specs=placed,
        out_specs=(
            P("rep", "fsdp", None),
            P("rep"),
            P("rep", "fsdp", None),
            P("rep"),
            P("rep", "fsdp", None),
        ),
        check_vma=False,
    )
```

```python
from functools import partial

import jax
import jax.numpy as jnp
from jax import lax
from jax.experimental import pallas as pl
from jax.experimental.pallas import tpu as pltpu
from jax.sharding import PartitionSpec as P

STREAMS = ((96, 96), (96, 96))
MIB = 1 << 20
TOKEN = jax.ShapeDtypeStruct((8, 128), jnp.float32)


def call(body, name, grid, ins, outs, scalars=(), scratch=(), flops=0, moved=0, vmem=12, aliases=None):
    return pl.pallas_call(
        body,
        name=name,
        out_shape=[jax.ShapeDtypeStruct(shape, kind) for shape, kind, _, _ in outs],
        grid_spec=pltpu.PrefetchScalarGridSpec(
            num_scalar_prefetch=len(scalars),
            grid=grid,
            in_specs=[pl.BlockSpec(block, place) for _, block, place in ins],
            out_specs=[pl.BlockSpec(block, place) for _, _, block, place in outs],
            scratch_shapes=scratch,
        ),
        input_output_aliases=aliases or {},
        compiler_params=pltpu.CompilerParams(vmem_limit_bytes=vmem * MIB),
        cost_estimate=pl.CostEstimate(flops=flops, bytes_accessed=moved, transcendentals=0),
    )(*scalars, *(array for array, _, _ in ins))


def fixed(*place):
    return lambda *_: place


def token_in(token):
    return (token, (8, 128), fixed(0, 0))


TOKEN_OUT = ((8, 128), jnp.float32, (8, 128), fixed(0, 0))


def hop(value, step, pairs):
    return lax.ppermute(value, "fsdp", [(i, i + step) for i in pairs])


def hops(right, left, rights, lefts):
    return hop(right, 1, rights), hop(left, -1, lefts)


def tile_of(width, most=512):
    tile = most
    while width % tile:
        tile //= 2
    return tile


def cut_heads(heads, start, size, members, token):
    inner = heads.shape[1]
    rows = inner // members
    step = size // 2

    def body(heads_ref, *refs):
        for k in range(members):
            refs[-1][k] = heads_ref[:, k * rows : (k + 1) * rows]

    return call(
        body,
        "cut_heads",
        (size // step,),
        [(heads, (step, inner), lambda i: (start // step + i, 0))]
        + ([] if token is None else [token_in(token)]),
        [((members, size, rows), heads.dtype, (members, step, rows), lambda i: (0, i, 0))],
        moved=4 * size * inner,
        vmem=12 if start else 56,
    )[0]


def scaled_weights(numer, weight_one, scaling):
    rows, width = numer.shape
    step = rows // 4

    def body(numer_ref, one_ref, out_ref, token_out):
        out_ref[...] = (numer_ref[...] / one_ref[...] * scaling).astype(jnp.bfloat16)
        token_out[...] = jnp.zeros((8, 128), jnp.float32)

    block = (step, width), lambda i: (i, 0)
    return call(
        body,
        "scaled_weights",
        (rows // step,),
        [(numer,) + block, (weight_one.reshape(1, 1), (1, 1), fixed(0, 0))],
        [((rows, width), jnp.bfloat16) + block, TOKEN_OUT],
        flops=2 * rows * width,
        moved=6 * rows * width,
        vmem=56,
    )


def partial_products(mine, weights, ends, token=None):
    mine, index, size = mine
    members, _, rows = mine.shape
    width = weights.shape[1]
    tile = tile_of(width, 1280)

    def body(mine_ref, weights_ref, *refs):
        out_ref, token_out, *end_refs = refs[0 if token is None else 1 :]
        product = jnp.dot(
            mine_ref[...].reshape(members * size, rows),
            weights_ref[...],
            preferred_element_type=jnp.float32,
        ).astype(jnp.bfloat16)
        out_ref[...] = product.reshape(members, size, tile)
        token_out[...] = jnp.zeros((8, 128), jnp.float32)
        if ends:
            end_refs[0][...] = product[(members - 1) * size :]
            end_refs[1][...] = product[:size]

    flat = ((size, width), jnp.bfloat16, (size, tile), lambda j: (0, j))
    return call(
        body,
        "partial_products",
        (width // tile,),
        [
            (mine, (members, size, rows), fixed(0, index, 0)),
            (weights, (rows, tile), lambda j: (0, j)),
        ]
        + ([] if token is None else [token_in(token)]),
        [
            ((members, size, width), jnp.bfloat16, (members, size, tile), lambda j: (0, 0, j)),
            TOKEN_OUT,
        ]
        + [flat, flat] * ends,
        flops=2 * members * size * rows * width,
        moved=2 * (members * size * (rows + width) + rows * width),
        vmem=20,
    )


def next_payload(right, left, parts, scalars, pick, token=None):
    members, size, width = parts.shape
    step = size // 2

    def joined(arrived, part, counts):
        if pick:
            return jnp.where(counts, part, arrived)
        weight = jnp.where(counts, 1.0, 0.0)
        return (arrived.astype(jnp.float32) + weight * part.astype(jnp.float32)).astype(
            jnp.bfloat16
        )

    def body(s, right_ref, left_ref, of_right, of_left, *refs):
        right_out, left_out, token_out = refs[-3:]
        right_out[...] = joined(right_ref[...], of_right[0], s[1] > 0)
        left_out[...] = joined(left_ref[...], of_left[0], s[3] > 0)
        token_out[...] = jnp.zeros((8, 128), jnp.float32)

    here = (step, width), lambda i, s: (i, 0)
    flat = ((size, width), jnp.bfloat16) + here
    return call(
        body,
        "next_payload",
        (size // step,),
        [
            (right,) + here,
            (left,) + here,
            (parts, (1, step, width), lambda i, s: (s[0], i, 0)),
            (parts, (1, step, width), lambda i, s: (s[2], i, 0)),
        ]
        + ([] if token is None else [token_in(token)]),
        [flat, flat, TOKEN_OUT],
        scalars=(scalars,),
        flops=2 * size * width,
        moved=12 * size * width,
    )


def unit_gradient(right, left, parts, place, residual, cotangent, gain, start, token):
    members, size, width = parts.shape
    step = size // 2

    def body(s, right_ref, left_ref, own_ref, residual_ref, cot_ref, gain_ref, *refs):
        product = (
            right_ref[...].astype(jnp.float32)
            + left_ref[...].astype(jnp.float32)
            + own_ref[0].astype(jnp.float32)
        )
        summed = residual_ref[...].astype(jnp.float32) + product
        inverse = lax.rsqrt(jnp.mean(summed * summed, axis=-1, keepdims=True) + 1e-05)
        scaled_cot = gain_ref[...] * cot_ref[...].astype(jnp.float32)
        along = jnp.mean(scaled_cot * summed, axis=-1, keepdims=True)
        refs[-1][...] = (
            inverse * scaled_cot - summed * (inverse * inverse * inverse * along)
        ).astype(jnp.bfloat16)

    here = (step, width), lambda i, s: (i, 0)
    there = (step, width), lambda i, s: (start // step + i, 0)
    return call(
        body,
        "unit_gradient",
        (size // step,),
        [
            (right,) + here,
            (left,) + here,
            (parts, (1, step, width), lambda i, s: (s[0], i, 0)),
            (residual,) + there,
            (cotangent,) + there,
            (gain, (1, width), fixed(0, 0)),
        ]
        + ([] if token is None else [token_in(token)]),
        [((size, width), jnp.bfloat16) + here],
        scalars=(place,),
        flops=12 * size * width,
        moved=12 * size * width,
    )[0]


def stack_of(refs, members, me):
    count = 2 * members - 1
    rows = []
    for c in range(len(refs) // count):
        own, rights, lefts = (
            refs[c * count],
            refs[c * count + 1 : c * count + members],
            refs[c * count + members : (c + 1) * count],
        )
        rows.append(own[...])
        for k in range(members - 1):
            rows.append(jnp.where(me > k, rights[k][...], lefts[members - 2 - k][...]))
    return jnp.concatenate(rows, axis=0)


def unit_ins(units, tile, first=0):
    ins = []
    for chunk in units:
        block = (chunk[0].shape[0], tile)
        members = (len(chunk) + 1) // 2
        ins.append((chunk[0], block, lambda j, s: (0, j + first)))
        for k in range(members - 1):
            place = lambda j, s, k=k: (0, jnp.where(s[0] > k, j, 0) + first)
            ins.append((chunk[1 + k], block, place))
        for m in range(members - 1):
            place = lambda j, s, k=members - 2 - m: (0, jnp.where(s[0] > k, 0, j) + first)
            ins.append((chunk[members + m], block, place))
    return ins


def mine_ins(mine):
    return [
        (array, (array.shape[0], size, array.shape[2]), fixed(0, index, 0))
        for array, index, size in mine
    ]


def turned_into(scratch, mine_refs, order):
    members = mine_refs[0].shape[0]
    stack = jnp.concatenate([ref[order[k]] for ref in mine_refs for k in range(members)], axis=0)
    scratch[...] = stack.T


def weight_step(units, mine, order, base, first, last, inbox=None, kept=None, new=False, token=None):
    members, _, rows = mine[0][0].shape
    width = base.shape[1]
    tile = tile_of(width)
    last = width // tile if last is None else last
    count = len(units) * len(units[0])
    chunks = len(units)
    total = sum(members * size for _, _, size in mine)
    early = inbox is None

    def body(s, *refs):
        units_ref, mine_refs = refs[:count], refs[count : count + chunks]
        base_ref = refs[count + chunks]
        turned = refs[-1]

        @pl.when(pl.program_id(0) == 0)
        def _():
            turned_into(turned, mine_refs, s)

        weight = jnp.dot(
            turned[...], stack_of(units_ref, members, s[0]), preferred_element_type=jnp.float32
        )
        if early:
            refs[-3][...] = 0.5 * (base_ref[...] - 0.004 * weight)
            refs[-2][...] = jnp.zeros((8, 128), jnp.float32)
        else:
            now = base_ref[...] - 0.5 * 0.004 * weight
            if new:
                refs[-2][...] = now + refs[count + chunks + 1][...]
            else:
                refs[-2][...] = now.astype(jnp.bfloat16)

    columns = (rows, tile), lambda j, s: (0, j + first)
    ins = unit_ins(units, tile, first) + mine_ins(mine) + [(base,) + columns]
    if new:
        ins.append((inbox,) + columns)
    if kept is not None:
        ins.append((kept, (8, 128), fixed(0, 0)))
    if token is not None:
        ins.append(token_in(token))
    kind = jnp.float32 if early or new else jnp.bfloat16
    outs = [((rows, width), kind) + columns]
    return call(
        body,
        "weight_step",
        (last - first,),
        ins,
        outs + [TOKEN_OUT] * early,
        scalars=(order,),
        scratch=[pltpu.VMEM((rows, total), jnp.bfloat16)],
        flops=2 * total * rows * tile * (last - first),
        moved=(2 * count * units[0][0].shape[0] + 12 * rows) * tile * (last - first),
        vmem=52,
        aliases={} if kept is None else {1 + count + chunks + 1: 0},
    )


def grad_rows(units, weights, order):
    members = (len(units[0]) + 1) // 2
    sizes = [chunk[0].shape[0] for chunk in units]
    rows, width = weights.shape
    tile = tile_of(width)
    steps = width // tile
    count = len(units) * len(units[0])
    total = members * sum(sizes)

    def body(s, *refs):
        weights_ref, grad_ref, token_out, acc = refs[count:]
        token_out[...] = jnp.zeros((8, 128), jnp.float32)
        j = pl.program_id(0)
        grad = lax.dot_general(
            stack_of(refs[:count], members, s[0]),
            weights_ref[...],
            (((1,), (1,)), ((), ())),
            preferred_element_type=jnp.float32,
        )

        @pl.when(j == 0)
        def _():
            acc[...] = grad

        @pl.when(j > 0)
        def _():
            acc[...] += grad

        @pl.when(j == steps - 1)
        def _():
            at, row = 0, 0
            for size in sizes:
                for k in range(members):
                    grad_ref[s[k], row : row + size] = acc[at : at + size].astype(jnp.bfloat16)
                    at += size
                row += size

    return call(
        body,
        "grad_rows",
        (steps,),
        unit_ins(units, tile) + [(weights, (rows, tile), lambda j, s: (0, j))],
        [
            (
                (members, sum(sizes), rows),
                jnp.bfloat16,
                (members, sum(sizes), rows),
                fixed(0, 0, 0),
            ),
            TOKEN_OUT,
        ],
        scalars=(order,),
        scratch=[pltpu.VMEM((total, rows), jnp.float32)],
        flops=2 * total * rows * width,
        moved=2 * count * sizes[0] * width + 2 * rows * width,
        vmem=50,
    )


def passed(right, left, token):
    size, width = right.shape
    step = size // 2

    def body(right_ref, left_ref, token_ref, right_out, left_out):
        right_out[...] = right_ref[...]
        left_out[...] = left_ref[...]

    here = (step, width), lambda i: (i, 0)
    flat = ((size, width), right.dtype) + here
    return call(
        body,
        "passed",
        (size // step,),
        [(right,) + here, (left,) + here, token_in(token)],
        [flat, flat],
        moved=8 * size * width,
    )


def joined_rows(blocks):
    members, tokens, rows = blocks.shape
    step = 96

    def body(blocks_ref, out_ref):
        for k in range(members):
            out_ref[:, k * rows : (k + 1) * rows] = blocks_ref[k]

    return call(
        body,
        "joined_rows",
        (tokens // step,),
        [(blocks, (members, step, rows), lambda i: (0, i, 0))],
        [
            (
                (tokens, members * rows),
                blocks.dtype,
                (step, members * rows),
                lambda i: (i, 0),
            )
        ],
        moved=4 * members * tokens * rows,
    )[0]


def widened(value):
    rows, width = value.shape
    step = rows // 2

    def body(value_ref, out_ref):
        out_ref[...] = value_ref[...].astype(jnp.float32)

    block = (step, width), lambda i: (i, 0)
    return call(
        body,
        "widened",
        (rows // step,),
        [(value,) + block],
        [((rows, width), jnp.float32) + block],
        moved=6 * rows * width,
        vmem=20,
    )[0]


def swapped(blocks):
    return lax.all_to_all(blocks, "fsdp", 0, 0, tiled=False)


def tail(half, early, late, mine, kept, inbox, weights, order, bit_place):
    length = lax.axis_size("rep")
    sent = lax.ppermute(
        half, "rep", [(i, (i + (1 << bit_place)) % length) for i in range(length)]
    )
    grads, token = grad_rows(early + late, weights, order)
    back = swapped(grads)
    new = weight_step(late, mine, order, kept, 0, None, inbox, new=True, token=token)[0]
    return sent, joined_rows(back), new


def local(
    params, push_weight, inbox_params, inbox_weight, heads, residual, cotangent, gain, offset
):
    numer = params[0]
    weight_one = push_weight[0]
    members = lax.axis_size("fsdp")
    me = lax.axis_index("fsdp").astype(jnp.int32)
    tokens, inner = heads.shape[1:]
    rows, width = numer.shape
    scaling = inner ** (-0.5)
    rounds = len(STREAMS[0])
    assert sum(map(sum, STREAMS)) == tokens

    replicas = lax.axis_size("rep")
    levels = replicas.bit_length() - 1
    powers = jnp.left_shift(jnp.ones((levels,), jnp.int32), jnp.arange(levels, dtype=jnp.int32))
    level_index = jnp.sum(jnp.where(powers == offset[0], jnp.arange(levels, dtype=jnp.int32), 0))

    def sent_weight(token):
        half = 0.5 * push_weight + token[0, :1]
        arrived = [
            lax.ppermute(half, "rep", [(i, (i + (1 << b)) % replicas) for i in range(replicas)])
            for b in range(levels)
        ]
        chosen = arrived[0]
        for b in range(1, levels):
            chosen = jnp.where(level_index == b, arrived[b], chosen)
        return chosen

    order = jnp.mod(me - jnp.arange(members, dtype=jnp.int32), members)
    own = me[None]
    weights, token = scaled_weights(numer, weight_one, scaling)
    everyone = range(members - 1), range(1, members)

    def scalars(t):
        ahead = members - 1 - t
        return jnp.stack(
            [
                jnp.minimum(me + ahead, members - 1),
                (me <= t).astype(jnp.int32),
                jnp.maximum(me - ahead, 0),
                (me >= ahead).astype(jnp.int32),
            ]
        )

    at = 0
    starts = []
    for e in range(rounds):
        starts.append([])
        for sizes in STREAMS:
            starts[e].append(at)
            at += sizes[e]

    count = len(STREAMS)
    mine = [[None] * count for _ in range(rounds)]
    units = [[None] * count for _ in range(rounds)]
    before = [None] * count
    hint = [None] * count

    def fetch(e, members_of, token):
        size = STREAMS[members_of[0]][e]
        piece = cut_heads(
            heads[0], starts[e][members_of[0]], size * len(members_of), members, token
        )
        array = swapped(piece)
        for index, q in enumerate(members_of):
            mine[e][q] = (array, index, size)

    for q in range(count):
        fetch(0, [q], token if q else None)
    parts = [None] * count
    token = None
    for q in range(count):
        parts[q], token, last, first = partial_products(mine[0][q], weights, True, token)
        hint[q] = (last, first)
        if q == 0:
            outbox_weight = sent_weight(token)
            token = jnp.broadcast_to(outbox_weight[None], (8, 128))
    for e in range(rounds):
        moving = [None] * count
        for q in range(count):
            if e == 0:
                moving[q] = hops(*hint[q], range(1), range(members - 1, members))
            else:
                right, left, _ = next_payload(*before[q], parts[q], scalars(0), True)
                moving[q] = hops(right, left, *everyone)
                units[e - 1][q][1].append(moving[q][0])
                units[e - 1][q][2].append(moving[q][1])
        for t in range(1, members - 1):
            for q in range(count):
                right, left, token = next_payload(
                    *moving[q], parts[q], scalars(t), False, token if (e, t, q) == (0, 1, 0) else None
                )
                if t == 1 and e + 1 < rounds:
                    fetch(e + 1, [q], token)
                if e == 0:
                    pairs = range(t + 1), range(members - 1 - t, members)
                else:
                    pairs = everyone
                moving[q] = hops(right, left, *pairs)
                if e > 0 and t < members - 2:
                    units[e - 1][q][1].append(moving[q][0])
                    units[e - 1][q][2].append(moving[q][1])
        later = [None] * count
        for q in range(count):
            token = None
            if e + 1 < rounds:
                later[q], token = partial_products(mine[e + 1][q], weights, False)
            unit = unit_gradient(
                *moving[q],
                parts[q],
                own,
                residual[0],
                cotangent[0],
                gain[None],
                starts[e][q],
                token,
            )
            before[q] = hops(unit, unit, *everyone)
            units[e][q] = (unit, [before[q][0]], [before[q][1]])
        parts = later
    kept = None
    for s in range(1, members - 1):
        for q in range(count):
            if (s, q) == (1, count - 1):
                early = [[u] + r + l for of_round in units[:-1] for u, r, l in of_round]
                early_mine = [m for of_round in mine[:-1] for m in of_round]
                kept, done = weight_step(early, early_mine, order, numer, 0, 3)
                before[q] = passed(*before[q], done)
            if (s, q) == (2, 0):
                kept, done = weight_step(early, early_mine, order, numer, 3, None, kept=kept)
                before[q] = passed(*before[q], done)
            before[q] = hops(*before[q], range(s, members - 1), range(1, members - s))
            units[-1][q][1].append(before[q][0])
            units[-1][q][2].append(before[q][1])
    flat = [[u] + r + l for u, r, l in units[-1]]
    half = weight_step(flat, mine[-1], order, kept, 0, None, inbox_params[0])[0]
    new_weight = 0.5 * push_weight + inbox_weight
    branches = [
        partial(
            tail, half, early, flat, mine[-1], kept, inbox_params[0], weights, order, place
        )
        for place in range(levels)
    ]
    sent, grad_heads, new_params = lax.switch(level_index, branches)
    return (new_params[None], new_weight, widened(sent)[None], outbox_weight, grad_heads[None])


def solution(mesh):
    placed = (
        P("rep", "fsdp", None),
        P("rep"),
        P("rep", "fsdp", None),
        P("rep"),
        P("rep", "fsdp", None),
        P("rep", "fsdp", None),
        P("rep", "fsdp", None),
        P(),
        P(),
    )
    return jax.shard_map(
        local,
        mesh=mesh,
        in_specs=placed,
        out_specs=(
            P("rep", "fsdp", None),
            P("rep"),
            P("rep", "fsdp", None),
            P("rep"),
            P("rep", "fsdp", None),
        ),
        check_vma=False,
    )
```

```python
from functools import partial

import jax
import jax.numpy as jnp
from jax import lax
from jax.experimental import pallas as pl
from jax.experimental.pallas import tpu as pltpu
from jax.sharding import PartitionSpec as P

STREAMS = ((96, 96), (96, 96))
MIB = 1 << 20
TOKEN = jax.ShapeDtypeStruct((8, 128), jnp.float32)


def call(body, name, grid, ins, outs, scalars=(), scratch=(), flops=0, moved=0, vmem=12, aliases=None):
    return pl.pallas_call(
        body,
        name=name,
        out_shape=[jax.ShapeDtypeStruct(shape, kind) for shape, kind, _, _ in outs],
        grid_spec=pltpu.PrefetchScalarGridSpec(
            num_scalar_prefetch=len(scalars),
            grid=grid,
            in_specs=[pl.BlockSpec(block, place) for _, block, place in ins],
            out_specs=[pl.BlockSpec(block, place) for _, _, block, place in outs],
            scratch_shapes=scratch,
        ),
        input_output_aliases=aliases or {},
        compiler_params=pltpu.CompilerParams(vmem_limit_bytes=vmem * MIB),
        cost_estimate=pl.CostEstimate(flops=flops, bytes_accessed=moved, transcendentals=0),
    )(*scalars, *(array for array, _, _ in ins))


def fixed(*place):
    return lambda *_: place


def token_in(token):
    return (token, (8, 128), fixed(0, 0))


TOKEN_OUT = ((8, 128), jnp.float32, (8, 128), fixed(0, 0))


def hop(value, step, pairs):
    return lax.ppermute(value, "fsdp", [(i, i + step) for i in pairs])


def hops(right, left, rights, lefts):
    return hop(right, 1, rights), hop(left, -1, lefts)


def tile_of(width, most=512):
    tile = most
    while width % tile:
        tile //= 2
    return tile


def cut_heads(heads, start, size, members, token):
    inner = heads.shape[1]
    rows = inner // members
    step = size // 2

    def body(heads_ref, *refs):
        for k in range(members):
            refs[-1][k] = heads_ref[:, k * rows : (k + 1) * rows]

    return call(
        body,
        "cut_heads",
        (size // step,),
        [(heads, (step, inner), lambda i: (start // step + i, 0))]
        + ([] if token is None else [token_in(token)]),
        [((members, size, rows), heads.dtype, (members, step, rows), lambda i: (0, i, 0))],
        moved=4 * size * inner,
        vmem=12 if start else 56,
    )[0]


def scaled_weights(numer, weight_one, scaling):
    rows, width = numer.shape
    step = rows // 4

    def body(numer_ref, one_ref, out_ref, token_out):
        out_ref[...] = (numer_ref[...] / one_ref[...] * scaling).astype(jnp.bfloat16)
        token_out[...] = jnp.zeros((8, 128), jnp.float32)

    block = (step, width), lambda i: (i, 0)
    return call(
        body,
        "scaled_weights",
        (rows // step,),
        [(numer,) + block, (weight_one.reshape(1, 1), (1, 1), fixed(0, 0))],
        [((rows, width), jnp.bfloat16) + block, TOKEN_OUT],
        flops=2 * rows * width,
        moved=6 * rows * width,
        vmem=56,
    )


def partial_products(mine, weights, ends, token=None):
    mine, index, size = mine
    members, _, rows = mine.shape
    width = weights.shape[1]
    tile = tile_of(width, 1280)

    def body(mine_ref, weights_ref, *refs):
        out_ref, token_out, *end_refs = refs[0 if token is None else 1 :]
        product = jnp.dot(
            mine_ref[...].reshape(members * size, rows),
            weights_ref[...],
            preferred_element_type=jnp.float32,
        ).astype(jnp.bfloat16)
        out_ref[...] = product.reshape(members, size, tile)
        token_out[...] = jnp.zeros((8, 128), jnp.float32)
        if ends:
            end_refs[0][...] = product[(members - 1) * size :]
            end_refs[1][...] = product[:size]

    flat = ((size, width), jnp.bfloat16, (size, tile), lambda j: (0, j))
    return call(
        body,
        "partial_products",
        (width // tile,),
        [
            (mine, (members, size, rows), fixed(0, index, 0)),
            (weights, (rows, tile), lambda j: (0, j)),
        ]
        + ([] if token is None else [token_in(token)]),
        [
            ((members, size, width), jnp.bfloat16, (members, size, tile), lambda j: (0, 0, j)),
            TOKEN_OUT,
        ]
        + [flat, flat] * ends,
        flops=2 * members * size * rows * width,
        moved=2 * (members * size * (rows + width) + rows * width),
        vmem=20,
    )


def next_payload(right, left, parts, scalars, pick, token=None):
    members, size, width = parts.shape
    step = size // 2

    def joined(arrived, part, counts):
        if pick:
            return jnp.where(counts, part, arrived)
        weight = jnp.where(counts, 1.0, 0.0)
        return (arrived.astype(jnp.float32) + weight * part.astype(jnp.float32)).astype(
            jnp.bfloat16
        )

    def body(s, right_ref, left_ref, of_right, of_left, *refs):
        right_out, left_out, token_out = refs[-3:]
        right_out[...] = joined(right_ref[...], of_right[0], s[1] > 0)
        left_out[...] = joined(left_ref[...], of_left[0], s[3] > 0)
        token_out[...] = jnp.zeros((8, 128), jnp.float32)

    here = (step, width), lambda i, s: (i, 0)
    flat = ((size, width), jnp.bfloat16) + here
    return call(
        body,
        "next_payload",
        (size // step,),
        [
            (right,) + here,
            (left,) + here,
            (parts, (1, step, width), lambda i, s: (s[0], i, 0)),
            (parts, (1, step, width), lambda i, s: (s[2], i, 0)),
        ]
        + ([] if token is None else [token_in(token)]),
        [flat, flat, TOKEN_OUT],
        scalars=(scalars,),
        flops=2 * size * width,
        moved=12 * size * width,
    )


def unit_gradient(right, left, parts, place, residual, cotangent, gain, start, token):
    members, size, width = parts.shape
    step = size // 2

    def body(s, right_ref, left_ref, own_ref, residual_ref, cot_ref, gain_ref, *refs):
        product = (
            right_ref[...].astype(jnp.float32)
            + left_ref[...].astype(jnp.float32)
            + own_ref[0].astype(jnp.float32)
        )
        summed = residual_ref[...].astype(jnp.float32) + product
        inverse = lax.rsqrt(jnp.mean(summed * summed, axis=-1, keepdims=True) + 1e-05)
        scaled_cot = gain_ref[...] * cot_ref[...].astype(jnp.float32)
        along = jnp.mean(scaled_cot * summed, axis=-1, keepdims=True)
        refs[-1][...] = (
            inverse * scaled_cot - summed * (inverse * inverse * inverse * along)
        ).astype(jnp.bfloat16)

    here = (step, width), lambda i, s: (i, 0)
    there = (step, width), lambda i, s: (start // step + i, 0)
    return call(
        body,
        "unit_gradient",
        (size // step,),
        [
            (right,) + here,
            (left,) + here,
            (parts, (1, step, width), lambda i, s: (s[0], i, 0)),
            (residual,) + there,
            (cotangent,) + there,
            (gain, (1, width), fixed(0, 0)),
        ]
        + ([] if token is None else [token_in(token)]),
        [((size, width), jnp.bfloat16) + here],
        scalars=(place,),
        flops=12 * size * width,
        moved=12 * size * width,
    )[0]


def stack_of(refs, members, me):
    count = 2 * members - 1
    rows = []
    for c in range(len(refs) // count):
        own, rights, lefts = (
            refs[c * count],
            refs[c * count + 1 : c * count + members],
            refs[c * count + members : (c + 1) * count],
        )
        rows.append(own[...])
        for k in range(members - 1):
            rows.append(jnp.where(me > k, rights[k][...], lefts[members - 2 - k][...]))
    return jnp.concatenate(rows, axis=0)


def unit_ins(units, tile, first=0):
    ins = []
    for chunk in units:
        block = (chunk[0].shape[0], tile)
        members = (len(chunk) + 1) // 2
        ins.append((chunk[0], block, lambda j, s: (0, j + first)))
        for k in range(members - 1):
            place = lambda j, s, k=k: (0, jnp.where(s[0] > k, j, 0) + first)
            ins.append((chunk[1 + k], block, place))
        for m in range(members - 1):
            place = lambda j, s, k=members - 2 - m: (0, jnp.where(s[0] > k, 0, j) + first)
            ins.append((chunk[members + m], block, place))
    return ins


def mine_ins(mine):
    return [
        (array, (array.shape[0], size, array.shape[2]), fixed(0, index, 0))
        for array, index, size in mine
    ]


def turned_heads(mine, order):
    members, _, rows = mine[0][0].shape
    total = sum(members * size for _, _, size in mine)

    def body(s, *refs):
        out_ref, token_out = refs[-2:]
        stack = jnp.concatenate([ref[s[k]] for ref in refs[:-2] for k in range(members)], axis=0)
        out_ref[...] = stack.T
        token_out[...] = jnp.zeros((8, 128), jnp.float32)

    return call(
        body,
        "turned_heads",
        (1,),
        mine_ins(mine),
        [((rows, total), jnp.bfloat16, (rows, total), fixed(0, 0)), TOKEN_OUT],
        scalars=(order,),
        moved=4 * rows * total,
        vmem=20,
    )


def weight_step(units, turned, order, base, first, last, inbox=None, kept=None, new=False, token=None):
    rows, total = turned.shape
    members = (len(units[0]) + 1) // 2
    width = base.shape[1]
    tile = tile_of(width)
    last = width // tile if last is None else last
    count = len(units) * len(units[0])
    early = inbox is None

    def body(s, *refs):
        turned_ref, base_ref = refs[count : count + 2]
        weight = jnp.dot(
            turned_ref[...],
            stack_of(refs[:count], members, s[0]),
            preferred_element_type=jnp.float32,
        )
        if early:
            refs[-2][...] = 0.5 * (base_ref[...] - 0.004 * weight)
            refs[-1][...] = jnp.zeros((8, 128), jnp.float32)
        else:
            now = base_ref[...] - 0.5 * 0.004 * weight
            if new:
                refs[-1][...] = now + refs[count + 2][...]
            else:
                refs[-1][...] = now.astype(jnp.bfloat16)

    columns = (rows, tile), lambda j, s: (0, j + first)
    ins = unit_ins(units, tile, first) + [
        (turned, (rows, total), fixed(0, 0)),
        (base,) + columns,
    ]
    if new:
        ins.append((inbox,) + columns)
    if kept is not None:
        ins.append((kept, (8, 128), fixed(0, 0)))
    if token is not None:
        ins.append(token_in(token))
    kind = jnp.float32 if early or new else jnp.bfloat16
    outs = [((rows, width), kind) + columns]
    return call(
        body,
        "weight_step",
        (last - first,),
        ins,
        outs + [TOKEN_OUT] * early,
        scalars=(order,),
        flops=2 * total * rows * tile * (last - first),
        moved=(2 * count * units[0][0].shape[0] + 12 * rows) * tile * (last - first),
        vmem=52,
        aliases={} if kept is None else {1 + count + 2: 0},
    )


def grad_rows(units, weights, order):
    members = (len(units[0]) + 1) // 2
    sizes = [chunk[0].shape[0] for chunk in units]
    rows, width = weights.shape
    tile = tile_of(width)
    steps = width // tile
    count = len(units) * len(units[0])
    total = members * sum(sizes)

    def body(s, *refs):
        weights_ref, grad_ref, token_out, acc = refs[count:]
        token_out[...] = jnp.zeros((8, 128), jnp.float32)
        j = pl.program_id(0)
        grad = lax.dot_general(
            stack_of(refs[:count], members, s[0]),
            weights_ref[...],
            (((1,), (1,)), ((), ())),
            preferred_element_type=jnp.float32,
        )

        @pl.when(j == 0)
        def _():
            acc[...] = grad

        @pl.when(j > 0)
        def _():
            acc[...] += grad

        @pl.when(j == steps - 1)
        def _():
            at, row = 0, 0
            for size in sizes:
                for k in range(members):
                    grad_ref[s[k], row : row + size] = acc[at : at + size].astype(jnp.bfloat16)
                    at += size
                row += size

    return call(
        body,
        "grad_rows",
        (steps,),
        unit_ins(units, tile) + [(weights, (rows, tile), lambda j, s: (0, j))],
        [
            (
                (members, sum(sizes), rows),
                jnp.bfloat16,
                (members, sum(sizes), rows),
                fixed(0, 0, 0),
            ),
            TOKEN_OUT,
        ],
        scalars=(order,),
        scratch=[pltpu.VMEM((total, rows), jnp.float32)],
        flops=2 * total * rows * width,
        moved=2 * count * sizes[0] * width + 2 * rows * width,
        vmem=50,
    )


def passed(right, left, token):
    size, width = right.shape
    step = size // 2

    def body(right_ref, left_ref, token_ref, right_out, left_out):
        right_out[...] = right_ref[...]
        left_out[...] = left_ref[...]

    here = (step, width), lambda i: (i, 0)
    flat = ((size, width), right.dtype) + here
    return call(
        body,
        "passed",
        (size // step,),
        [(right,) + here, (left,) + here, token_in(token)],
        [flat, flat],
        moved=8 * size * width,
    )


def joined_rows(groups):
    members, size, rows = groups[0].shape
    tokens = size * len(groups)

    def body(*refs):
        out_ref = refs[-1]
        for g, blocks_ref in enumerate(refs[:-1]):

            @pl.when(pl.program_id(0) == g)
            def _(blocks_ref=blocks_ref):
                for k in range(members):
                    out_ref[:, k * rows : (k + 1) * rows] = blocks_ref[k]

    return call(
        body,
        "joined_rows",
        (len(groups),),
        [(blocks, (members, size, rows), fixed(0, 0, 0)) for blocks in groups],
        [
            (
                (tokens, members * rows),
                groups[0].dtype,
                (size, members * rows),
                lambda i: (i, 0),
            )
        ],
        moved=4 * members * tokens * rows,
        vmem=24,
    )[0]


def widened(value):
    rows, width = value.shape
    step = rows // 2

    def body(value_ref, out_ref):
        out_ref[...] = value_ref[...].astype(jnp.float32)

    block = (step, width), lambda i: (i, 0)
    return call(
        body,
        "widened",
        (rows // step,),
        [(value,) + block],
        [((rows, width), jnp.float32) + block],
        moved=6 * rows * width,
        vmem=20,
    )[0]


def swapped(blocks):
    return lax.all_to_all(blocks, "fsdp", 0, 0, tiled=False)


def tail(half, grads, late, turned, kept, inbox, weights, order, bit_place):
    length = lax.axis_size("rep")
    sent = lax.ppermute(
        half, "rep", [(i, (i + (1 << bit_place)) % length) for i in range(length)]
    )
    back = swapped(grads)
    late_grads, token = grad_rows(late, weights, order)
    late_back = swapped(late_grads)
    new = weight_step(late, turned, order, kept, 0, None, inbox, new=True, token=token)[0]
    return sent, joined_rows([back, late_back]), new


def local(
    params, push_weight, inbox_params, inbox_weight, heads, residual, cotangent, gain, offset
):
    numer = params[0]
    weight_one = push_weight[0]
    members = lax.axis_size("fsdp")
    me = lax.axis_index("fsdp").astype(jnp.int32)
    tokens, inner = heads.shape[1:]
    rows, width = numer.shape
    scaling = inner ** (-0.5)
    rounds = len(STREAMS[0])
    assert sum(map(sum, STREAMS)) == tokens

    replicas = lax.axis_size("rep")
    levels = replicas.bit_length() - 1
    powers = jnp.left_shift(jnp.ones((levels,), jnp.int32), jnp.arange(levels, dtype=jnp.int32))
    level_index = jnp.sum(jnp.where(powers == offset[0], jnp.arange(levels, dtype=jnp.int32), 0))

    arrived = [None] * levels
    slots = [(1, 0), (1, 1), (2, 0)]

    def levels_of(slot):
        return [b for b in range(levels) if min(b, len(slots) - 1) == slot]

    def sent_weight(token, b):
        half = 0.5 * push_weight + token[0, :1]
        return lax.ppermute(
            half, "rep", [(i, (i + (1 << b)) % replicas) for i in range(replicas)]
        )

    def seen(slot):
        return jnp.broadcast_to(sum(arrived[b] for b in levels_of(slot))[None], (8, 128))

    order = jnp.mod(me - jnp.arange(members, dtype=jnp.int32), members)
    own = me[None]
    weights, token = scaled_weights(numer, weight_one, scaling)
    everyone = range(members - 1), range(1, members)

    def scalars(t):
        ahead = members - 1 - t
        return jnp.stack(
            [
                jnp.minimum(me + ahead, members - 1),
                (me <= t).astype(jnp.int32),
                jnp.maximum(me - ahead, 0),
                (me >= ahead).astype(jnp.int32),
            ]
        )

    at = 0
    starts = []
    for e in range(rounds):
        starts.append([])
        for sizes in STREAMS:
            starts[e].append(at)
            at += sizes[e]

    count = len(STREAMS)
    mine = [[None] * count for _ in range(rounds)]
    units = [[None] * count for _ in range(rounds)]
    before = [None] * count
    hint = [None] * count

    def fetch(e, members_of, token):
        size = STREAMS[members_of[0]][e]
        piece = cut_heads(
            heads[0], starts[e][members_of[0]], size * len(members_of), members, token
        )
        array = swapped(piece)
        for index, q in enumerate(members_of):
            mine[e][q] = (array, index, size)

    for q in range(count):
        fetch(0, [q], token if q else None)
    parts = [None] * count
    token = None
    for q in range(count):
        parts[q], token, last, first = partial_products(mine[0][q], weights, True, token)
        hint[q] = (last, first)
    for e in range(rounds):
        moving = [None] * count
        for q in range(count):
            if e == 0:
                moving[q] = hops(*hint[q], range(1), range(members - 1, members))
            else:
                right, left, _ = next_payload(*before[q], parts[q], scalars(0), True)
                moving[q] = hops(right, left, *everyone)
                units[e - 1][q][1].append(moving[q][0])
                units[e - 1][q][2].append(moving[q][1])
        for t in range(1, members - 1):
            for q in range(count):
                order_token = token if (e, t, q) == (0, 1, 0) else None
                if e + 1 == rounds and t == 2:
                    order_token = seen(slots.index((1, q)))
                right, left, token = next_payload(
                    *moving[q], parts[q], scalars(t), False, order_token
                )
                if t == members - 2 and e + 1 < rounds:
                    fetch(e + 1, [q], token)
                if e + 1 == rounds and (t, q) in slots:
                    for b in levels_of(slots.index((t, q))):
                        arrived[b] = sent_weight(token, b)
                if e == 0:
                    pairs = range(t + 1), range(members - 1 - t, members)
                else:
                    pairs = everyone
                moving[q] = hops(right, left, *pairs)
                if e > 0 and t < members - 2:
                    units[e - 1][q][1].append(moving[q][0])
                    units[e - 1][q][2].append(moving[q][1])
        later = [None] * count
        for q in range(count):
            token = None
            if e + 1 < rounds:
                later[q], token = partial_products(mine[e + 1][q], weights, False)
            unit = unit_gradient(
                *moving[q],
                parts[q],
                own,
                residual[0],
                cotangent[0],
                gain[None],
                starts[e][q],
                seen(2) if (e + 1, q + 1) == (rounds, count) else token,
            )
            before[q] = hops(unit, unit, *everyone)
            units[e][q] = (unit, [before[q][0]], [before[q][1]])
        parts = later
    kept = None
    for s in range(1, members - 1):
        for q in range(count):
            if (s, q) == (1, count - 1):
                early = [[u] + r + l for of_round in units[:-1] for u, r, l in of_round]
                early_turned, _ = turned_heads([m for of_round in mine[:-1] for m in of_round], order)
                kept, done = weight_step(early, early_turned, order, numer, 0, 3)
                before[q] = passed(*before[q], done)
            if (s, q) == (2, 0):
                turned, token = turned_heads(mine[-1], order)
                kept, done = weight_step(
                    early, early_turned, order, numer, 3, None, kept=kept, token=token
                )
                before[q] = passed(*before[q], done)
            before[q] = hops(*before[q], range(s, members - 1), range(1, members - s))
            units[-1][q][1].append(before[q][0])
            units[-1][q][2].append(before[q][1])
    flat = [[u] + r + l for u, r, l in units[-1]]
    grads, _ = grad_rows(early, weights, order)
    half = weight_step(flat, turned, order, kept, 0, None, inbox_params[0])[0]
    new_weight = 0.5 * push_weight + inbox_weight
    branches = [
        partial(
            tail, half, grads, flat, turned, kept, inbox_params[0], weights, order, place
        )
        for place in range(levels)
    ]
    outbox_weight = arrived[0]
    for b in range(1, levels):
        outbox_weight = jnp.where(level_index == b, arrived[b], outbox_weight)
    sent, grad_heads, new_params = lax.switch(level_index, branches)
    return (new_params[None], new_weight, widened(sent)[None], outbox_weight, grad_heads[None])


def solution(mesh):
    placed = (
        P("rep", "fsdp", None),
        P("rep"),
        P("rep", "fsdp", None),
        P("rep"),
        P("rep", "fsdp", None),
        P("rep", "fsdp", None),
        P("rep", "fsdp", None),
        P(),
        P(),
    )
    return jax.shard_map(
        local,
        mesh=mesh,
        in_specs=placed,
        out_specs=(
            P("rep", "fsdp", None),
            P("rep"),
            P("rep", "fsdp", None),
            P("rep"),
            P("rep", "fsdp", None),
        ),
        check_vma=False,
    )
```

```python
from functools import partial

import jax
import jax.numpy as jnp
from jax import lax
from jax.experimental import pallas as pl
from jax.experimental.pallas import tpu as pltpu
from jax.sharding import PartitionSpec as P

STREAMS = ((96, 96), (96, 96))
MIB = 1 << 20
TOKEN = jax.ShapeDtypeStruct((8, 128), jnp.float32)


def call(body, name, grid, ins, outs, scalars=(), scratch=(), flops=0, moved=0, vmem=12, aliases=None):
    return pl.pallas_call(
        body,
        name=name,
        out_shape=[jax.ShapeDtypeStruct(shape, kind) for shape, kind, _, _ in outs],
        grid_spec=pltpu.PrefetchScalarGridSpec(
            num_scalar_prefetch=len(scalars),
            grid=grid,
            in_specs=[pl.BlockSpec(block, place) for _, block, place in ins],
            out_specs=[pl.BlockSpec(block, place) for _, _, block, place in outs],
            scratch_shapes=scratch,
        ),
        input_output_aliases=aliases or {},
        compiler_params=pltpu.CompilerParams(vmem_limit_bytes=vmem * MIB),
        cost_estimate=pl.CostEstimate(flops=flops, bytes_accessed=moved, transcendentals=0),
    )(*scalars, *(array for array, _, _ in ins))


def fixed(*place):
    return lambda *_: place


def token_in(token):
    return (token, (8, 128), fixed(0, 0))


TOKEN_OUT = ((8, 128), jnp.float32, (8, 128), fixed(0, 0))


def hop(value, step, pairs):
    return lax.ppermute(value, "fsdp", [(i, i + step) for i in pairs])


def hops(right, left, rights, lefts):
    return hop(right, 1, rights), hop(left, -1, lefts)


def tile_of(width, most=512):
    tile = most
    while width % tile:
        tile //= 2
    return tile


def cut_heads(heads, start, size, members, token):
    inner = heads.shape[1]
    rows = inner // members
    step = size // 2

    def body(heads_ref, *refs):
        for k in range(members):
            refs[-1][k] = heads_ref[:, k * rows : (k + 1) * rows]

    return call(
        body,
        "cut_heads",
        (size // step,),
        [(heads, (step, inner), lambda i: (start // step + i, 0))]
        + ([] if token is None else [token_in(token)]),
        [((members, size, rows), heads.dtype, (members, step, rows), lambda i: (0, i, 0))],
        moved=4 * size * inner,
        vmem=12 if start else 56,
    )[0]


def scaled_weights(numer, weight_one, scaling):
    rows, width = numer.shape
    step = rows // 4

    def body(numer_ref, one_ref, out_ref, token_out):
        out_ref[...] = (numer_ref[...] / one_ref[...] * scaling).astype(jnp.bfloat16)
        token_out[...] = jnp.zeros((8, 128), jnp.float32)

    block = (step, width), lambda i: (i, 0)
    return call(
        body,
        "scaled_weights",
        (rows // step,),
        [(numer,) + block, (weight_one.reshape(1, 1), (1, 1), fixed(0, 0))],
        [((rows, width), jnp.bfloat16) + block, TOKEN_OUT],
        flops=2 * rows * width,
        moved=6 * rows * width,
        vmem=56,
    )


def partial_products(mine, weights, ends, token=None):
    mine, index, size = mine
    members, _, rows = mine.shape
    width = weights.shape[1]
    tile = tile_of(width, 1280)

    def body(mine_ref, weights_ref, *refs):
        out_ref, token_out, *end_refs = refs[0 if token is None else 1 :]
        product = jnp.dot(
            mine_ref[...].reshape(members * size, rows),
            weights_ref[...],
            preferred_element_type=jnp.float32,
        ).astype(jnp.bfloat16)
        out_ref[...] = product.reshape(members, size, tile)
        token_out[...] = jnp.zeros((8, 128), jnp.float32)
        if ends:
            end_refs[0][...] = product[(members - 1) * size :]
            end_refs[1][...] = product[:size]

    flat = ((size, width), jnp.bfloat16, (size, tile), lambda j: (0, j))
    return call(
        body,
        "partial_products",
        (width // tile,),
        [
            (mine, (members, size, rows), fixed(0, index, 0)),
            (weights, (rows, tile), lambda j: (0, j)),
        ]
        + ([] if token is None else [token_in(token)]),
        [
            ((members, size, width), jnp.bfloat16, (members, size, tile), lambda j: (0, 0, j)),
            TOKEN_OUT,
        ]
        + [flat, flat] * ends,
        flops=2 * members * size * rows * width,
        moved=2 * (members * size * (rows + width) + rows * width),
        vmem=20,
    )


def next_payload(right, left, parts, scalars, pick, token=None):
    members, size, width = parts.shape
    step = size // 2

    def joined(arrived, part, counts):
        if pick:
            return jnp.where(counts, part, arrived)
        weight = jnp.where(counts, 1.0, 0.0)
        return (arrived.astype(jnp.float32) + weight * part.astype(jnp.float32)).astype(
            jnp.bfloat16
        )

    def body(s, right_ref, left_ref, of_right, of_left, *refs):
        right_out, left_out, token_out = refs[-3:]
        right_out[...] = joined(right_ref[...], of_right[0], s[1] > 0)
        left_out[...] = joined(left_ref[...], of_left[0], s[3] > 0)
        token_out[...] = jnp.zeros((8, 128), jnp.float32)

    here = (step, width), lambda i, s: (i, 0)
    flat = ((size, width), jnp.bfloat16) + here
    return call(
        body,
        "next_payload",
        (size // step,),
        [
            (right,) + here,
            (left,) + here,
            (parts, (1, step, width), lambda i, s: (s[0], i, 0)),
            (parts, (1, step, width), lambda i, s: (s[2], i, 0)),
        ]
        + ([] if token is None else [token_in(token)]),
        [flat, flat, TOKEN_OUT],
        scalars=(scalars,),
        flops=2 * size * width,
        moved=12 * size * width,
    )


def unit_gradient(right, left, parts, place, residual, cotangent, gain, start, token):
    members, size, width = parts.shape
    step = size // 2

    def body(s, right_ref, left_ref, own_ref, residual_ref, cot_ref, gain_ref, *refs):
        product = (
            right_ref[...].astype(jnp.float32)
            + left_ref[...].astype(jnp.float32)
            + own_ref[0].astype(jnp.float32)
        )
        summed = residual_ref[...].astype(jnp.float32) + product
        inverse = lax.rsqrt(jnp.mean(summed * summed, axis=-1, keepdims=True) + 1e-05)
        scaled_cot = gain_ref[...] * cot_ref[...].astype(jnp.float32)
        along = jnp.mean(scaled_cot * summed, axis=-1, keepdims=True)
        refs[-1][...] = (
            inverse * scaled_cot - summed * (inverse * inverse * inverse * along)
        ).astype(jnp.bfloat16)

    here = (step, width), lambda i, s: (i, 0)
    there = (step, width), lambda i, s: (start // step + i, 0)
    return call(
        body,
        "unit_gradient",
        (size // step,),
        [
            (right,) + here,
            (left,) + here,
            (parts, (1, step, width), lambda i, s: (s[0], i, 0)),
            (residual,) + there,
            (cotangent,) + there,
            (gain, (1, width), fixed(0, 0)),
        ]
        + ([] if token is None else [token_in(token)]),
        [((size, width), jnp.bfloat16) + here],
        scalars=(place,),
        flops=12 * size * width,
        moved=12 * size * width,
    )[0]


def stack_of(refs, members, me):
    count = 2 * members - 1
    rows = []
    for c in range(len(refs) // count):
        own, rights, lefts = (
            refs[c * count],
            refs[c * count + 1 : c * count + members],
            refs[c * count + members : (c + 1) * count],
        )
        rows.append(own[...])
        for k in range(members - 1):
            rows.append(jnp.where(me > k, rights[k][...], lefts[members - 2 - k][...]))
    return jnp.concatenate(rows, axis=0)


def unit_ins(units, tile, first=0):
    ins = []
    for chunk in units:
        block = (chunk[0].shape[0], tile)
        members = (len(chunk) + 1) // 2
        ins.append((chunk[0], block, lambda j, s: (0, j + first)))
        for k in range(members - 1):
            place = lambda j, s, k=k: (0, jnp.where(s[0] > k, j, 0) + first)
            ins.append((chunk[1 + k], block, place))
        for m in range(members - 1):
            place = lambda j, s, k=members - 2 - m: (0, jnp.where(s[0] > k, 0, j) + first)
            ins.append((chunk[members + m], block, place))
    return ins


def mine_ins(mine):
    return [
        (array, (array.shape[0], size, array.shape[2]), fixed(0, index, 0))
        for array, index, size in mine
    ]


def turned_into(scratch, mine_refs, order):
    members = mine_refs[0].shape[0]
    stack = jnp.concatenate([ref[order[k]] for ref in mine_refs for k in range(members)], axis=0)
    scratch[...] = stack.T


def weight_step(units, mine, order, base, first, last, inbox=None, kept=None, new=False, token=None):
    members, _, rows = mine[0][0].shape
    width = base.shape[1]
    tile = tile_of(width)
    last = width // tile if last is None else last
    count = len(units) * len(units[0])
    chunks = len(units)
    total = sum(members * size for _, _, size in mine)
    early = inbox is None

    def body(s, *refs):
        units_ref, mine_refs = refs[:count], refs[count : count + chunks]
        base_ref = refs[count + chunks]
        turned = refs[-1]

        @pl.when(pl.program_id(0) == 0)
        def _():
            turned_into(turned, mine_refs, s)

        weight = jnp.dot(
            turned[...], stack_of(units_ref, members, s[0]), preferred_element_type=jnp.float32
        )
        if early:
            refs[-3][...] = 0.5 * (base_ref[...] - 0.004 * weight)
            refs[-2][...] = jnp.zeros((8, 128), jnp.float32)
        else:
            now = base_ref[...] - 0.5 * 0.004 * weight
            if new:
                refs[-2][...] = now + refs[count + chunks + 1][...]
            else:
                refs[-2][...] = now.astype(jnp.bfloat16)

    columns = (rows, tile), lambda j, s: (0, j + first)
    ins = unit_ins(units, tile, first) + mine_ins(mine) + [(base,) + columns]
    if new:
        ins.append((inbox,) + columns)
    if kept is not None:
        ins.append((kept, (8, 128), fixed(0, 0)))
    if token is not None:
        ins.append(token_in(token))
    kind = jnp.float32 if early or new else jnp.bfloat16
    outs = [((rows, width), kind) + columns]
    return call(
        body,
        "weight_step",
        (last - first,),
        ins,
        outs + [TOKEN_OUT] * early,
        scalars=(order,),
        scratch=[pltpu.VMEM((rows, total), jnp.bfloat16)],
        flops=2 * total * rows * tile * (last - first),
        moved=(2 * count * units[0][0].shape[0] + 12 * rows) * tile * (last - first),
        vmem=52,
        aliases={} if kept is None else {1 + count + chunks + 1: 0},
    )


def grad_rows(units, weights, order):
    members = (len(units[0]) + 1) // 2
    sizes = [chunk[0].shape[0] for chunk in units]
    rows, width = weights.shape
    tile = tile_of(width)
    steps = width // tile
    count = len(units) * len(units[0])
    total = members * sum(sizes)

    def body(s, *refs):
        weights_ref, grad_ref, token_out, acc = refs[count:]
        token_out[...] = jnp.zeros((8, 128), jnp.float32)
        j = pl.program_id(0)
        grad = lax.dot_general(
            stack_of(refs[:count], members, s[0]),
            weights_ref[...],
            (((1,), (1,)), ((), ())),
            preferred_element_type=jnp.float32,
        )

        @pl.when(j == 0)
        def _():
            acc[...] = grad

        @pl.when(j > 0)
        def _():
            acc[...] += grad

        @pl.when(j == steps - 1)
        def _():
            at, row = 0, 0
            for size in sizes:
                for k in range(members):
                    grad_ref[s[k], row : row + size] = acc[at : at + size].astype(jnp.bfloat16)
                    at += size
                row += size

    return call(
        body,
        "grad_rows",
        (steps,),
        unit_ins(units, tile) + [(weights, (rows, tile), lambda j, s: (0, j))],
        [
            (
                (members, sum(sizes), rows),
                jnp.bfloat16,
                (members, sum(sizes), rows),
                fixed(0, 0, 0),
            ),
            TOKEN_OUT,
        ],
        scalars=(order,),
        scratch=[pltpu.VMEM((total, rows), jnp.float32)],
        flops=2 * total * rows * width,
        moved=2 * count * sizes[0] * width + 2 * rows * width,
        vmem=50,
    )


def passed(right, left, token):
    size, width = right.shape
    step = size // 2

    def body(right_ref, left_ref, token_ref, right_out, left_out):
        right_out[...] = right_ref[...]
        left_out[...] = left_ref[...]

    here = (step, width), lambda i: (i, 0)
    flat = ((size, width), right.dtype) + here
    return call(
        body,
        "passed",
        (size // step,),
        [(right,) + here, (left,) + here, token_in(token)],
        [flat, flat],
        moved=8 * size * width,
    )


def joined_rows(groups):
    members, size, rows = groups[0].shape
    tokens = size * len(groups)

    def body(*refs):
        out_ref = refs[-1]
        for g, blocks_ref in enumerate(refs[:-1]):

            @pl.when(pl.program_id(0) == g)
            def _(blocks_ref=blocks_ref):
                for k in range(members):
                    out_ref[:, k * rows : (k + 1) * rows] = blocks_ref[k]

    return call(
        body,
        "joined_rows",
        (len(groups),),
        [(blocks, (members, size, rows), fixed(0, 0, 0)) for blocks in groups],
        [
            (
                (tokens, members * rows),
                groups[0].dtype,
                (size, members * rows),
                lambda i: (i, 0),
            )
        ],
        moved=4 * members * tokens * rows,
        vmem=24,
    )[0]


def widened(value):
    rows, width = value.shape
    step = rows // 2

    def body(value_ref, out_ref):
        out_ref[...] = value_ref[...].astype(jnp.float32)

    block = (step, width), lambda i: (i, 0)
    return call(
        body,
        "widened",
        (rows // step,),
        [(value,) + block],
        [((rows, width), jnp.float32) + block],
        moved=6 * rows * width,
        vmem=20,
    )[0]


def swapped(blocks):
    return lax.all_to_all(blocks, "fsdp", 0, 0, tiled=False)


def tail(half, grads, late, mine, kept, inbox, weights, order, bit_place):
    length = lax.axis_size("rep")
    sent = lax.ppermute(
        half, "rep", [(i, (i + (1 << bit_place)) % length) for i in range(length)]
    )
    back = swapped(grads)
    late_grads, token = grad_rows(late, weights, order)
    late_back = swapped(late_grads)
    new = weight_step(late, mine, order, kept, 0, None, inbox, new=True, token=token)[0]
    return sent, joined_rows([back, late_back]), new


def local(
    params, push_weight, inbox_params, inbox_weight, heads, residual, cotangent, gain, offset
):
    numer = params[0]
    weight_one = push_weight[0]
    members = lax.axis_size("fsdp")
    me = lax.axis_index("fsdp").astype(jnp.int32)
    tokens, inner = heads.shape[1:]
    rows, width = numer.shape
    scaling = inner ** (-0.5)
    rounds = len(STREAMS[0])
    assert sum(map(sum, STREAMS)) == tokens

    replicas = lax.axis_size("rep")
    levels = replicas.bit_length() - 1
    powers = jnp.left_shift(jnp.ones((levels,), jnp.int32), jnp.arange(levels, dtype=jnp.int32))
    level_index = jnp.sum(jnp.where(powers == offset[0], jnp.arange(levels, dtype=jnp.int32), 0))

    arrived = [None] * levels
    slots = [(0, 1), (1, 0), (1, 1)]

    def levels_of(slot):
        return [b for b in range(levels) if min(b, len(slots) - 1) == slot]

    def sent_weight(token, b):
        half = 0.5 * push_weight + token[0, :1]
        return lax.ppermute(
            half, "rep", [(i, (i + (1 << b)) % replicas) for i in range(replicas)]
        )

    def pass_weight(e, t, q, token):
        if e + 1 == rounds and (t, q) in slots:
            for b in levels_of(slots.index((t, q))):
                arrived[b] = sent_weight(token, b)

    def seen(slot):
        return jnp.broadcast_to(sum(arrived[b] for b in levels_of(slot))[None], (8, 128))

    order = jnp.mod(me - jnp.arange(members, dtype=jnp.int32), members)
    own = me[None]
    weights, token = scaled_weights(numer, weight_one, scaling)
    everyone = range(members - 1), range(1, members)

    def scalars(t):
        ahead = members - 1 - t
        return jnp.stack(
            [
                jnp.minimum(me + ahead, members - 1),
                (me <= t).astype(jnp.int32),
                jnp.maximum(me - ahead, 0),
                (me >= ahead).astype(jnp.int32),
            ]
        )

    at = 0
    starts = []
    for e in range(rounds):
        starts.append([])
        for sizes in STREAMS:
            starts[e].append(at)
            at += sizes[e]

    count = len(STREAMS)
    mine = [[None] * count for _ in range(rounds)]
    units = [[None] * count for _ in range(rounds)]
    before = [None] * count
    hint = [None] * count

    def fetch(e, members_of, token):
        size = STREAMS[members_of[0]][e]
        piece = cut_heads(
            heads[0], starts[e][members_of[0]], size * len(members_of), members, token
        )
        array = swapped(piece)
        for index, q in enumerate(members_of):
            mine[e][q] = (array, index, size)

    for q in range(count):
        fetch(0, [q], token if q else None)
    parts = [None] * count
    token = None
    for q in range(count):
        parts[q], token, last, first = partial_products(mine[0][q], weights, True, token)
        hint[q] = (last, first)
    for e in range(rounds):
        moving = [None] * count
        for q in range(count):
            if e == 0:
                moving[q] = hops(*hint[q], range(1), range(members - 1, members))
            else:
                right, left, token = next_payload(*before[q], parts[q], scalars(0), True)
                pass_weight(e, 0, q, token)
                moving[q] = hops(right, left, *everyone)
                units[e - 1][q][1].append(moving[q][0])
                units[e - 1][q][2].append(moving[q][1])
        for t in range(1, members - 1):
            for q in range(count):
                order_token = token if (e, t, q) == (0, 1, 0) else None
                if e + 1 == rounds and (t - 1, q) in slots:
                    order_token = seen(slots.index((t - 1, q)))
                right, left, token = next_payload(
                    *moving[q], parts[q], scalars(t), False, order_token
                )
                if (t, q) == (1, count - 1) and e + 1 < rounds:
                    fetch(e + 1, list(range(count)), token)
                pass_weight(e, t, q, token)
                if e == 0:
                    pairs = range(t + 1), range(members - 1 - t, members)
                else:
                    pairs = everyone
                moving[q] = hops(right, left, *pairs)
                if e > 0 and t < members - 2:
                    units[e - 1][q][1].append(moving[q][0])
                    units[e - 1][q][2].append(moving[q][1])
        later = [None] * count
        for q in range(count):
            token = None
            if e + 1 < rounds:
                later[q], token = partial_products(mine[e + 1][q], weights, False)
            unit = unit_gradient(
                *moving[q],
                parts[q],
                own,
                residual[0],
                cotangent[0],
                gain[None],
                starts[e][q],
                token,
            )
            before[q] = hops(unit, unit, *everyone)
            units[e][q] = (unit, [before[q][0]], [before[q][1]])
        parts = later
    kept = None
    for s in range(1, members - 1):
        for q in range(count):
            if (s, q) == (1, count - 1):
                early = [[u] + r + l for of_round in units[:-1] for u, r, l in of_round]
                early_mine = [m for of_round in mine[:-1] for m in of_round]
                kept, done = weight_step(early, early_mine, order, numer, 0, 3)
                before[q] = passed(*before[q], done)
            if (s, q) == (2, 0):
                kept, done = weight_step(early, early_mine, order, numer, 3, None, kept=kept)
                before[q] = passed(*before[q], done)
            before[q] = hops(*before[q], range(s, members - 1), range(1, members - s))
            units[-1][q][1].append(before[q][0])
            units[-1][q][2].append(before[q][1])
    flat = [[u] + r + l for u, r, l in units[-1]]
    grads, _ = grad_rows(early, weights, order)
    half = weight_step(flat, mine[-1], order, kept, 0, None, inbox_params[0])[0]
    new_weight = 0.5 * push_weight + inbox_weight
    branches = [
        partial(
            tail, half, grads, flat, mine[-1], kept, inbox_params[0], weights, order, place
        )
        for place in range(levels)
    ]
    outbox_weight = arrived[0]
    for b in range(1, levels):
        outbox_weight = jnp.where(level_index == b, arrived[b], outbox_weight)
    sent, grad_heads, new_params = lax.switch(level_index, branches)
    return (new_params[None], new_weight, widened(sent)[None], outbox_weight, grad_heads[None])


def solution(mesh):
    placed = (
        P("rep", "fsdp", None),
        P("rep"),
        P("rep", "fsdp", None),
        P("rep"),
        P("rep", "fsdp", None),
        P("rep", "fsdp", None),
        P("rep", "fsdp", None),
        P(),
        P(),
    )
    return jax.shard_map(
        local,
        mesh=mesh,
        in_specs=placed,
        out_specs=(
            P("rep", "fsdp", None),
            P("rep"),
            P("rep", "fsdp", None),
            P("rep"),
            P("rep", "fsdp", None),
        ),
        check_vma=False,
    )
```

```python
from functools import partial

import jax
import jax.numpy as jnp
from jax import lax
from jax.experimental import pallas as pl
from jax.experimental.pallas import tpu as pltpu
from jax.sharding import PartitionSpec as P

STREAMS = ((96, 96), (96, 96))
MIB = 1 << 20
TOKEN = jax.ShapeDtypeStruct((8, 128), jnp.float32)


def call(body, name, grid, ins, outs, scalars=(), scratch=(), flops=0, moved=0, vmem=12):
    return pl.pallas_call(
        body,
        name=name,
        out_shape=[jax.ShapeDtypeStruct(shape, kind) for shape, kind, _, _ in outs],
        grid_spec=pltpu.PrefetchScalarGridSpec(
            num_scalar_prefetch=len(scalars),
            grid=grid,
            in_specs=[pl.BlockSpec(block, place) for _, block, place in ins],
            out_specs=[pl.BlockSpec(block, place) for _, _, block, place in outs],
            scratch_shapes=scratch,
        ),
        compiler_params=pltpu.CompilerParams(vmem_limit_bytes=vmem * MIB),
        cost_estimate=pl.CostEstimate(flops=flops, bytes_accessed=moved, transcendentals=0),
    )(*scalars, *(array for array, _, _ in ins))


def fixed(*place):
    return lambda *_: place


def token_in(token):
    return (token, (8, 128), fixed(0, 0))


TOKEN_OUT = ((8, 128), jnp.float32, (8, 128), fixed(0, 0))


def hop(value, step, pairs):
    return lax.ppermute(value, "fsdp", [(i, i + step) for i in pairs])


def hops(right, left, rights, lefts):
    return hop(right, 1, rights), hop(left, -1, lefts)


def tile_of(width, most=512):
    tile = most
    while width % tile:
        tile //= 2
    return tile


def cut_heads(heads, start, size, members, token):
    inner = heads.shape[1]
    rows = inner // members
    step = size // 2

    def body(heads_ref, *refs):
        for k in range(members):
            refs[-1][k] = heads_ref[:, k * rows : (k + 1) * rows]

    return call(
        body,
        "cut_heads",
        (size // step,),
        [(heads, (step, inner), lambda i: (start // step + i, 0))]
        + ([] if token is None else [token_in(token)]),
        [((members, size, rows), heads.dtype, (members, step, rows), lambda i: (0, i, 0))],
        moved=4 * size * inner,
        vmem=12 if start else 56,
    )[0]


def scaled_weights(numer, weight_one, scaling):
    rows, width = numer.shape
    step = rows // 4

    def body(numer_ref, one_ref, out_ref, token_out):
        out_ref[...] = (numer_ref[...] / one_ref[...] * scaling).astype(jnp.bfloat16)
        token_out[...] = jnp.zeros((8, 128), jnp.float32)

    block = (step, width), lambda i: (i, 0)
    return call(
        body,
        "scaled_weights",
        (rows // step,),
        [(numer,) + block, (weight_one.reshape(1, 1), (1, 1), fixed(0, 0))],
        [((rows, width), jnp.bfloat16) + block, TOKEN_OUT],
        flops=2 * rows * width,
        moved=6 * rows * width,
        vmem=56,
    )


def partial_products(mine, weights, ends, token=None):
    mine, index, size = mine
    members, _, rows = mine.shape
    width = weights.shape[1]
    tile = tile_of(width, 1280)

    def body(mine_ref, weights_ref, *refs):
        out_ref, token_out, *end_refs = refs[0 if token is None else 1 :]
        product = jnp.dot(
            mine_ref[...].reshape(members * size, rows),
            weights_ref[...],
            preferred_element_type=jnp.float32,
        ).astype(jnp.bfloat16)
        out_ref[...] = product.reshape(members, size, tile)
        token_out[...] = jnp.zeros((8, 128), jnp.float32)
        if ends:
            end_refs[0][...] = product[(members - 1) * size :]
            end_refs[1][...] = product[:size]

    flat = ((size, width), jnp.bfloat16, (size, tile), lambda j: (0, j))
    return call(
        body,
        "partial_products",
        (width // tile,),
        [
            (mine, (members, size, rows), fixed(0, index, 0)),
            (weights, (rows, tile), lambda j: (0, j)),
        ]
        + ([] if token is None else [token_in(token)]),
        [
            ((members, size, width), jnp.bfloat16, (members, size, tile), lambda j: (0, 0, j)),
            TOKEN_OUT,
        ]
        + [flat, flat] * ends,
        flops=2 * members * size * rows * width,
        moved=2 * (members * size * (rows + width) + rows * width),
        vmem=20,
    )


def next_payload(right, left, parts, scalars, pick, token=None):
    members, size, width = parts.shape
    step = size // 2

    def joined(arrived, part, counts):
        if pick:
            return jnp.where(counts, part, arrived)
        weight = jnp.where(counts, 1.0, 0.0)
        return (arrived.astype(jnp.float32) + weight * part.astype(jnp.float32)).astype(
            jnp.bfloat16
        )

    def body(s, right_ref, left_ref, of_right, of_left, *refs):
        right_out, left_out, token_out = refs[-3:]
        right_out[...] = joined(right_ref[...], of_right[0], s[1] > 0)
        left_out[...] = joined(left_ref[...], of_left[0], s[3] > 0)
        token_out[...] = jnp.zeros((8, 128), jnp.float32)

    here = (step, width), lambda i, s: (i, 0)
    flat = ((size, width), jnp.bfloat16) + here
    return call(
        body,
        "next_payload",
        (size // step,),
        [
            (right,) + here,
            (left,) + here,
            (parts, (1, step, width), lambda i, s: (s[0], i, 0)),
            (parts, (1, step, width), lambda i, s: (s[2], i, 0)),
        ]
        + ([] if token is None else [token_in(token)]),
        [flat, flat, TOKEN_OUT],
        scalars=(scalars,),
        flops=2 * size * width,
        moved=12 * size * width,
    )


def unit_gradient(right, left, parts, place, residual, cotangent, gain, start, token):
    members, size, width = parts.shape
    step = size // 2

    def body(s, right_ref, left_ref, own_ref, residual_ref, cot_ref, gain_ref, *refs):
        product = (
            right_ref[...].astype(jnp.float32)
            + left_ref[...].astype(jnp.float32)
            + own_ref[0].astype(jnp.float32)
        )
        summed = residual_ref[...].astype(jnp.float32) + product
        inverse = lax.rsqrt(jnp.mean(summed * summed, axis=-1, keepdims=True) + 1e-05)
        scaled_cot = gain_ref[...] * cot_ref[...].astype(jnp.float32)
        along = jnp.mean(scaled_cot * summed, axis=-1, keepdims=True)
        refs[-1][...] = (
            inverse * scaled_cot - summed * (inverse * inverse * inverse * along)
        ).astype(jnp.bfloat16)

    here = (step, width), lambda i, s: (i, 0)
    there = (step, width), lambda i, s: (start // step + i, 0)
    return call(
        body,
        "unit_gradient",
        (size // step,),
        [
            (right,) + here,
            (left,) + here,
            (parts, (1, step, width), lambda i, s: (s[0], i, 0)),
            (residual,) + there,
            (cotangent,) + there,
            (gain, (1, width), fixed(0, 0)),
        ]
        + ([] if token is None else [token_in(token)]),
        [((size, width), jnp.bfloat16) + here],
        scalars=(place,),
        flops=12 * size * width,
        moved=12 * size * width,
    )[0]


def stack_of(refs, members, me):
    count = 2 * members - 1
    rows = []
    for c in range(len(refs) // count):
        own, rights, lefts = (
            refs[c * count],
            refs[c * count + 1 : c * count + members],
            refs[c * count + members : (c + 1) * count],
        )
        rows.append(own[...])
        for k in range(members - 1):
            rows.append(jnp.where(me > k, rights[k][...], lefts[members - 2 - k][...]))
    return jnp.concatenate(rows, axis=0)


def unit_ins(units, tile):
    ins = []
    for chunk in units:
        block = (chunk[0].shape[0], tile)
        members = (len(chunk) + 1) // 2
        ins.append((chunk[0], block, lambda j, s: (0, j)))
        for k in range(members - 1):
            place = lambda j, s, k=k: (0, jnp.where(s[0] > k, j, 0))
            ins.append((chunk[1 + k], block, place))
        for m in range(members - 1):
            place = lambda j, s, k=members - 2 - m: (0, jnp.where(s[0] > k, 0, j))
            ins.append((chunk[members + m], block, place))
    return ins


def mine_ins(mine):
    return [
        (array, (array.shape[0], size, array.shape[2]), fixed(0, index, 0))
        for array, index, size in mine
    ]


def turned_into(scratch, mine_refs, order):
    members = mine_refs[0].shape[0]
    stack = jnp.concatenate([ref[order[k]] for ref in mine_refs for k in range(members)], axis=0)
    scratch[...] = stack.T


def weight_step(units, mine, order, base, half=False, inbox=None, token=None):
    members, _, rows = mine[0][0].shape
    width = base.shape[1]
    tile = tile_of(width)
    count = len(units) * len(units[0])
    chunks = len(units)
    total = sum(members * size for _, _, size in mine)
    early = inbox is None and not half

    def body(s, *refs):
        units_ref, mine_refs = refs[:count], refs[count : count + chunks]
        base_ref = refs[count + chunks]
        turned = refs[-1]

        @pl.when(pl.program_id(0) == 0)
        def _():
            turned_into(turned, mine_refs, s)

        weight = jnp.dot(
            turned[...], stack_of(units_ref, members, s[0]), preferred_element_type=jnp.float32
        )
        if early:
            refs[-3][...] = 0.5 * (base_ref[...] - 0.004 * weight)
            refs[-2][...] = jnp.zeros((8, 128), jnp.float32)
        else:
            now = base_ref[...] - 0.5 * 0.004 * weight
            if inbox is not None:
                refs[-2][...] = now + refs[count + chunks + 1][...]
            else:
                refs[-2][...] = now.astype(jnp.bfloat16)

    columns = (rows, tile), lambda j, s: (0, j)
    ins = unit_ins(units, tile) + mine_ins(mine) + [(base,) + columns]
    if inbox is not None:
        ins.append((inbox,) + columns)
    if token is not None:
        ins.append(token_in(token))
    kind = jnp.bfloat16 if half else jnp.float32
    outs = [((rows, width), kind) + columns]
    return call(
        body,
        "weight_step",
        (width // tile,),
        ins,
        outs + [TOKEN_OUT] * early,
        scalars=(order,),
        scratch=[pltpu.VMEM((rows, total), jnp.bfloat16)],
        flops=2 * total * rows * width,
        moved=(2 * count * units[0][0].shape[0] + 12 * rows) * width,
        vmem=26 if early else 52,
    )


def grad_rows(units, weights, order):
    members = (len(units[0]) + 1) // 2
    sizes = [chunk[0].shape[0] for chunk in units]
    rows, width = weights.shape
    tile = tile_of(width)
    steps = width // tile
    count = len(units) * len(units[0])
    total = members * sum(sizes)

    def body(s, *refs):
        weights_ref, grad_ref, token_out, acc = refs[count:]
        token_out[...] = jnp.zeros((8, 128), jnp.float32)
        j = pl.program_id(0)
        grad = lax.dot_general(
            stack_of(refs[:count], members, s[0]),
            weights_ref[...],
            (((1,), (1,)), ((), ())),
            preferred_element_type=jnp.float32,
        )

        @pl.when(j == 0)
        def _():
            acc[...] = grad

        @pl.when(j > 0)
        def _():
            acc[...] += grad

        @pl.when(j == steps - 1)
        def _():
            at, row = 0, 0
            for size in sizes:
                for k in range(members):
                    grad_ref[s[k], row : row + size] = acc[at : at + size].astype(jnp.bfloat16)
                    at += size
                row += size

    return call(
        body,
        "grad_rows",
        (steps,),
        unit_ins(units, tile) + [(weights, (rows, tile), lambda j, s: (0, j))],
        [
            (
                (members, sum(sizes), rows),
                jnp.bfloat16,
                (members, sum(sizes), rows),
                fixed(0, 0, 0),
            ),
            TOKEN_OUT,
        ],
        scalars=(order,),
        scratch=[pltpu.VMEM((total, rows), jnp.float32)],
        flops=2 * total * rows * width,
        moved=2 * count * sizes[0] * width + 2 * rows * width,
        vmem=50,
    )


def joined_rows(groups):
    members, size, rows = groups[0].shape
    tokens = size * len(groups)

    def body(*refs):
        out_ref = refs[-1]
        for g, blocks_ref in enumerate(refs[:-1]):

            @pl.when(pl.program_id(0) == g)
            def _(blocks_ref=blocks_ref):
                for k in range(members):
                    out_ref[:, k * rows : (k + 1) * rows] = blocks_ref[k]

    return call(
        body,
        "joined_rows",
        (len(groups),),
        [(blocks, (members, size, rows), fixed(0, 0, 0)) for blocks in groups],
        [
            (
                (tokens, members * rows),
                groups[0].dtype,
                (size, members * rows),
                lambda i: (i, 0),
            )
        ],
        moved=4 * members * tokens * rows,
        vmem=24,
    )[0]


def widened(value):
    rows, width = value.shape
    step = rows // 2

    def body(value_ref, out_ref):
        out_ref[...] = value_ref[...].astype(jnp.float32)

    block = (step, width), lambda i: (i, 0)
    return call(
        body,
        "widened",
        (rows // step,),
        [(value,) + block],
        [((rows, width), jnp.float32) + block],
        moved=6 * rows * width,
        vmem=20,
    )[0]


def swapped(blocks):
    return lax.all_to_all(blocks, "fsdp", 0, 0, tiled=False)


def tail(half, grads, late, mine, kept, inbox, weights, order, bit_place):
    length = lax.axis_size("rep")
    sent = lax.ppermute(
        half, "rep", [(i, (i + (1 << bit_place)) % length) for i in range(length)]
    )
    back = swapped(grads)
    late_grads, token = grad_rows(late, weights, order)
    late_back = swapped(late_grads)
    new = weight_step(late, mine, order, kept, inbox=inbox, token=token)[0]
    return sent, joined_rows([back, late_back]), new


def local(
    params, push_weight, inbox_params, inbox_weight, heads, residual, cotangent, gain, offset
):
    numer = params[0]
    weight_one = push_weight[0]
    members = lax.axis_size("fsdp")
    me = lax.axis_index("fsdp").astype(jnp.int32)
    tokens, inner = heads.shape[1:]
    rows, width = numer.shape
    scaling = inner ** (-0.5)
    rounds = len(STREAMS[0])
    assert sum(map(sum, STREAMS)) == tokens

    replicas = lax.axis_size("rep")
    levels = replicas.bit_length() - 1
    powers = jnp.left_shift(jnp.ones((levels,), jnp.int32), jnp.arange(levels, dtype=jnp.int32))
    level_index = jnp.sum(jnp.where(powers == offset[0], jnp.arange(levels, dtype=jnp.int32), 0))

    half_weight = 0.5 * push_weight
    arrived = [
        lax.ppermute(half_weight, "rep", [(i, (i + (1 << b)) % replicas) for i in range(replicas)])
        for b in range(levels)
    ]
    outbox_weight = arrived[0]
    for b in range(1, levels):
        outbox_weight = jnp.where(level_index == b, arrived[b], outbox_weight)

    order = jnp.mod(me - jnp.arange(members, dtype=jnp.int32), members)
    own = me[None]
    weights, token = scaled_weights(numer, weight_one, scaling)
    everyone = range(members - 1), range(1, members)

    def scalars(t):
        ahead = members - 1 - t
        return jnp.stack(
            [
                jnp.minimum(me + ahead, members - 1),
                (me <= t).astype(jnp.int32),
                jnp.maximum(me - ahead, 0),
                (me >= ahead).astype(jnp.int32),
            ]
        )

    at = 0
    starts = []
    for e in range(rounds):
        starts.append([])
        for sizes in STREAMS:
            starts[e].append(at)
            at += sizes[e]

    count = len(STREAMS)
    mine = [[None] * count for _ in range(rounds)]
    units = [[None] * count for _ in range(rounds)]
    before = [None] * count
    hint = [None] * count

    def fetch(e, members_of, token):
        size = STREAMS[members_of[0]][e]
        piece = cut_heads(
            heads[0], starts[e][members_of[0]], size * len(members_of), members, token
        )
        array = swapped(piece)
        for index, q in enumerate(members_of):
            mine[e][q] = (array, index, size)

    for q in range(count):
        fetch(0, [q], token + outbox_weight[0] if q else None)
    parts = [None] * count
    token = None
    for q in range(count):
        parts[q], token, last, first = partial_products(mine[0][q], weights, True, token)
        hint[q] = (last, first)
    for e in range(rounds):
        moving = [None] * count
        for q in range(count):
            if e == 0:
                moving[q] = hops(*hint[q], range(1), range(members - 1, members))
            else:
                right, left, _ = next_payload(*before[q], parts[q], scalars(0), True)
                moving[q] = hops(right, left, *everyone)
                units[e - 1][q][1].append(moving[q][0])
                units[e - 1][q][2].append(moving[q][1])
        for t in range(1, members - 1):
            for q in range(count):
                order_token = token if (e, t, q) == (0, 1, 0) else None
                right, left, token = next_payload(
                    *moving[q], parts[q], scalars(t), False, order_token
                )
                if q == count - 1 and t <= count and e + 1 < rounds:
                    fetch(e + 1, [t - 1], token)
                if e == 0:
                    pairs = range(t + 1), range(members - 1 - t, members)
                else:
                    pairs = everyone
                moving[q] = hops(right, left, *pairs)
                if e > 0 and t < members - 2:
                    units[e - 1][q][1].append(moving[q][0])
                    units[e - 1][q][2].append(moving[q][1])
        later = [None] * count
        for q in range(count):
            token = None
            if e + 1 < rounds:
                later[q], token = partial_products(mine[e + 1][q], weights, False)
            elif q == count - 1:
                early = [[u] + r + l for of_round in units[:-1] for u, r, l in of_round]
                early_mine = [m for of_round in mine[:-1] for m in of_round]
                kept, token = weight_step(early, early_mine, order, numer)
            unit = unit_gradient(
                *moving[q],
                parts[q],
                own,
                residual[0],
                cotangent[0],
                gain[None],
                starts[e][q],
                token,
            )
            before[q] = hops(unit, unit, *everyone)
            units[e][q] = (unit, [before[q][0]], [before[q][1]])
        parts = later
    for s in range(1, members - 1):
        for q in range(count):
            before[q] = hops(*before[q], range(s, members - 1), range(1, members - s))
            units[-1][q][1].append(before[q][0])
            units[-1][q][2].append(before[q][1])
    flat = [[u] + r + l for u, r, l in units[-1]]
    grads, _ = grad_rows(early, weights, order)
    half = weight_step(flat, mine[-1], order, kept, half=True)[0]
    new_weight = 0.5 * push_weight + inbox_weight
    branches = [
        partial(
            tail, half, grads, flat, mine[-1], kept, inbox_params[0], weights, order, place
        )
        for place in range(levels)
    ]
    sent, grad_heads, new_params = lax.switch(level_index, branches)
    return (new_params[None], new_weight, widened(sent)[None], outbox_weight, grad_heads[None])


def solution(mesh):
    placed = (
        P("rep", "fsdp", None),
        P("rep"),
        P("rep", "fsdp", None),
        P("rep"),
        P("rep", "fsdp", None),
        P("rep", "fsdp", None),
        P("rep", "fsdp", None),
        P(),
        P(),
    )
    return jax.shard_map(
        local,
        mesh=mesh,
        in_specs=placed,
        out_specs=(
            P("rep", "fsdp", None),
            P("rep"),
            P("rep", "fsdp", None),
            P("rep"),
            P("rep", "fsdp", None),
        ),
        check_vma=False,
    )
```

```python
from functools import partial

import jax
import jax.numpy as jnp
from jax import lax
from jax.experimental import pallas as pl
from jax.experimental.pallas import tpu as pltpu
from jax.sharding import PartitionSpec as P

STREAMS = ((96, 96), (96, 96))
MIB = 1 << 20
TOKEN = jax.ShapeDtypeStruct((8, 128), jnp.float32)


def call(body, name, grid, ins, outs, scalars=(), scratch=(), flops=0, moved=0, vmem=12):
    return pl.pallas_call(
        body,
        name=name,
        out_shape=[jax.ShapeDtypeStruct(shape, kind) for shape, kind, _, _ in outs],
        grid_spec=pltpu.PrefetchScalarGridSpec(
            num_scalar_prefetch=len(scalars),
            grid=grid,
            in_specs=[pl.BlockSpec(block, place) for _, block, place in ins],
            out_specs=[pl.BlockSpec(block, place) for _, _, block, place in outs],
            scratch_shapes=scratch,
        ),
        compiler_params=pltpu.CompilerParams(vmem_limit_bytes=vmem * MIB),
        cost_estimate=pl.CostEstimate(flops=flops, bytes_accessed=moved, transcendentals=0),
    )(*scalars, *(array for array, _, _ in ins))


def fixed(*place):
    return lambda *_: place


def token_in(token):
    return (token, (8, 128), fixed(0, 0))


TOKEN_OUT = ((8, 128), jnp.float32, (8, 128), fixed(0, 0))


def hop(value, step, pairs):
    return lax.ppermute(value, "fsdp", [(i, i + step) for i in pairs])


def hops(right, left, rights, lefts):
    return hop(right, 1, rights), hop(left, -1, lefts)


def tile_of(width, most=512):
    tile = most
    while width % tile:
        tile //= 2
    return tile


def cut_heads(heads, start, size, members, token):
    inner = heads.shape[1]
    rows = inner // members
    step = 48

    def body(heads_ref, *refs):
        for k in range(members):
            refs[-1][k] = heads_ref[:, k * rows : (k + 1) * rows]

    return call(
        body,
        "cut_heads",
        (size // step,),
        [(heads, (step, inner), lambda i: (start // step + i, 0))]
        + ([] if token is None else [token_in(token)]),
        [((members, size, rows), heads.dtype, (members, step, rows), lambda i: (0, i, 0))],
        moved=4 * size * inner,
    )[0]


def partial_products(mine, weights, token):
    members, size, rows = mine.shape
    width = weights.shape[1]
    tile = tile_of(width, 1280)

    def body(mine_ref, weights_ref, *refs):
        out_ref, last_ref, first_ref = refs[-3:]
        product = jnp.dot(
            mine_ref[...].reshape(members * size, rows),
            weights_ref[...],
            preferred_element_type=jnp.float32,
        ).astype(jnp.bfloat16)
        out_ref[...] = product.reshape(members, size, tile)
        last_ref[...] = product[(members - 1) * size :]
        first_ref[...] = product[:size]

    flat = ((size, width), jnp.bfloat16, (size, tile), lambda j: (0, j))
    return call(
        body,
        "partial_products",
        (width // tile,),
        [
            (mine, (members, size, rows), fixed(0, 0, 0)),
            (weights, (rows, tile), lambda j: (0, j)),
        ]
        + ([] if token is None else [token_in(token)]),
        [
            (
                (members, size, width),
                jnp.bfloat16,
                (members, size, tile),
                lambda j: (0, 0, j),
            ),
            flat,
            flat,
        ],
        flops=2 * members * size * rows * width,
        moved=2 * (members * size * (rows + width) + rows * width),
        vmem=20,
    )


def next_payload(right, left, parts, scalars, pick):
    members, size, width = parts.shape
    step = 48

    def joined(arrived, part, counts):
        if pick:
            return jnp.where(counts, part, arrived)
        weight = jnp.where(counts, 1.0, 0.0)
        return (arrived.astype(jnp.float32) + weight * part.astype(jnp.float32)).astype(
            jnp.bfloat16
        )

    def body(s, right_ref, left_ref, of_right, of_left, right_out, left_out, token_out):
        right_out[...] = joined(right_ref[...], of_right[0], s[1] > 0)
        left_out[...] = joined(left_ref[...], of_left[0], s[3] > 0)
        token_out[...] = jnp.zeros((8, 128), jnp.float32)

    here = (step, width), lambda i, s: (i, 0)
    flat = ((size, width), jnp.bfloat16) + here
    return call(
        body,
        "next_payload",
        (size // step,),
        [
            (right,) + here,
            (left,) + here,
            (parts, (1, step, width), lambda i, s: (s[0], i, 0)),
            (parts, (1, step, width), lambda i, s: (s[2], i, 0)),
        ],
        [flat, flat, TOKEN_OUT],
        scalars=(scalars,),
        flops=2 * size * width,
        moved=12 * size * width,
    )


def unit_gradient(right, left, parts, place, residual, cotangent, gain, start, token):
    members, size, width = parts.shape
    step = 48

    def body(s, right_ref, left_ref, own_ref, residual_ref, cot_ref, gain_ref, *refs):
        product = (
            right_ref[...].astype(jnp.float32)
            + left_ref[...].astype(jnp.float32)
            + own_ref[0].astype(jnp.float32)
        )
        summed = residual_ref[...].astype(jnp.float32) + product
        inverse = lax.rsqrt(jnp.mean(summed * summed, axis=-1, keepdims=True) + 1e-05)
        scaled_cot = gain_ref[...] * cot_ref[...].astype(jnp.float32)
        along = jnp.mean(scaled_cot * summed, axis=-1, keepdims=True)
        refs[-1][...] = (
            inverse * scaled_cot - summed * (inverse * inverse * inverse * along)
        ).astype(jnp.bfloat16)

    here = (step, width), lambda i, s: (i, 0)
    there = (step, width), lambda i, s: (start // step + i, 0)
    return call(
        body,
        "unit_gradient",
        (size // step,),
        [
            (right,) + here,
            (left,) + here,
            (parts, (1, step, width), lambda i, s: (s[0], i, 0)),
            (residual,) + there,
            (cotangent,) + there,
            (gain, (1, width), fixed(0, 0)),
        ]
        + ([] if token is None else [token_in(token)]),
        [((size, width), jnp.bfloat16) + here],
        scalars=(place,),
        flops=12 * size * width,
        moved=12 * size * width,
    )[0]


def stack_of(refs, members, me):
    count = 2 * members - 1
    rows = []
    for c in range(len(refs) // count):
        own, rights, lefts = (
            refs[c * count],
            refs[c * count + 1 : c * count + members],
            refs[c * count + members : (c + 1) * count],
        )
        rows.append(own[...])
        for k in range(members - 1):
            rows.append(jnp.where(me > k, rights[k][...], lefts[members - 2 - k][...]))
    return jnp.concatenate(rows, axis=0)


def unit_ins(units, tile):
    ins = []
    for chunk in units:
        block = (chunk[0].shape[0], tile)
        members = (len(chunk) + 1) // 2
        ins.append((chunk[0], block, lambda j, s: (0, j)))
        for k in range(members - 1):
            place = lambda j, s, k=k: (0, jnp.where(s[0] > k, j, 0))
            ins.append((chunk[1 + k], block, place))
        for m in range(members - 1):
            place = lambda j, s, k=members - 2 - m: (0, jnp.where(s[0] > k, 0, j))
            ins.append((chunk[members + m], block, place))
    return ins


def mine_ins(mine):
    return [(block, block.shape, fixed(0, 0, 0)) for block in mine]


def turned_into(scratch, mine_refs, order):
    members = mine_refs[0].shape[0]
    stack = jnp.concatenate([ref[order[k]] for ref in mine_refs for k in range(members)], axis=0)
    scratch[...] = stack.T


def weight_step(units, mine, order, base, half=False, inbox=None, token=None):
    members, _, rows = mine[0].shape
    width = base.shape[1]
    tile = tile_of(width)
    count = len(units) * len(units[0])
    chunks = len(units)
    total = sum(members * block.shape[1] for block in mine)
    early = inbox is None and not half

    def body(s, *refs):
        units_ref, mine_refs = refs[:count], refs[count : count + chunks]
        base_ref = refs[count + chunks]
        turned = refs[-1]

        @pl.when(pl.program_id(0) == 0)
        def _():
            turned_into(turned, mine_refs, s)

        weight = jnp.dot(
            turned[...], stack_of(units_ref, members, s[0]), preferred_element_type=jnp.float32
        )
        if early:
            refs[-3][...] = 0.5 * (base_ref[...] - 0.004 * weight)
            refs[-2][...] = jnp.zeros((8, 128), jnp.float32)
        else:
            now = base_ref[...] - 0.5 * 0.004 * weight
            if inbox is not None:
                refs[-2][...] = now + refs[count + chunks + 1][...]
            else:
                refs[-2][...] = now.astype(jnp.bfloat16)

    columns = (rows, tile), lambda j, s: (0, j)
    ins = unit_ins(units, tile) + mine_ins(mine) + [(base,) + columns]
    if inbox is not None:
        ins.append((inbox,) + columns)
    if token is not None:
        ins.append(token_in(token))
    kind = jnp.bfloat16 if half else jnp.float32
    outs = [((rows, width), kind) + columns]
    return call(
        body,
        "weight_step",
        (width // tile,),
        ins,
        outs + [TOKEN_OUT] * early,
        scalars=(order,),
        scratch=[pltpu.VMEM((rows, total), jnp.bfloat16)],
        flops=2 * total * rows * width,
        moved=(2 * count * units[0][0].shape[0] + 12 * rows) * width,
        vmem=26 if early else 52,
    )


def grad_rows(units, weights, order):
    members = (len(units[0]) + 1) // 2
    sizes = [chunk[0].shape[0] for chunk in units]
    rows, width = weights.shape
    tile = tile_of(width)
    steps = width // tile
    count = len(units) * len(units[0])
    total = members * sum(sizes)

    def body(s, *refs):
        weights_ref, grad_ref, token_out, acc = refs[count:]
        token_out[...] = jnp.zeros((8, 128), jnp.float32)
        j = pl.program_id(0)
        grad = lax.dot_general(
            stack_of(refs[:count], members, s[0]),
            weights_ref[...],
            (((1,), (1,)), ((), ())),
            preferred_element_type=jnp.float32,
        )

        @pl.when(j == 0)
        def _():
            acc[...] = grad

        @pl.when(j > 0)
        def _():
            acc[...] += grad

        @pl.when(j == steps - 1)
        def _():
            at, row = 0, 0
            for size in sizes:
                for k in range(members):
                    grad_ref[s[k], row : row + size] = acc[at : at + size].astype(jnp.bfloat16)
                    at += size
                row += size

    return call(
        body,
        "grad_rows",
        (steps,),
        unit_ins(units, tile) + [(weights, (rows, tile), lambda j, s: (0, j))],
        [
            (
                (members, sum(sizes), rows),
                jnp.bfloat16,
                (members, sum(sizes), rows),
                fixed(0, 0, 0),
            ),
            TOKEN_OUT,
        ],
        scalars=(order,),
        scratch=[pltpu.VMEM((total, rows), jnp.float32)],
        flops=2 * total * rows * width,
        moved=2 * count * sizes[0] * width + 2 * rows * width,
        vmem=50,
    )


def joined_rows(groups):
    members, size, rows = groups[0].shape
    tokens = size * len(groups)

    def body(*refs):
        out_ref = refs[-1]
        for g, blocks_ref in enumerate(refs[:-1]):

            @pl.when(pl.program_id(0) == g)
            def _(blocks_ref=blocks_ref):
                for k in range(members):
                    out_ref[:, k * rows : (k + 1) * rows] = blocks_ref[k]

    return call(
        body,
        "joined_rows",
        (len(groups),),
        [(blocks, (members, size, rows), fixed(0, 0, 0)) for blocks in groups],
        [
            (
                (tokens, members * rows),
                groups[0].dtype,
                (size, members * rows),
                lambda i: (i, 0),
            )
        ],
        moved=4 * members * tokens * rows,
        vmem=24,
    )[0]


def widened(value):
    rows, width = value.shape
    step = rows // 2

    def body(value_ref, out_ref):
        out_ref[...] = value_ref[...].astype(jnp.float32)

    block = (step, width), lambda i: (i, 0)
    return call(
        body,
        "widened",
        (rows // step,),
        [(value,) + block],
        [((rows, width), jnp.float32) + block],
        moved=6 * rows * width,
        vmem=20,
    )[0]


def swapped(blocks):
    return lax.all_to_all(blocks, "fsdp", 0, 0, tiled=False)


def tail(half, grads, late, mine, kept, inbox, weights, order, bit_place):
    length = lax.axis_size("rep")
    sent = lax.ppermute(
        half, "rep", [(i, (i + (1 << bit_place)) % length) for i in range(length)]
    )
    back = swapped(grads)
    late_grads, token = grad_rows(late, weights, order)
    late_back = swapped(late_grads)
    new = weight_step(late, mine, order, kept, inbox=inbox, token=token)[0]
    return sent, joined_rows([back, late_back]), new


def local(
    params, push_weight, inbox_params, inbox_weight, heads, residual, cotangent, gain, offset
):
    numer = params[0]
    weight_one = push_weight[0]
    members = lax.axis_size("fsdp")
    me = lax.axis_index("fsdp").astype(jnp.int32)
    tokens, inner = heads.shape[1:]
    rows, width = numer.shape
    scaling = inner ** (-0.5)
    rounds = len(STREAMS[0])
    assert sum(map(sum, STREAMS)) == tokens

    replicas = lax.axis_size("rep")
    levels = replicas.bit_length() - 1
    powers = jnp.left_shift(jnp.ones((levels,), jnp.int32), jnp.arange(levels, dtype=jnp.int32))
    level_index = jnp.sum(jnp.where(powers == offset[0], jnp.arange(levels, dtype=jnp.int32), 0))
    half_weight = 0.5 * push_weight
    arrived = [
        lax.ppermute(half_weight, "rep", [(i, (i + (1 << b)) % replicas) for i in range(replicas)])
        for b in range(levels)
    ]
    outbox_weight = arrived[0]
    for b in range(1, levels):
        outbox_weight = jnp.where(level_index == b, arrived[b], outbox_weight)

    order = jnp.mod(me - jnp.arange(members, dtype=jnp.int32), members)
    own = me[None]
    weights = (numer / weight_one * scaling).astype(jnp.bfloat16)
    everyone = range(members - 1), range(1, members)

    def scalars(t):
        ahead = members - 1 - t
        return jnp.stack(
            [
                jnp.minimum(me + ahead, members - 1),
                (me <= t).astype(jnp.int32),
                jnp.maximum(me - ahead, 0),
                (me >= ahead).astype(jnp.int32),
            ]
        )

    at = 0
    starts = []
    for e in range(rounds):
        starts.append([])
        for sizes in STREAMS:
            starts[e].append(at)
            at += sizes[e]

    count = len(STREAMS)
    mine = [[None] * count for _ in range(rounds)]
    units = [[None] * count for _ in range(rounds)]
    before = [None] * count
    hint = [None] * (count - 1) + [jnp.broadcast_to(outbox_weight[None], (8, 128))]

    def fetch(e, q, token):
        piece = cut_heads(heads[0], starts[e][q], STREAMS[q][e], members, token)
        mine[e][q] = swapped(piece)

    for q in range(count):
        fetch(0, q, None)
    done = None
    for e in range(rounds):
        parts, moving = [None] * count, [None] * count
        for q in range(count):
            parts[q], last, first = partial_products(mine[e][q], weights, hint[q])
            if e == 0:
                moving[q] = hops(last, first, range(1), range(members - 1, members))
            else:
                right, left, _ = next_payload(*before[q], parts[q], scalars(0), True)
                moving[q] = hops(right, left, *everyone)
                units[e - 1][q][1].append(moving[q][0])
                units[e - 1][q][2].append(moving[q][1])
        for t in range(1, members - 1):
            for q in range(count):
                right, left, token = next_payload(*moving[q], parts[q], scalars(t), False)
                if t == 1 and e + 1 < rounds:
                    fetch(e + 1, q, token)
                hint[q] = token
                if e == 0:
                    pairs = range(t + 1), range(members - 1 - t, members)
                else:
                    pairs = everyone
                moving[q] = hops(right, left, *pairs)
                if e > 0 and t < members - 2:
                    units[e - 1][q][1].append(moving[q][0])
                    units[e - 1][q][2].append(moving[q][1])
        if e > 0:
            early = [[u] + r + l for u, r, l in units[e - 1]]
            kept, done = weight_step(early, mine[e - 1], order, numer)
            grads, _ = grad_rows(early, weights, order)
        for q in range(count):
            unit = unit_gradient(
                *moving[q],
                parts[q],
                own,
                residual[0],
                cotangent[0],
                gain[None],
                starts[e][q],
                done if q == count - 1 else None,
            )
            before[q] = hops(unit, unit, *everyone)
            units[e][q] = (unit, [before[q][0]], [before[q][1]])
    for s in range(1, members - 1):
        for q in range(count):
            before[q] = hops(*before[q], range(s, members - 1), range(1, members - s))
            units[-1][q][1].append(before[q][0])
            units[-1][q][2].append(before[q][1])
    flat = [[u] + r + l for u, r, l in units[-1]]
    half = weight_step(flat, mine[-1], order, kept, half=True)[0]
    new_weight = 0.5 * push_weight + inbox_weight
    branches = [
        partial(
            tail, half, grads, flat, mine[-1], kept, inbox_params[0], weights, order, place
        )
        for place in range(levels)
    ]
    sent, grad_heads, new_params = lax.switch(level_index, branches)
    return (new_params[None], new_weight, widened(sent)[None], outbox_weight, grad_heads[None])


def solution(mesh):
    placed = (
        P("rep", "fsdp", None),
        P("rep"),
        P("rep", "fsdp", None),
        P("rep"),
        P("rep", "fsdp", None),
        P("rep", "fsdp", None),
        P("rep", "fsdp", None),
        P(),
        P(),
    )
    return jax.shard_map(
        local,
        mesh=mesh,
        in_specs=placed,
        out_specs=(
            P("rep", "fsdp", None),
            P("rep"),
            P("rep", "fsdp", None),
            P("rep"),
            P("rep", "fsdp", None),
        ),
        check_vma=False,
    )
```

```python
from functools import partial

import jax
import jax.numpy as jnp
from jax import lax
from jax.experimental import pallas as pl
from jax.experimental.pallas import tpu as pltpu
from jax.sharding import PartitionSpec as P

STREAMS = ((96, 96), (96, 96))
MIB = 1 << 20
HEAD_TILES = 2
TOKEN = jax.ShapeDtypeStruct((8, 128), jnp.float32)


def call(body, name, grid, ins, outs, scalars=(), scratch=(), flops=0, moved=0, vmem=12):
    return pl.pallas_call(
        body,
        name=name,
        out_shape=[jax.ShapeDtypeStruct(shape, kind) for shape, kind, _, _ in outs],
        grid_spec=pltpu.PrefetchScalarGridSpec(
            num_scalar_prefetch=len(scalars),
            grid=grid,
            in_specs=[pl.BlockSpec(block, place) for _, block, place in ins],
            out_specs=[pl.BlockSpec(block, place) for _, _, block, place in outs],
            scratch_shapes=scratch,
        ),
        compiler_params=pltpu.CompilerParams(vmem_limit_bytes=vmem * MIB),
        cost_estimate=pl.CostEstimate(flops=flops, bytes_accessed=moved, transcendentals=0),
    )(*scalars, *(array for array, _, _ in ins))


def fixed(*place):
    return lambda *_: place


def token_in(token):
    return (token, (8, 128), fixed(0, 0))


TOKEN_OUT = ((8, 128), jnp.float32, (8, 128), fixed(0, 0))


def hop(value, step, pairs):
    return lax.ppermute(value, "fsdp", [(i, i + step) for i in pairs])


def hops(right, left, rights, lefts):
    return hop(right, 1, rights), hop(left, -1, lefts)


def tile_of(width, most=512):
    tile = most
    while width % tile:
        tile //= 2
    return tile


def cut_heads(heads, start, size, members, token):
    inner = heads.shape[1]
    rows = inner // members
    step = 48

    def body(heads_ref, *refs):
        for k in range(members):
            refs[-1][k] = heads_ref[:, k * rows : (k + 1) * rows]

    return call(
        body,
        "cut_heads",
        (size // step,),
        [(heads, (step, inner), lambda i: (start // step + i, 0))]
        + ([] if token is None else [token_in(token)]),
        [((members, size, rows), heads.dtype, (members, step, rows), lambda i: (0, i, 0))],
        moved=4 * size * inner,
    )[0]


def partial_products(mine, weights, token):
    members, size, rows = mine.shape
    width = weights.shape[1]
    tile = tile_of(width, 1280)

    def body(mine_ref, weights_ref, *refs):
        out_ref, last_ref, first_ref = refs[-3:]
        product = jnp.dot(
            mine_ref[...].reshape(members * size, rows),
            weights_ref[...],
            preferred_element_type=jnp.float32,
        ).astype(jnp.bfloat16)
        out_ref[...] = product.reshape(members, size, tile)
        last_ref[...] = product[(members - 1) * size :]
        first_ref[...] = product[:size]

    flat = ((size, width), jnp.bfloat16, (size, tile), lambda j: (0, j))
    return call(
        body,
        "partial_products",
        (width // tile,),
        [
            (mine, (members, size, rows), fixed(0, 0, 0)),
            (weights, (rows, tile), lambda j: (0, j)),
        ]
        + ([] if token is None else [token_in(token)]),
        [
            (
                (members, size, width),
                jnp.bfloat16,
                (members, size, tile),
                lambda j: (0, 0, j),
            ),
            flat,
            flat,
        ],
        flops=2 * members * size * rows * width,
        moved=2 * (members * size * (rows + width) + rows * width),
        vmem=20,
    )


def next_payload(right, left, parts, scalars, pick):
    members, size, width = parts.shape
    step = 48

    def joined(arrived, part, counts):
        if pick:
            return jnp.where(counts, part, arrived)
        weight = jnp.where(counts, 1.0, 0.0)
        return (arrived.astype(jnp.float32) + weight * part.astype(jnp.float32)).astype(
            jnp.bfloat16
        )

    def body(s, right_ref, left_ref, of_right, of_left, right_out, left_out, token_out):
        right_out[...] = joined(right_ref[...], of_right[0], s[1] > 0)
        left_out[...] = joined(left_ref[...], of_left[0], s[3] > 0)
        token_out[...] = jnp.zeros((8, 128), jnp.float32)

    here = (step, width), lambda i, s: (i, 0)
    flat = ((size, width), jnp.bfloat16) + here
    return call(
        body,
        "next_payload",
        (size // step,),
        [
            (right,) + here,
            (left,) + here,
            (parts, (1, step, width), lambda i, s: (s[0], i, 0)),
            (parts, (1, step, width), lambda i, s: (s[2], i, 0)),
        ],
        [flat, flat, TOKEN_OUT],
        scalars=(scalars,),
        flops=2 * size * width,
        moved=12 * size * width,
    )


def unit_gradient(right, left, parts, place, residual, cotangent, gain, start, token):
    members, size, width = parts.shape
    step = 48

    def body(s, right_ref, left_ref, own_ref, residual_ref, cot_ref, gain_ref, *refs):
        product = (
            right_ref[...].astype(jnp.float32)
            + left_ref[...].astype(jnp.float32)
            + own_ref[0].astype(jnp.float32)
        )
        summed = residual_ref[...].astype(jnp.float32) + product
        inverse = lax.rsqrt(jnp.mean(summed * summed, axis=-1, keepdims=True) + 1e-05)
        scaled_cot = gain_ref[...] * cot_ref[...].astype(jnp.float32)
        along = jnp.mean(scaled_cot * summed, axis=-1, keepdims=True)
        refs[-1][...] = (
            inverse * scaled_cot - summed * (inverse * inverse * inverse * along)
        ).astype(jnp.bfloat16)

    here = (step, width), lambda i, s: (i, 0)
    there = (step, width), lambda i, s: (start // step + i, 0)
    return call(
        body,
        "unit_gradient",
        (size // step,),
        [
            (right,) + here,
            (left,) + here,
            (parts, (1, step, width), lambda i, s: (s[0], i, 0)),
            (residual,) + there,
            (cotangent,) + there,
            (gain, (1, width), fixed(0, 0)),
        ]
        + ([] if token is None else [token_in(token)]),
        [((size, width), jnp.bfloat16) + here],
        scalars=(place,),
        flops=12 * size * width,
        moved=12 * size * width,
    )[0]


def stack_of(refs, members, me):
    count = 2 * members - 1
    rows = []
    for c in range(len(refs) // count):
        own, rights, lefts = (
            refs[c * count],
            refs[c * count + 1 : c * count + members],
            refs[c * count + members : (c + 1) * count],
        )
        rows.append(own[...])
        for k in range(members - 1):
            rows.append(jnp.where(me > k, rights[k][...], lefts[members - 2 - k][...]))
    return jnp.concatenate(rows, axis=0)


def unit_ins(units, tile, first=0):
    ins = []
    for chunk in units:
        block = (chunk[0].shape[0], tile)
        members = (len(chunk) + 1) // 2
        ins.append((chunk[0], block, lambda j, s: (0, j + first)))
        for k in range(members - 1):
            place = lambda j, s, k=k: (0, jnp.where(s[0] > k, j, 0) + first)
            ins.append((chunk[1 + k], block, place))
        for m in range(members - 1):
            place = lambda j, s, k=members - 2 - m: (0, jnp.where(s[0] > k, 0, j) + first)
            ins.append((chunk[members + m], block, place))
    return ins


def mine_ins(mine):
    return [(block, block.shape, fixed(0, 0, 0)) for block in mine]


def turned_into(scratch, mine_refs, order):
    members = mine_refs[0].shape[0]
    stack = jnp.concatenate([ref[order[k]] for ref in mine_refs for k in range(members)], axis=0)
    scratch[...] = stack.T


def weight_step(units, mine, order, base, half=False, inbox=None, token=None, span=(0, None)):
    members, _, rows = mine[0].shape
    width = base.shape[1]
    tile = tile_of(width)
    count = len(units) * len(units[0])
    chunks = len(units)
    total = sum(members * block.shape[1] for block in mine)
    early = inbox is None and not half
    first, last = span
    tiles = (width // tile if last is None else last) - first

    def body(s, *refs):
        units_ref, mine_refs = refs[:count], refs[count : count + chunks]
        base_ref = refs[count + chunks]
        turned = refs[-1]

        @pl.when(pl.program_id(0) == 0)
        def _():
            turned_into(turned, mine_refs, s)

        weight = jnp.dot(
            turned[...], stack_of(units_ref, members, s[0]), preferred_element_type=jnp.float32
        )
        if early:
            refs[-3][...] = 0.5 * (base_ref[...] - 0.004 * weight)
            refs[-2][...] = jnp.zeros((8, 128), jnp.float32)
        else:
            now = base_ref[...] - 0.5 * 0.004 * weight
            if inbox is not None:
                refs[-2][...] = now + refs[count + chunks + 1][...]
            else:
                refs[-2][...] = now.astype(jnp.bfloat16)

    columns = (rows, tile), lambda j, s: (0, j + first)
    ins = unit_ins(units, tile, first) + mine_ins(mine) + [(base,) + columns]
    if inbox is not None:
        ins.append((inbox,) + columns)
    if token is not None:
        ins.append(token_in(token))
    kind = jnp.bfloat16 if half else jnp.float32
    outs = [((rows, tile * tiles), kind, (rows, tile), lambda j, s: (0, j))]
    return call(
        body,
        "weight_step",
        (tiles,),
        ins,
        outs + [TOKEN_OUT] * early,
        scalars=(order,),
        scratch=[pltpu.VMEM((rows, total), jnp.bfloat16)],
        flops=2 * total * rows * tile * tiles,
        moved=(2 * count * units[0][0].shape[0] + 12 * rows) * tile * tiles,
        vmem=26 if early else 52,
    )


def grad_rows(units, weights, order):
    members = (len(units[0]) + 1) // 2
    sizes = [chunk[0].shape[0] for chunk in units]
    rows, width = weights.shape
    tile = tile_of(width)
    steps = width // tile
    count = len(units) * len(units[0])
    total = members * sum(sizes)

    def body(s, *refs):
        weights_ref, grad_ref, token_out, acc = refs[count:]
        token_out[...] = jnp.zeros((8, 128), jnp.float32)
        j = pl.program_id(0)
        grad = lax.dot_general(
            stack_of(refs[:count], members, s[0]),
            weights_ref[...],
            (((1,), (1,)), ((), ())),
            preferred_element_type=jnp.float32,
        )

        @pl.when(j == 0)
        def _():
            acc[...] = grad

        @pl.when(j > 0)
        def _():
            acc[...] += grad

        @pl.when(j == steps - 1)
        def _():
            at, row = 0, 0
            for size in sizes:
                for k in range(members):
                    grad_ref[s[k], row : row + size] = acc[at : at + size].astype(jnp.bfloat16)
                    at += size
                row += size

    return call(
        body,
        "grad_rows",
        (steps,),
        unit_ins(units, tile) + [(weights, (rows, tile), lambda j, s: (0, j))],
        [
            (
                (members, sum(sizes), rows),
                jnp.bfloat16,
                (members, sum(sizes), rows),
                fixed(0, 0, 0),
            ),
            TOKEN_OUT,
        ],
        scalars=(order,),
        scratch=[pltpu.VMEM((total, rows), jnp.float32)],
        flops=2 * total * rows * width,
        moved=2 * count * sizes[0] * width + 2 * rows * width,
        vmem=50,
    )


def joined_rows(groups):
    members, size, rows = groups[0].shape
    tokens = size * len(groups)

    def body(*refs):
        out_ref = refs[-1]
        for g, blocks_ref in enumerate(refs[:-1]):

            @pl.when(pl.program_id(0) == g)
            def _(blocks_ref=blocks_ref):
                for k in range(members):
                    out_ref[:, k * rows : (k + 1) * rows] = blocks_ref[k]

    return call(
        body,
        "joined_rows",
        (len(groups),),
        [(blocks, (members, size, rows), fixed(0, 0, 0)) for blocks in groups],
        [
            (
                (tokens, members * rows),
                groups[0].dtype,
                (size, members * rows),
                lambda i: (i, 0),
            )
        ],
        moved=4 * members * tokens * rows,
        vmem=24,
    )[0]


def widened(parts):
    rows = parts[0].shape[0]
    widths = [part.shape[1] for part in parts]
    step = rows // 2

    def body(*refs):
        at = 0
        for part_ref, width in zip(refs[:-1], widths):
            refs[-1][:, at : at + width] = part_ref[...].astype(jnp.float32)
            at += width

    return call(
        body,
        "widened",
        (rows // step,),
        [(part, (step, width), lambda i: (i, 0)) for part, width in zip(parts, widths)],
        [((rows, sum(widths)), jnp.float32, (step, sum(widths)), lambda i: (i, 0))],
        moved=6 * rows * sum(widths),
        vmem=20,
    )[0]


def swapped(blocks):
    return lax.all_to_all(blocks, "fsdp", 0, 0, tiled=False)


def tail(half, grads, late, mine, kept, inbox, weights, order, bit_place):
    length = lax.axis_size("rep")
    pairs = [(i, (i + (1 << bit_place)) % length) for i in range(length)]
    sent = lax.ppermute(half, "rep", pairs)
    back = swapped(grads)
    late_grads, token = grad_rows(late, weights, order)
    late_back = swapped(late_grads)
    other = weight_step(late, mine, order, kept, half=True, token=token, span=(HEAD_TILES, None))[0]
    other_sent = lax.ppermute(other, "rep", pairs)
    new = weight_step(late, mine, order, kept, inbox=inbox, token=token)[0]
    return sent, other_sent, joined_rows([back, late_back]), new


def local(
    params, push_weight, inbox_params, inbox_weight, heads, residual, cotangent, gain, offset
):
    numer = params[0]
    weight_one = push_weight[0]
    members = lax.axis_size("fsdp")
    me = lax.axis_index("fsdp").astype(jnp.int32)
    tokens, inner = heads.shape[1:]
    rows, width = numer.shape
    scaling = inner ** (-0.5)
    rounds = len(STREAMS[0])
    assert sum(map(sum, STREAMS)) == tokens

    replicas = lax.axis_size("rep")
    levels = replicas.bit_length() - 1
    powers = jnp.left_shift(jnp.ones((levels,), jnp.int32), jnp.arange(levels, dtype=jnp.int32))
    level_index = jnp.sum(jnp.where(powers == offset[0], jnp.arange(levels, dtype=jnp.int32), 0))
    half_weight = 0.5 * push_weight
    arrived = [
        lax.ppermute(half_weight, "rep", [(i, (i + (1 << b)) % replicas) for i in range(replicas)])
        for b in range(levels)
    ]
    outbox_weight = arrived[0]
    for b in range(1, levels):
        outbox_weight = jnp.where(level_index == b, arrived[b], outbox_weight)

    order = jnp.mod(me - jnp.arange(members, dtype=jnp.int32), members)
    own = me[None]
    weights = (numer / weight_one * scaling).astype(jnp.bfloat16)
    everyone = range(members - 1), range(1, members)

    def scalars(t):
        ahead = members - 1 - t
        return jnp.stack(
            [
                jnp.minimum(me + ahead, members - 1),
                (me <= t).astype(jnp.int32),
                jnp.maximum(me - ahead, 0),
                (me >= ahead).astype(jnp.int32),
            ]
        )

    at = 0
    starts = []
    for e in range(rounds):
        starts.append([])
        for sizes in STREAMS:
            starts[e].append(at)
            at += sizes[e]

    count = len(STREAMS)
    mine = [[None] * count for _ in range(rounds)]
    units = [[None] * count for _ in range(rounds)]
    before = [None] * count
    hint = [None] * (count - 1) + [jnp.broadcast_to(outbox_weight[None], (8, 128))]

    def fetch(e, q, token):
        piece = cut_heads(heads[0], starts[e][q], STREAMS[q][e], members, token)
        mine[e][q] = swapped(piece)

    for q in range(count):
        fetch(0, q, None)
    done = None
    for e in range(rounds):
        parts, moving = [None] * count, [None] * count
        for q in range(count):
            parts[q], last, first = partial_products(mine[e][q], weights, hint[q])
            if e == 0:
                moving[q] = hops(last, first, range(1), range(members - 1, members))
            else:
                right, left, _ = next_payload(*before[q], parts[q], scalars(0), True)
                moving[q] = hops(right, left, *everyone)
                units[e - 1][q][1].append(moving[q][0])
                units[e - 1][q][2].append(moving[q][1])
        for t in range(1, members - 1):
            for q in range(count):
                right, left, token = next_payload(*moving[q], parts[q], scalars(t), False)
                if t == 1 and e + 1 < rounds:
                    fetch(e + 1, q, token)
                hint[q] = token
                if e == 0:
                    pairs = range(t + 1), range(members - 1 - t, members)
                else:
                    pairs = everyone
                moving[q] = hops(right, left, *pairs)
                if e > 0 and t < members - 2:
                    units[e - 1][q][1].append(moving[q][0])
                    units[e - 1][q][2].append(moving[q][1])
        if e > 0:
            early = [[u] + r + l for u, r, l in units[e - 1]]
            kept, done = weight_step(early, mine[e - 1], order, numer)
            grads, _ = grad_rows(early, weights, order)
        for q in range(count):
            unit = unit_gradient(
                *moving[q],
                parts[q],
                own,
                residual[0],
                cotangent[0],
                gain[None],
                starts[e][q],
                done if q == count - 1 else None,
            )
            before[q] = hops(unit, unit, *everyone)
            units[e][q] = (unit, [before[q][0]], [before[q][1]])
    for s in range(1, members - 1):
        for q in range(count):
            before[q] = hops(*before[q], range(s, members - 1), range(1, members - s))
            units[-1][q][1].append(before[q][0])
            units[-1][q][2].append(before[q][1])
    flat = [[u] + r + l for u, r, l in units[-1]]
    half = weight_step(flat, mine[-1], order, kept, half=True, span=(0, HEAD_TILES))[0]
    new_weight = 0.5 * push_weight + inbox_weight
    branches = [
        partial(
            tail, half, grads, flat, mine[-1], kept, inbox_params[0], weights, order, place
        )
        for place in range(levels)
    ]
    *sent, grad_heads, new_params = lax.switch(level_index, branches)
    return (new_params[None], new_weight, widened(sent)[None], outbox_weight, grad_heads[None])


def solution(mesh):
    placed = (
        P("rep", "fsdp", None),
        P("rep"),
        P("rep", "fsdp", None),
        P("rep"),
        P("rep", "fsdp", None),
        P("rep", "fsdp", None),
        P("rep", "fsdp", None),
        P(),
        P(),
    )
    return jax.shard_map(
        local,
        mesh=mesh,
        in_specs=placed,
        out_specs=(
            P("rep", "fsdp", None),
            P("rep"),
            P("rep", "fsdp", None),
            P("rep"),
            P("rep", "fsdp", None),
        ),
        check_vma=False,
    )
```

```python
from functools import partial

import jax
import jax.numpy as jnp
from jax import lax
from jax.experimental import pallas as pl
from jax.experimental.pallas import tpu as pltpu
from jax.sharding import PartitionSpec as P

STREAMS = ((96, 96), (96, 96))
MIB = 1 << 20
TOKEN = jax.ShapeDtypeStruct((8, 128), jnp.float32)


def call(body, name, grid, ins, outs, scalars=(), scratch=(), flops=0, moved=0, vmem=12):
    return pl.pallas_call(
        body,
        name=name,
        out_shape=[jax.ShapeDtypeStruct(shape, kind) for shape, kind, _, _ in outs],
        grid_spec=pltpu.PrefetchScalarGridSpec(
            num_scalar_prefetch=len(scalars),
            grid=grid,
            in_specs=[pl.BlockSpec(block, place) for _, block, place in ins],
            out_specs=[pl.BlockSpec(block, place) for _, _, block, place in outs],
            scratch_shapes=scratch,
        ),
        compiler_params=pltpu.CompilerParams(vmem_limit_bytes=vmem * MIB),
        cost_estimate=pl.CostEstimate(flops=flops, bytes_accessed=moved, transcendentals=0),
    )(*scalars, *(array for array, _, _ in ins))


def fixed(*place):
    return lambda *_: place


def token_in(token):
    return (token, (8, 128), fixed(0, 0))


TOKEN_OUT = ((8, 128), jnp.float32, (8, 128), fixed(0, 0))


def hop(value, step, pairs):
    return lax.ppermute(value, "fsdp", [(i, i + step) for i in pairs])


def hops(right, left, rights, lefts):
    return hop(right, 1, rights), hop(left, -1, lefts)


def tile_of(width, most=512):
    tile = most
    while width % tile:
        tile //= 2
    return tile


def cut_heads(heads, start, size, members, token):
    inner = heads.shape[1]
    rows = inner // members
    step = 48

    def body(heads_ref, *refs):
        for k in range(members):
            refs[-1][k] = heads_ref[:, k * rows : (k + 1) * rows]

    return call(
        body,
        "cut_heads",
        (size // step,),
        [(heads, (step, inner), lambda i: (start // step + i, 0))]
        + ([] if token is None else [token_in(token)]),
        [((members, size, rows), heads.dtype, (members, step, rows), lambda i: (0, i, 0))],
        moved=4 * size * inner,
    )[0]


def token_of(weights):
    def body(weights_ref, token_out):
        token_out[...] = jnp.zeros((8, 128), jnp.float32)

    return call(
        body,
        "token_of",
        (1,),
        [(weights, (16, 128), fixed(0, 0))],
        [TOKEN_OUT],
        moved=8192,
    )[0]


def partial_products(mine, weights, token):
    members, size, rows = mine.shape
    width = weights.shape[1]
    tile = tile_of(width, 1280)

    def body(mine_ref, weights_ref, *refs):
        out_ref, last_ref, first_ref = refs[-3:]
        product = jnp.dot(
            mine_ref[...].reshape(members * size, rows),
            weights_ref[...],
            preferred_element_type=jnp.float32,
        ).astype(jnp.bfloat16)
        out_ref[...] = product.reshape(members, size, tile)
        last_ref[...] = product[(members - 1) * size :]
        first_ref[...] = product[:size]

    flat = ((size, width), jnp.bfloat16, (size, tile), lambda j: (0, j))
    return call(
        body,
        "partial_products",
        (width // tile,),
        [
            (mine, (members, size, rows), fixed(0, 0, 0)),
            (weights, (rows, tile), lambda j: (0, j)),
        ]
        + ([] if token is None else [token_in(token)]),
        [
            (
                (members, size, width),
                jnp.bfloat16,
                (members, size, tile),
                lambda j: (0, 0, j),
            ),
            flat,
            flat,
        ],
        flops=2 * members * size * rows * width,
        moved=2 * (members * size * (rows + width) + rows * width),
        vmem=20,
    )


def next_payload(right, left, parts, scalars, pick):
    members, size, width = parts.shape
    step = 48

    def joined(arrived, part, counts):
        if pick:
            return jnp.where(counts, part, arrived)
        weight = jnp.where(counts, 1.0, 0.0)
        return (arrived.astype(jnp.float32) + weight * part.astype(jnp.float32)).astype(
            jnp.bfloat16
        )

    def body(s, right_ref, left_ref, of_right, of_left, right_out, left_out, token_out):
        right_out[...] = joined(right_ref[...], of_right[0], s[1] > 0)
        left_out[...] = joined(left_ref[...], of_left[0], s[3] > 0)
        token_out[...] = jnp.zeros((8, 128), jnp.float32)

    here = (step, width), lambda i, s: (i, 0)
    flat = ((size, width), jnp.bfloat16) + here
    return call(
        body,
        "next_payload",
        (size // step,),
        [
            (right,) + here,
            (left,) + here,
            (parts, (1, step, width), lambda i, s: (s[0], i, 0)),
            (parts, (1, step, width), lambda i, s: (s[2], i, 0)),
        ],
        [flat, flat, TOKEN_OUT],
        scalars=(scalars,),
        flops=2 * size * width,
        moved=12 * size * width,
    )


def unit_gradient(right, left, parts, place, residual, cotangent, gain, start, token):
    members, size, width = parts.shape
    step = 48

    def body(s, right_ref, left_ref, own_ref, residual_ref, cot_ref, gain_ref, *refs):
        product = (
            right_ref[...].astype(jnp.float32)
            + left_ref[...].astype(jnp.float32)
            + own_ref[0].astype(jnp.float32)
        )
        summed = residual_ref[...].astype(jnp.float32) + product
        inverse = lax.rsqrt(jnp.mean(summed * summed, axis=-1, keepdims=True) + 1e-05)
        scaled_cot = gain_ref[...] * cot_ref[...].astype(jnp.float32)
        along = jnp.mean(scaled_cot * summed, axis=-1, keepdims=True)
        refs[-1][...] = (
            inverse * scaled_cot - summed * (inverse * inverse * inverse * along)
        ).astype(jnp.bfloat16)

    here = (step, width), lambda i, s: (i, 0)
    there = (step, width), lambda i, s: (start // step + i, 0)
    return call(
        body,
        "unit_gradient",
        (size // step,),
        [
            (right,) + here,
            (left,) + here,
            (parts, (1, step, width), lambda i, s: (s[0], i, 0)),
            (residual,) + there,
            (cotangent,) + there,
            (gain, (1, width), fixed(0, 0)),
        ]
        + ([] if token is None else [token_in(token)]),
        [((size, width), jnp.bfloat16) + here],
        scalars=(place,),
        flops=12 * size * width,
        moved=12 * size * width,
    )[0]


def stack_of(refs, members, me):
    count = 2 * members - 1
    rows = []
    for c in range(len(refs) // count):
        own, rights, lefts = (
            refs[c * count],
            refs[c * count + 1 : c * count + members],
            refs[c * count + members : (c + 1) * count],
        )
        rows.append(own[...])
        for k in range(members - 1):
            rows.append(jnp.where(me > k, rights[k][...], lefts[members - 2 - k][...]))
    return jnp.concatenate(rows, axis=0)


def unit_ins(units, tile):
    ins = []
    for chunk in units:
        block = (chunk[0].shape[0], tile)
        members = (len(chunk) + 1) // 2
        ins.append((chunk[0], block, lambda j, s: (0, j)))
        for k in range(members - 1):
            place = lambda j, s, k=k: (0, jnp.where(s[0] > k, j, 0))
            ins.append((chunk[1 + k], block, place))
        for m in range(members - 1):
            place = lambda j, s, k=members - 2 - m: (0, jnp.where(s[0] > k, 0, j))
            ins.append((chunk[members + m], block, place))
    return ins


def mine_ins(mine):
    return [(block, block.shape, fixed(0, 0, 0)) for block in mine]


def turned_into(scratch, mine_refs, order):
    members = mine_refs[0].shape[0]
    stack = jnp.concatenate([ref[order[k]] for ref in mine_refs for k in range(members)], axis=0)
    scratch[...] = stack.T


def weight_step(units, mine, order, base, half=False, inbox=None, token=None):
    members, _, rows = mine[0].shape
    width = base.shape[1]
    tile = tile_of(width)
    count = len(units) * len(units[0])
    chunks = len(units)
    total = sum(members * block.shape[1] for block in mine)
    early = inbox is None and not half

    def body(s, *refs):
        units_ref, mine_refs = refs[:count], refs[count : count + chunks]
        base_ref = refs[count + chunks]
        turned = refs[-1]

        @pl.when(pl.program_id(0) == 0)
        def _():
            turned_into(turned, mine_refs, s)

        weight = jnp.dot(
            turned[...], stack_of(units_ref, members, s[0]), preferred_element_type=jnp.float32
        )
        if early:
            refs[-3][...] = 0.5 * (base_ref[...] - 0.004 * weight)
            refs[-2][...] = jnp.zeros((8, 128), jnp.float32)
        else:
            now = base_ref[...] - 0.5 * 0.004 * weight
            if inbox is not None:
                refs[-2][...] = now + refs[count + chunks + 1][...]
            else:
                refs[-2][...] = now.astype(jnp.bfloat16)

    columns = (rows, tile), lambda j, s: (0, j)
    ins = unit_ins(units, tile) + mine_ins(mine) + [(base,) + columns]
    if inbox is not None:
        ins.append((inbox,) + columns)
    if token is not None:
        ins.append(token_in(token))
    kind = jnp.bfloat16 if half else jnp.float32
    outs = [((rows, width), kind) + columns]
    return call(
        body,
        "weight_step",
        (width // tile,),
        ins,
        outs + [TOKEN_OUT] * early,
        scalars=(order,),
        scratch=[pltpu.VMEM((rows, total), jnp.bfloat16)],
        flops=2 * total * rows * width,
        moved=(2 * count * units[0][0].shape[0] + 12 * rows) * width,
        vmem=26 if early else 52,
    )


def grad_rows(units, weights, order):
    members = (len(units[0]) + 1) // 2
    sizes = [chunk[0].shape[0] for chunk in units]
    rows, width = weights.shape
    tile = tile_of(width)
    steps = width // tile
    count = len(units) * len(units[0])
    total = members * sum(sizes)

    def body(s, *refs):
        weights_ref, grad_ref, token_out, acc = refs[count:]
        token_out[...] = jnp.zeros((8, 128), jnp.float32)
        j = pl.program_id(0)
        grad = lax.dot_general(
            stack_of(refs[:count], members, s[0]),
            weights_ref[...],
            (((1,), (1,)), ((), ())),
            preferred_element_type=jnp.float32,
        )

        @pl.when(j == 0)
        def _():
            acc[...] = grad

        @pl.when(j > 0)
        def _():
            acc[...] += grad

        @pl.when(j == steps - 1)
        def _():
            at, row = 0, 0
            for size in sizes:
                for k in range(members):
                    grad_ref[s[k], row : row + size] = acc[at : at + size].astype(jnp.bfloat16)
                    at += size
                row += size

    return call(
        body,
        "grad_rows",
        (steps,),
        unit_ins(units, tile) + [(weights, (rows, tile), lambda j, s: (0, j))],
        [
            (
                (members, sum(sizes), rows),
                jnp.bfloat16,
                (members, sum(sizes), rows),
                fixed(0, 0, 0),
            ),
            TOKEN_OUT,
        ],
        scalars=(order,),
        scratch=[pltpu.VMEM((total, rows), jnp.float32)],
        flops=2 * total * rows * width,
        moved=2 * count * sizes[0] * width + 2 * rows * width,
        vmem=50,
    )


def joined_rows(groups):
    members, size, rows = groups[0].shape
    tokens = size * len(groups)

    def body(*refs):
        out_ref = refs[-1]
        for g, blocks_ref in enumerate(refs[:-1]):

            @pl.when(pl.program_id(0) == g)
            def _(blocks_ref=blocks_ref):
                for k in range(members):
                    out_ref[:, k * rows : (k + 1) * rows] = blocks_ref[k]

    return call(
        body,
        "joined_rows",
        (len(groups),),
        [(blocks, (members, size, rows), fixed(0, 0, 0)) for blocks in groups],
        [
            (
                (tokens, members * rows),
                groups[0].dtype,
                (size, members * rows),
                lambda i: (i, 0),
            )
        ],
        moved=4 * members * tokens * rows,
        vmem=24,
    )[0]


def widened(value):
    rows, width = value.shape
    step = rows // 2

    def body(value_ref, out_ref):
        out_ref[...] = value_ref[...].astype(jnp.float32)

    block = (step, width), lambda i: (i, 0)
    return call(
        body,
        "widened",
        (rows // step,),
        [(value,) + block],
        [((rows, width), jnp.float32) + block],
        moved=6 * rows * width,
        vmem=20,
    )[0]


def swapped(blocks):
    return lax.all_to_all(blocks, "fsdp", 0, 0, tiled=False)


def tail(half, grads, late, mine, kept, inbox, weights, order, bit_place):
    length = lax.axis_size("rep")
    sent = lax.ppermute(
        half, "rep", [(i, (i + (1 << bit_place)) % length) for i in range(length)]
    )
    back = swapped(grads)
    late_grads, token = grad_rows(late, weights, order)
    late_back = swapped(late_grads)
    new = weight_step(late, mine, order, kept, inbox=inbox, token=token)[0]
    return sent, joined_rows([back, late_back]), new


def local(
    params, push_weight, inbox_params, inbox_weight, heads, residual, cotangent, gain, offset
):
    numer = params[0]
    weight_one = push_weight[0]
    members = lax.axis_size("fsdp")
    me = lax.axis_index("fsdp").astype(jnp.int32)
    tokens, inner = heads.shape[1:]
    rows, width = numer.shape
    scaling = inner ** (-0.5)
    rounds = len(STREAMS[0])
    assert sum(map(sum, STREAMS)) == tokens

    replicas = lax.axis_size("rep")
    levels = replicas.bit_length() - 1
    powers = jnp.left_shift(jnp.ones((levels,), jnp.int32), jnp.arange(levels, dtype=jnp.int32))
    level_index = jnp.sum(jnp.where(powers == offset[0], jnp.arange(levels, dtype=jnp.int32), 0))
    half_weight = 0.5 * push_weight
    arrived = [
        lax.ppermute(half_weight, "rep", [(i, (i + (1 << b)) % replicas) for i in range(replicas)])
        for b in range(levels)
    ]
    outbox_weight = arrived[0]
    for b in range(1, levels):
        outbox_weight = jnp.where(level_index == b, arrived[b], outbox_weight)

    order = jnp.mod(me - jnp.arange(members, dtype=jnp.int32), members)
    own = me[None]
    weights = (numer / weight_one * scaling).astype(jnp.bfloat16)
    everyone = range(members - 1), range(1, members)

    def scalars(t):
        ahead = members - 1 - t
        return jnp.stack(
            [
                jnp.minimum(me + ahead, members - 1),
                (me <= t).astype(jnp.int32),
                jnp.maximum(me - ahead, 0),
                (me >= ahead).astype(jnp.int32),
            ]
        )

    at = 0
    starts = []
    for e in range(rounds):
        starts.append([])
        for sizes in STREAMS:
            starts[e].append(at)
            at += sizes[e]

    count = len(STREAMS)
    mine = [[None] * count for _ in range(rounds)]
    units = [[None] * count for _ in range(rounds)]
    before = [None] * count
    hint = [None] * (count - 1) + [jnp.broadcast_to(outbox_weight[None], (8, 128))]

    def fetch(e, q, token):
        piece = cut_heads(heads[0], starts[e][q], STREAMS[q][e], members, token)
        mine[e][q] = swapped(piece)

    for q in range(count):
        fetch(0, q, token_of(weights) if q else None)
    done = None
    for e in range(rounds):
        parts, moving = [None] * count, [None] * count
        for q in range(count):
            parts[q], last, first = partial_products(mine[e][q], weights, hint[q])
            if e == 0:
                moving[q] = hops(last, first, range(1), range(members - 1, members))
            else:
                right, left, _ = next_payload(*before[q], parts[q], scalars(0), True)
                moving[q] = hops(right, left, *everyone)
                units[e - 1][q][1].append(moving[q][0])
                units[e - 1][q][2].append(moving[q][1])
        for t in range(1, members - 1):
            for q in range(count):
                right, left, token = next_payload(*moving[q], parts[q], scalars(t), False)
                if t == 1 and e + 1 < rounds:
                    fetch(e + 1, q, token)
                hint[q] = token
                if e == 0:
                    pairs = range(t + 1), range(members - 1 - t, members)
                else:
                    pairs = everyone
                moving[q] = hops(right, left, *pairs)
                if e > 0 and t < members - 2:
                    units[e - 1][q][1].append(moving[q][0])
                    units[e - 1][q][2].append(moving[q][1])
        if e > 0:
            early = [[u] + r + l for u, r, l in units[e - 1]]
            kept, done = weight_step(early, mine[e - 1], order, numer)
            grads, _ = grad_rows(early, weights, order)
        for q in range(count):
            unit = unit_gradient(
                *moving[q],
                parts[q],
                own,
                residual[0],
                cotangent[0],
                gain[None],
                starts[e][q],
                done if q == count - 1 else None,
            )
            before[q] = hops(unit, unit, *everyone)
            units[e][q] = (unit, [before[q][0]], [before[q][1]])
    for s in range(1, members - 1):
        for q in range(count):
            before[q] = hops(*before[q], range(s, members - 1), range(1, members - s))
            units[-1][q][1].append(before[q][0])
            units[-1][q][2].append(before[q][1])
    flat = [[u] + r + l for u, r, l in units[-1]]
    half = weight_step(flat, mine[-1], order, kept, half=True)[0]
    new_weight = 0.5 * push_weight + inbox_weight
    branches = [
        partial(
            tail, half, grads, flat, mine[-1], kept, inbox_params[0], weights, order, place
        )
        for place in range(levels)
    ]
    sent, grad_heads, new_params = lax.switch(level_index, branches)
    return (new_params[None], new_weight, widened(sent)[None], outbox_weight, grad_heads[None])


def solution(mesh):
    placed = (
        P("rep", "fsdp", None),
        P("rep"),
        P("rep", "fsdp", None),
        P("rep"),
        P("rep", "fsdp", None),
        P("rep", "fsdp", None),
        P("rep", "fsdp", None),
        P(),
        P(),
    )
    return jax.shard_map(
        local,
        mesh=mesh,
        in_specs=placed,
        out_specs=(
            P("rep", "fsdp", None),
            P("rep"),
            P("rep", "fsdp", None),
            P("rep"),
            P("rep", "fsdp", None),
        ),
        check_vma=False,
    )
```

```python
from functools import partial

import jax
import jax.numpy as jnp
from jax import lax
from jax.experimental import pallas as pl
from jax.experimental.pallas import tpu as pltpu
from jax.sharding import PartitionSpec as P

STREAMS = ((96, 96), (96, 96))
MIB = 1 << 20
TOKEN = jax.ShapeDtypeStruct((8, 128), jnp.float32)


def call(body, name, grid, ins, outs, scalars=(), scratch=(), flops=0, moved=0, vmem=12):
    return pl.pallas_call(
        body,
        name=name,
        out_shape=[jax.ShapeDtypeStruct(shape, kind) for shape, kind, _, _ in outs],
        grid_spec=pltpu.PrefetchScalarGridSpec(
            num_scalar_prefetch=len(scalars),
            grid=grid,
            in_specs=[pl.BlockSpec(block, place) for _, block, place in ins],
            out_specs=[pl.BlockSpec(block, place) for _, _, block, place in outs],
            scratch_shapes=scratch,
        ),
        compiler_params=pltpu.CompilerParams(vmem_limit_bytes=vmem * MIB),
        cost_estimate=pl.CostEstimate(flops=flops, bytes_accessed=moved, transcendentals=0),
    )(*scalars, *(array for array, _, _ in ins))


def fixed(*place):
    return lambda *_: place


def token_in(token):
    return (token, (8, 128), fixed(0, 0))


TOKEN_OUT = ((8, 128), jnp.float32, (8, 128), fixed(0, 0))


def hop(value, step, pairs):
    return lax.ppermute(value, "fsdp", [(i, i + step) for i in pairs])


def hops(right, left, rights, lefts):
    return hop(right, 1, rights), hop(left, -1, lefts)


def tile_of(width, most=512):
    tile = most
    while width % tile:
        tile //= 2
    return tile


def cut_heads(heads, start, size, members, token):
    inner = heads.shape[1]
    rows = inner // members
    step = 48

    def body(heads_ref, *refs):
        for k in range(members):
            refs[-1][k] = heads_ref[:, k * rows : (k + 1) * rows]

    return call(
        body,
        "cut_heads",
        (size // step,),
        [(heads, (step, inner), lambda i: (start // step + i, 0))]
        + ([] if token is None else [token_in(token)]),
        [((members, size, rows), heads.dtype, (members, step, rows), lambda i: (0, i, 0))],
        moved=4 * size * inner,
    )[0]


def token_of(weights):
    def body(weights_ref, token_out):
        token_out[...] = jnp.zeros((8, 128), jnp.float32)

    return call(
        body,
        "token_of",
        (1,),
        [(weights, (16, 128), fixed(0, 0))],
        [TOKEN_OUT],
        moved=8192,
    )[0]


def partial_products(mine, weights, token):
    members, size, rows = mine.shape
    width = weights.shape[1]
    tile = tile_of(width, 1280)

    def body(mine_ref, weights_ref, *refs):
        out_ref, last_ref, first_ref = refs[-3:]
        product = jnp.dot(
            mine_ref[...].reshape(members * size, rows),
            weights_ref[...],
            preferred_element_type=jnp.float32,
        ).astype(jnp.bfloat16)
        out_ref[...] = product.reshape(members, size, tile)
        last_ref[...] = product[(members - 1) * size :]
        first_ref[...] = product[:size]

    flat = ((size, width), jnp.bfloat16, (size, tile), lambda j: (0, j))
    return call(
        body,
        "partial_products",
        (width // tile,),
        [
            (mine, (members, size, rows), fixed(0, 0, 0)),
            (weights, (rows, tile), lambda j: (0, j)),
        ]
        + ([] if token is None else [token_in(token)]),
        [
            (
                (members, size, width),
                jnp.bfloat16,
                (members, size, tile),
                lambda j: (0, 0, j),
            ),
            flat,
            flat,
        ],
        flops=2 * members * size * rows * width,
        moved=2 * (members * size * (rows + width) + rows * width),
        vmem=20,
    )


def next_payload(right, left, parts, scalars, pick):
    members, size, width = parts.shape
    step = 48

    def joined(arrived, part, counts):
        if pick:
            return jnp.where(counts, part, arrived)
        weight = jnp.where(counts, 1.0, 0.0)
        return (arrived.astype(jnp.float32) + weight * part.astype(jnp.float32)).astype(
            jnp.bfloat16
        )

    def body(s, right_ref, left_ref, of_right, of_left, right_out, left_out, token_out):
        right_out[...] = joined(right_ref[...], of_right[0], s[1] > 0)
        left_out[...] = joined(left_ref[...], of_left[0], s[3] > 0)
        token_out[...] = jnp.zeros((8, 128), jnp.float32)

    here = (step, width), lambda i, s: (i, 0)
    flat = ((size, width), jnp.bfloat16) + here
    return call(
        body,
        "next_payload",
        (size // step,),
        [
            (right,) + here,
            (left,) + here,
            (parts, (1, step, width), lambda i, s: (s[0], i, 0)),
            (parts, (1, step, width), lambda i, s: (s[2], i, 0)),
        ],
        [flat, flat, TOKEN_OUT],
        scalars=(scalars,),
        flops=2 * size * width,
        moved=12 * size * width,
    )


def unit_gradient(right, left, parts, place, residual, cotangent, gain, start, token):
    members, size, width = parts.shape
    step = 48

    def body(s, right_ref, left_ref, own_ref, residual_ref, cot_ref, gain_ref, *refs):
        product = (
            right_ref[...].astype(jnp.float32)
            + left_ref[...].astype(jnp.float32)
            + own_ref[0].astype(jnp.float32)
        )
        summed = residual_ref[...].astype(jnp.float32) + product
        inverse = lax.rsqrt(jnp.mean(summed * summed, axis=-1, keepdims=True) + 1e-05)
        scaled_cot = gain_ref[...] * cot_ref[...].astype(jnp.float32)
        along = jnp.mean(scaled_cot * summed, axis=-1, keepdims=True)
        refs[-1][...] = (
            inverse * scaled_cot - summed * (inverse * inverse * inverse * along)
        ).astype(jnp.bfloat16)

    here = (step, width), lambda i, s: (i, 0)
    there = (step, width), lambda i, s: (start // step + i, 0)
    return call(
        body,
        "unit_gradient",
        (size // step,),
        [
            (right,) + here,
            (left,) + here,
            (parts, (1, step, width), lambda i, s: (s[0], i, 0)),
            (residual,) + there,
            (cotangent,) + there,
            (gain, (1, width), fixed(0, 0)),
        ]
        + ([] if token is None else [token_in(token)]),
        [((size, width), jnp.bfloat16) + here],
        scalars=(place,),
        flops=12 * size * width,
        moved=12 * size * width,
    )[0]


def stack_of(refs, members, me):
    count = 2 * members - 1
    rows = []
    for c in range(len(refs) // count):
        own, rights, lefts = (
            refs[c * count],
            refs[c * count + 1 : c * count + members],
            refs[c * count + members : (c + 1) * count],
        )
        rows.append(own[...])
        for k in range(members - 1):
            rows.append(jnp.where(me > k, rights[k][...], lefts[members - 2 - k][...]))
    return jnp.concatenate(rows, axis=0)


def unit_ins(units, tile):
    ins = []
    for chunk in units:
        block = (chunk[0].shape[0], tile)
        members = (len(chunk) + 1) // 2
        ins.append((chunk[0], block, lambda j, s: (0, j)))
        for k in range(members - 1):
            place = lambda j, s, k=k: (0, jnp.where(s[0] > k, j, 0))
            ins.append((chunk[1 + k], block, place))
        for m in range(members - 1):
            place = lambda j, s, k=members - 2 - m: (0, jnp.where(s[0] > k, 0, j))
            ins.append((chunk[members + m], block, place))
    return ins


def mine_ins(mine):
    return [(block, block.shape, fixed(0, 0, 0)) for block in mine]


def turned_into(scratch, mine_refs, order):
    members = mine_refs[0].shape[0]
    stack = jnp.concatenate([ref[order[k]] for ref in mine_refs for k in range(members)], axis=0)
    scratch[...] = stack.T


def weight_step(units, mine, order, base, half=False, inbox=None, token=None):
    members, _, rows = mine[0].shape
    width = base.shape[1]
    tile = tile_of(width)
    count = len(units) * len(units[0])
    chunks = len(units)
    total = sum(members * block.shape[1] for block in mine)
    early = inbox is None and not half

    def body(s, *refs):
        units_ref, mine_refs = refs[:count], refs[count : count + chunks]
        base_ref = refs[count + chunks]
        turned = refs[-1]

        @pl.when(pl.program_id(0) == 0)
        def _():
            turned_into(turned, mine_refs, s)

        weight = jnp.dot(
            turned[...], stack_of(units_ref, members, s[0]), preferred_element_type=jnp.float32
        )
        if early:
            refs[-3][...] = 0.5 * (base_ref[...] - 0.004 * weight)
            refs[-2][...] = jnp.zeros((8, 128), jnp.float32)
        else:
            now = base_ref[...] - 0.5 * 0.004 * weight
            if inbox is not None:
                refs[-2][...] = now + refs[count + chunks + 1][...]
            else:
                refs[-2][...] = now.astype(jnp.bfloat16)

    columns = (rows, tile), lambda j, s: (0, j)
    ins = unit_ins(units, tile) + mine_ins(mine) + [(base,) + columns]
    if inbox is not None:
        ins.append((inbox,) + columns)
    if token is not None:
        ins.append(token_in(token))
    kind = jnp.bfloat16 if half else jnp.float32
    outs = [((rows, width), kind) + columns]
    return call(
        body,
        "weight_step",
        (width // tile,),
        ins,
        outs + [TOKEN_OUT] * early,
        scalars=(order,),
        scratch=[pltpu.VMEM((rows, total), jnp.bfloat16)],
        flops=2 * total * rows * width,
        moved=(2 * count * units[0][0].shape[0] + 12 * rows) * width,
        vmem=26 if early else 52,
    )


def grad_rows(units, weights, order):
    members = (len(units[0]) + 1) // 2
    sizes = [chunk[0].shape[0] for chunk in units]
    rows, width = weights.shape
    tile = tile_of(width)
    steps = width // tile
    count = len(units) * len(units[0])
    total = members * sum(sizes)

    def body(s, *refs):
        weights_ref, grad_ref, token_out, acc = refs[count:]
        token_out[...] = jnp.zeros((8, 128), jnp.float32)
        j = pl.program_id(0)
        grad = lax.dot_general(
            stack_of(refs[:count], members, s[0]),
            weights_ref[...],
            (((1,), (1,)), ((), ())),
            preferred_element_type=jnp.float32,
        )

        @pl.when(j == 0)
        def _():
            acc[...] = grad

        @pl.when(j > 0)
        def _():
            acc[...] += grad

        @pl.when(j == steps - 1)
        def _():
            at, row = 0, 0
            for size in sizes:
                for k in range(members):
                    grad_ref[s[k], row : row + size] = acc[at : at + size].astype(jnp.bfloat16)
                    at += size
                row += size

    return call(
        body,
        "grad_rows",
        (steps,),
        unit_ins(units, tile) + [(weights, (rows, tile), lambda j, s: (0, j))],
        [
            (
                (members, sum(sizes), rows),
                jnp.bfloat16,
                (members, sum(sizes), rows),
                fixed(0, 0, 0),
            ),
            TOKEN_OUT,
        ],
        scalars=(order,),
        scratch=[pltpu.VMEM((total, rows), jnp.float32)],
        flops=2 * total * rows * width,
        moved=2 * count * sizes[0] * width + 2 * rows * width,
        vmem=50,
    )


def joined_rows(groups):
    members, size, rows = groups[0].shape
    tokens = size * len(groups)

    def body(*refs):
        out_ref = refs[-1]
        for g, blocks_ref in enumerate(refs[:-1]):

            @pl.when(pl.program_id(0) == g)
            def _(blocks_ref=blocks_ref):
                for k in range(members):
                    out_ref[:, k * rows : (k + 1) * rows] = blocks_ref[k]

    return call(
        body,
        "joined_rows",
        (len(groups),),
        [(blocks, (members, size, rows), fixed(0, 0, 0)) for blocks in groups],
        [
            (
                (tokens, members * rows),
                groups[0].dtype,
                (size, members * rows),
                lambda i: (i, 0),
            )
        ],
        moved=4 * members * tokens * rows,
        vmem=24,
    )[0]


def widened(value):
    rows, width = value.shape
    step = rows // 2

    def body(value_ref, out_ref):
        out_ref[...] = value_ref[...].astype(jnp.float32)

    block = (step, width), lambda i: (i, 0)
    return call(
        body,
        "widened",
        (rows // step,),
        [(value,) + block],
        [((rows, width), jnp.float32) + block],
        moved=6 * rows * width,
        vmem=20,
    )[0]


def swapped(blocks):
    return lax.all_to_all(blocks, "fsdp", 0, 0, tiled=False)


def tail(half, grads, late, mine, kept, inbox, weights, order, bit_place):
    length = lax.axis_size("rep")
    sent = lax.ppermute(
        half, "rep", [(i, (i + (1 << bit_place)) % length) for i in range(length)]
    )
    back = swapped(grads)
    late_grads, token = grad_rows(late, weights, order)
    late_back = swapped(late_grads)
    new = weight_step(late, mine, order, kept, inbox=inbox, token=token)[0]
    return sent, joined_rows([back, late_back]), new


def local(
    params, push_weight, inbox_params, inbox_weight, heads, residual, cotangent, gain, offset
):
    numer = params[0]
    weight_one = push_weight[0]
    members = lax.axis_size("fsdp")
    me = lax.axis_index("fsdp").astype(jnp.int32)
    tokens, inner = heads.shape[1:]
    rows, width = numer.shape
    scaling = inner ** (-0.5)
    rounds = len(STREAMS[0])
    assert sum(map(sum, STREAMS)) == tokens

    replicas = lax.axis_size("rep")
    levels = replicas.bit_length() - 1
    powers = jnp.left_shift(jnp.ones((levels,), jnp.int32), jnp.arange(levels, dtype=jnp.int32))
    level_index = jnp.sum(jnp.where(powers == offset[0], jnp.arange(levels, dtype=jnp.int32), 0))
    half_weight = 0.5 * push_weight
    arrived = [
        lax.ppermute(half_weight, "rep", [(i, (i + (1 << b)) % replicas) for i in range(replicas)])
        for b in range(levels)
    ]
    outbox_weight = arrived[0]
    for b in range(1, levels):
        outbox_weight = jnp.where(level_index == b, arrived[b], outbox_weight)

    order = jnp.mod(me - jnp.arange(members, dtype=jnp.int32), members)
    own = me[None]
    weights = (numer / weight_one * scaling).astype(jnp.bfloat16)
    everyone = range(members - 1), range(1, members)

    def scalars(t):
        ahead = members - 1 - t
        return jnp.stack(
            [
                jnp.minimum(me + ahead, members - 1),
                (me <= t).astype(jnp.int32),
                jnp.maximum(me - ahead, 0),
                (me >= ahead).astype(jnp.int32),
            ]
        )

    at = 0
    starts = []
    for e in range(rounds):
        starts.append([])
        for sizes in STREAMS:
            starts[e].append(at)
            at += sizes[e]

    count = len(STREAMS)
    mine = [[None] * count for _ in range(rounds)]
    units = [[None] * count for _ in range(rounds)]
    before = [None] * count
    hint = [None] * (count - 1) + [jnp.broadcast_to(outbox_weight[None], (8, 128))]

    def fetch(e, q, token):
        piece = cut_heads(heads[0], starts[e][q], STREAMS[q][e], members, token)
        mine[e][q] = swapped(piece)

    for q in range(count):
        fetch(0, q, token_of(weights) + outbox_weight[0] if q else None)
    done = None
    for e in range(rounds):
        parts, moving = [None] * count, [None] * count
        for q in range(count):
            parts[q], last, first = partial_products(mine[e][q], weights, hint[q])
            if e == 0:
                moving[q] = hops(last, first, range(1), range(members - 1, members))
            else:
                right, left, _ = next_payload(*before[q], parts[q], scalars(0), True)
                moving[q] = hops(right, left, *everyone)
                units[e - 1][q][1].append(moving[q][0])
                units[e - 1][q][2].append(moving[q][1])
        for t in range(1, members - 1):
            for q in range(count):
                right, left, token = next_payload(*moving[q], parts[q], scalars(t), False)
                if t == 1 and e + 1 < rounds:
                    fetch(e + 1, q, token)
                hint[q] = token
                if e == 0:
                    pairs = range(t + 1), range(members - 1 - t, members)
                else:
                    pairs = everyone
                moving[q] = hops(right, left, *pairs)
                if e > 0 and t < members - 2:
                    units[e - 1][q][1].append(moving[q][0])
                    units[e - 1][q][2].append(moving[q][1])
        if e > 0:
            early = [[u] + r + l for u, r, l in units[e - 1]]
            kept, done = weight_step(early, mine[e - 1], order, numer)
            grads, _ = grad_rows(early, weights, order)
        for q in range(count):
            unit = unit_gradient(
                *moving[q],
                parts[q],
                own,
                residual[0],
                cotangent[0],
                gain[None],
                starts[e][q],
                done if q == count - 1 else None,
            )
            before[q] = hops(unit, unit, *everyone)
            units[e][q] = (unit, [before[q][0]], [before[q][1]])
    for s in range(1, members - 1):
        for q in range(count):
            before[q] = hops(*before[q], range(s, members - 1), range(1, members - s))
            units[-1][q][1].append(before[q][0])
            units[-1][q][2].append(before[q][1])
    flat = [[u] + r + l for u, r, l in units[-1]]
    half = weight_step(flat, mine[-1], order, kept, half=True)[0]
    new_weight = 0.5 * push_weight + inbox_weight
    branches = [
        partial(
            tail, half, grads, flat, mine[-1], kept, inbox_params[0], weights, order, place
        )
        for place in range(levels)
    ]
    sent, grad_heads, new_params = lax.switch(level_index, branches)
    return (new_params[None], new_weight, widened(sent)[None], outbox_weight, grad_heads[None])


def solution(mesh):
    placed = (
        P("rep", "fsdp", None),
        P("rep"),
        P("rep", "fsdp", None),
        P("rep"),
        P("rep", "fsdp", None),
        P("rep", "fsdp", None),
        P("rep", "fsdp", None),
        P(),
        P(),
    )
    return jax.shard_map(
        local,
        mesh=mesh,
        in_specs=placed,
        out_specs=(
            P("rep", "fsdp", None),
            P("rep"),
            P("rep", "fsdp", None),
            P("rep"),
            P("rep", "fsdp", None),
        ),
        check_vma=False,
    )
```
